32 devices in a mesh: crops: 2 (over x), tile: 16 (over z, y, core).
Axes of the slice: x: 2, y: 2, z: 4, core: 2. Of those that a mesh axis runs over, the one named last changes fastest.
Arguments:
- pair_input: bfloat16 [1024, 512, 128], P(('crops', 'tile')), parts along dimension 0, may hold values from -40 to 40
- d_update: bfloat16 [1024, 512, 128], P(('crops', 'tile')), parts along dimension 0, may hold values from -6 to 6
- token_mask: int32 [1024], P('crops'), parts along dimension 0, may hold values 0 or 1
- ln_in_gain: float32 [128], replicated, may hold values from 0.25 to 1.75
- ln_in_bias: float32 [128], replicated, may hold values from -2 to 2
- w_ab: bfloat16 [128, 512], replicated, may hold values from -0.5 to 0.5
- w_gate: bfloat16 [128, 128], replicated, may hold values from -0.5 to 0.5
- ln_out_gain: float32 [128], replicated, may hold values from 0.25 to 1.75
- ln_out_bias: float32 [128], replicated, may hold values from -2 to 2
- w_out: bfloat16 [128, 128], replicated, may hold values from -0.5 to 0.5
Outputs:
- pair_grad: bfloat16 [1024, 512, 128], P(('crops', 'tile')), parts along dimension 0
- grad_w_ab: float32 [256, 512], P('crops'), parts along dimension 0
- grad_w_gate: float32 [256, 128], P('crops'), parts along dimension 0
- grad_w_out: float32 [256, 128], P('crops'), parts along dimension 0
The draws below stay inside these ranges and needn't reach their ends.
There are 2 independent parts, one for each index of `crops`. The reference program is written for one: setup_inputs(seed, part) draws one part's arguments, and reference() takes and returns one part's arrays. A program takes and returns all parts, laid end to end along the dimension named above; an argument that names none is the same for every part. Nothing has to cross between parts.
All inputs are finite; a program needn't handle non-finite values.
Results may differ from the reference program's by a relative error of at most 0.015.
Values may be sent and summed in bfloat16 or wider, within the bound.
No kernel may reach another device: no remote copies, remote signals or barrier semaphores. Data moves between devices by JAX's collectives and lax.ppermute only.
A program may use at most 192 MiB of HBM per device.

```python
import jax
import jax.numpy as jnp
from jax import lax

C = 128
H = 128
N = 512


def draw_pair_input(key, part):
    key = jax.random.fold_in(key, 11)
    key_base = jax.random.fold_in(key, 0)
    values = jax.random.normal(key_base, (N, N, C), jnp.float32)
    return jnp.clip(values, -6.0, 6.0).astype(jnp.bfloat16)


def place_ends(entries, key, low, largest):
    shape = entries.shape
    place = [jax.random.randint(jax.random.fold_in(key, axis), (), 0, shape[axis]) for axis in range(len(shape))]
    entries = entries.at[tuple(place)].set(low)
    longest = shape.index(max(shape))
    place[longest] = (place[longest] + 1) % shape[longest]
    return entries.at[tuple(place)].set(largest)


def steps_of(rng, dims, shards, low, largest):
    loudness = 1.0
    for dim, blocks in shards:
        heights = jax.random.uniform(jax.random.fold_in(jax.random.fold_in(rng, 6), dim), (blocks,), jnp.float32, low / len(shards), largest / len(shards))
        loudness = loudness * jnp.repeat(jnp.exp(heights), dims[dim] // blocks).reshape((-1,) + (1,) * (len(dims) - 1 - dim))
    return loudness


def bell_draw(own_key, shape, width, bound, shards=(), kind=jnp.bfloat16):
    factor_of = steps_of(own_key, shape, shards, -0.22, 0.18) if shards else 1.0
    result = jax.random.normal(own_key, shape, jnp.float32) * width * factor_of
    return jnp.minimum(jnp.maximum(result, -bound), bound).astype(kind)


def setup_inputs(seed: int = 0, part: int = 0) -> dict:
    key_list = jax.random.split(jax.random.key(seed), 11)
    part_keys = jax.random.split(jax.random.fold_in(key_list[10], part), 11)
    pair_input = draw_pair_input(jax.random.fold_in(jax.random.fold_in(key_list[10], part), 71), part)
    d_update = bell_draw(part_keys[1], (N, N, C), 1.0, 6.0, ((0, 16),))
    token_mask = place_ends((jax.random.randint(part_keys[2], (N,), 0, 4) < 3).astype(jnp.int32), jax.random.fold_in(part_keys[2], 1), 0, 1)
    ln_in_gain = jnp.clip(1.0 + 0.15 * jax.random.normal(key_list[3], (C,), jnp.float32), 0.25, 1.75)
    ln_in_bias = bell_draw(key_list[4], (C,), 0.5, 2.0, (), jnp.float32)
    w_ab = bell_draw(key_list[5], (C, 4 * H), C ** -0.5, 0.5)
    w_gate = bell_draw(key_list[6], (C, C), C ** -0.5, 0.5)
    ln_out_gain = jnp.clip(1.0 + 0.15 * jax.random.normal(key_list[7], (H,), jnp.float32), 0.25, 1.75)
    ln_out_bias = bell_draw(key_list[8], (H,), 0.5, 2.0, (), jnp.float32)
    w_out = bell_draw(key_list[9], (H, C), H ** -0.5, 0.5)
    return dict(pair_input=pair_input, d_update=d_update, token_mask=token_mask, ln_in_gain=ln_in_gain, ln_in_bias=ln_in_bias, w_ab=w_ab, w_gate=w_gate, ln_out_gain=ln_out_gain, ln_out_bias=ln_out_bias, w_out=w_out)


EPS = 1e-05

def norm_stats(value, axis_id):
    center = lax.optimization_barrier(jnp.mean(value, axis=axis_id, keepdims=True))
    centered = value - center
    variance = lax.optimization_barrier(jnp.mean(centered * centered, axis=axis_id, keepdims=True))
    inv_std = lax.rsqrt(variance + EPS)
    return (centered * inv_std, inv_std)

def norm_back(upstream, scaled, inv_std, axis_id):
    mean_up = lax.optimization_barrier(jnp.mean(upstream, axis=axis_id, keepdims=True))
    mean_cross = lax.optimization_barrier(jnp.mean(upstream * scaled, axis=axis_id, keepdims=True))
    return inv_std * (upstream - mean_up - scaled * mean_cross)

def linear(form, left, right):
    return jnp.einsum(form, left.astype(jnp.float32), right.astype(jnp.float32), precision=lax.Precision.HIGHEST)

def reference(pair_input, d_update, token_mask, ln_in_gain, ln_in_bias, w_ab, w_gate, ln_out_gain, ln_out_bias, w_out):
    token_valid = token_mask.astype(jnp.float32)
    pair_mask = (token_valid[:, None] * token_valid[None, :])[:, :, None]
    z_hat, inv_in = norm_stats(pair_input.astype(jnp.float32), 2)
    normed = (z_hat * ln_in_gain + ln_in_bias).astype(jnp.bfloat16)
    value_a = linear('rnc,ce->rne', normed, w_ab[:, 0:H])
    gate_a = linear('rnc,ce->rne', normed, w_ab[:, H:2 * H])
    value_b = linear('rnc,ce->rne', normed, w_ab[:, 2 * H:3 * H])
    gate_b = linear('rnc,ce->rne', normed, w_ab[:, 3 * H:4 * H])
    sig_a = jax.nn.sigmoid(gate_a)
    sig_b = jax.nn.sigmoid(gate_b)
    factor_a = (pair_mask * sig_a * value_a).astype(jnp.bfloat16)
    factor_b = (pair_mask * sig_b * value_b).astype(jnp.bfloat16)
    gate = jax.nn.sigmoid(linear('rnc,cd->rnd', normed, w_gate))
    product = linear('ikh,jkh->ijh', factor_a, factor_b).astype(jnp.bfloat16)
    x_hat, inv_std = norm_stats(product.astype(jnp.float32), 2)
    x_norm = (x_hat * ln_out_gain + ln_out_bias).astype(jnp.bfloat16)
    out_lin = linear('rne,ec->rnc', x_norm, w_out)
    upstream = d_update.astype(jnp.float32)
    grad_lin = (upstream * gate).astype(jnp.bfloat16)
    gate_back = (upstream * out_lin * gate * (1.0 - gate)).astype(jnp.bfloat16)
    grad_xnorm = linear('rnc,ec->rne', grad_lin, w_out)
    grad_prod = norm_back(grad_xnorm * ln_out_gain, x_hat, inv_std, 2).astype(jnp.bfloat16)
    grad_fac_a = linear('ijh,jkh->ikh', grad_prod, factor_b).astype(jnp.bfloat16)
    grad_fac_b = linear('ijh,ikh->jkh', grad_prod, factor_a).astype(jnp.bfloat16)
    masked_a = grad_fac_a.astype(jnp.float32) * pair_mask
    masked_b = grad_fac_b.astype(jnp.float32) * pair_mask
    grad_proj = jnp.concatenate([masked_a * sig_a, masked_a * value_a * sig_a * (1.0 - sig_a), masked_b * sig_b, masked_b * value_b * sig_b * (1.0 - sig_b)], axis=2).astype(jnp.bfloat16)
    grad_normed = linear('rne,ce->rnc', grad_proj, w_ab) + linear('rnd,cd->rnc', gate_back, w_gate)
    pair_grad = norm_back(grad_normed * ln_in_gain, z_hat, inv_in, 2).astype(jnp.bfloat16)
    grad_w_ab = linear('rnc,rne->ce', normed, grad_proj) / N
    grad_w_gate = linear('rnc,rnd->cd', normed, gate_back) / N
    grad_w_out = linear('rne,rnc->ec', x_norm, grad_lin) / N
    return (pair_grad, grad_w_ab, grad_w_gate, grad_w_out)
```

```python
import functools

import jax
import jax.numpy as jnp
from jax import lax
from jax.experimental import pallas as pl
from jax.experimental.pallas import tpu as pltpu
from jax.sharding import PartitionSpec as P

EPS = 1e-05
F32 = jnp.float32
BF16 = jnp.bfloat16
NN = (((1,), (0,)), ((), ()))
NT = (((1,), (1,)), ((), ()))
TN = (((0,), (0,)), ((), ()))


def params(steps):
    return pltpu.CompilerParams(
        dimension_semantics=("arbitrary",) * steps, vmem_limit_bytes=50 * 1024 * 1024
    )


def dot(left, right, form=NN):
    return lax.dot_general(left, right, form, preferred_element_type=F32)


def sigmoid(value):
    return 0.5 * jnp.tanh(0.5 * value) + 0.5


def col_mean(value):
    return jnp.mean(value, axis=0, keepdims=True)


def stats(value):
    centered = value - col_mean(value)
    inv_std = lax.rsqrt(col_mean(centered * centered) + EPS)
    return centered * inv_std, inv_std


def norm_back(upstream, scaled, inv_std):
    return inv_std * (upstream - col_mean(upstream) - scaled * col_mean(upstream * scaled))


def turned(ref, row):
    return ref[row].astype(F32).T


def factors_kernel(x_ref, mask_ref, gain_ref, bias_ref, w_ref, fa_ref, fb_ref, sa_ref, sb_ref):
    rows, cols, chans = x_ref.shape
    hidden = fa_ref.shape[0]

    @pl.loop(0, rows)
    def _(row):
        z_hat, _ = stats(turned(x_ref, row))
        normed = (z_hat * gain_ref[...] + bias_ref[...]).astype(BF16)
        mask = mask_ref[pl.ds(row, 1), :]
        proj = dot(w_ref[...], normed)
        value_a, gate_a = proj[:hidden], proj[hidden : 2 * hidden]
        value_b, gate_b = proj[2 * hidden : 3 * hidden], proj[3 * hidden :]
        store_rows(sa_ref, row, rows, mask * sigmoid(gate_a) * value_a)
        store_rows(sb_ref, row, rows, mask * sigmoid(gate_b) * value_b)

    gather_out(sa_ref, fa_ref)
    gather_out(sb_ref, fb_ref)


def store_rows(ref, row, rows, value):
    hidden = value.shape[0]
    for lane in range(ref.shape[0]):
        ref[lane, pl.ds(row, hidden, stride=rows), :] = value[:, lane * 128 : (lane + 1) * 128]


def load_rows(ref, row, rows):
    hidden = ref.shape[1] // rows
    return jnp.concatenate(
        [ref[lane, pl.ds(row, hidden, stride=rows), :] for lane in range(ref.shape[0])], axis=1
    )


def gather_out(scratch, out_ref):
    hidden, rows, cols = out_ref.shape
    for lane in range(scratch.shape[0]):
        out_ref[:, :, lane * 128 : (lane + 1) * 128] = (
            scratch[lane].reshape(hidden, rows, 128).astype(BF16)
        )


def spread_in(in_ref, scratch):
    hidden, rows, cols = in_ref.shape
    for lane in range(scratch.shape[0]):
        scratch[lane] = (
            in_ref[:, :, lane * 128 : (lane + 1) * 128].astype(F32).reshape(hidden * rows, 128)
        )


def whole(array):
    return pl.BlockSpec(array.shape, lambda *_: (0,) * array.ndim)


def row_block(rows, cols, chans):
    return pl.BlockSpec((rows, cols, chans), lambda i, j: (i, j, 0))


def chan_block(hidden, rows, cols):
    return pl.BlockSpec((hidden, rows, cols), lambda i, j: (0, i, j))


def plane(rows, cols):
    return pltpu.VMEM((cols // 128, rows * 128, 128), F32)


def make_factors(x, mask, gain, bias, w_t, rows, cols):
    count, crop, chans = x.shape
    hidden = w_t.shape[0] // 4
    out = jax.ShapeDtypeStruct((hidden, count, crop), BF16)
    return pl.pallas_call(
        factors_kernel,
        grid=(count // rows, crop // cols),
        in_specs=[
            row_block(rows, cols, chans),
            pl.BlockSpec((rows, cols), lambda i, j: (i, j)),
            whole(gain),
            whole(bias),
            whole(w_t),
        ],
        out_specs=[chan_block(hidden, rows, cols)] * 2,
        out_shape=[out, out],
        scratch_shapes=[pltpu.VMEM((cols // 128, rows * hidden, 128), F32)] * 2,
        compiler_params=params(2),
        name="factors",
    )(x, mask, gain, bias, w_t)


def product_kernel(a_ref, b_ref, p_ref):
    src, _, rows, crop = a_ref.shape
    a = a_ref[...].reshape(src * rows, crop)
    b = b_ref[...].reshape(crop, crop)
    p_ref[...] = dot(a, b, NT).astype(BF16).reshape(p_ref.shape)


def own_block(array):
    src, _, rows, crop = array.shape
    return pl.BlockSpec((src, 1, rows, crop), lambda h: (0, h, 0, 0))


def make_product(a, b):
    return pl.pallas_call(
        product_kernel,
        grid=(a.shape[1],),
        in_specs=[own_block(a), own_block(b)],
        out_specs=own_block(a),
        out_shape=jax.ShapeDtypeStruct(a.shape, BF16),
        compiler_params=params(1),
        name="product",
    )(a, b)


def back_kernel(g_ref, a_ref, b_ref, da_ref, db_ref):
    src, _, rows, crop = a_ref.shape
    g = g_ref[...].reshape(src * rows, crop)
    a = a_ref[...].reshape(src * rows, crop)
    b = b_ref[...].reshape(crop, crop)
    da_ref[...] = dot(g, b).astype(BF16).reshape(da_ref.shape)
    db_ref[...] = dot(g, a, TN).astype(BF16).reshape(db_ref.shape)


def make_back(g, a, b):
    return pl.pallas_call(
        back_kernel,
        grid=(a.shape[1],),
        in_specs=[own_block(g), own_block(a), own_block(b)],
        out_specs=[own_block(a), own_block(b)],
        out_shape=[jax.ShapeDtypeStruct(a.shape, BF16), jax.ShapeDtypeStruct(b.shape, BF16)],
        compiler_params=params(1),
        name="back",
    )(g, a, b)


def middle_kernel(
    x_ref, d_ref, p_ref, gain_ref, bias_ref, wg_ref, og_ref, ob_ref, wo_ref, wot_ref,
    g_ref, gb_ref, gwo_ref, gwg_ref, s_ref,
):
    rows, cols, chans = x_ref.shape

    @pl.when((pl.program_id(0) == 0) & (pl.program_id(1) == 0))
    def _():
        gwo_ref[...] = jnp.zeros_like(gwo_ref)
        gwg_ref[...] = jnp.zeros_like(gwg_ref)

    spread_in(p_ref, s_ref)

    @pl.loop(0, rows)
    def _(row):
        z_hat, _ = stats(turned(x_ref, row))
        normed = (z_hat * gain_ref[...] + bias_ref[...]).astype(BF16)
        gate = sigmoid(dot(wg_ref[...], normed))
        x_hat, inv_std = stats(load_rows(s_ref, row, rows))
        x_norm = (x_hat * og_ref[...] + ob_ref[...]).astype(BF16)
        out_lin = dot(wot_ref[...], x_norm)
        lin = turned(d_ref, row) * gate
        grad_lin = lin.astype(BF16)
        gate_back = (lin * out_lin * (1.0 - gate)).astype(BF16)
        upstream = dot(wo_ref[...], grad_lin) * og_ref[...]
        store_rows(s_ref, row, rows, norm_back(upstream, x_hat, inv_std))
        gb_ref[row] = gate_back
        gwo_ref[...] += dot(x_norm, grad_lin, NT)
        gwg_ref[...] += dot(normed, gate_back, NT)

    gather_out(s_ref, g_ref)


def make_middle(x, d, p, gain, bias, w_gate_t, out_gain, out_bias, w_out, w_out_t, rows, cols):
    count, crop, chans = x.shape
    hidden = w_out.shape[0]
    grads = [jax.ShapeDtypeStruct((hidden, chans), F32), jax.ShapeDtypeStruct((chans, chans), F32)]
    small = [gain, bias, w_gate_t, out_gain, out_bias, w_out, w_out_t]
    return pl.pallas_call(
        middle_kernel,
        grid=(count // rows, crop // cols),
        in_specs=[row_block(rows, cols, chans)] * 2
        + [chan_block(hidden, rows, cols)]
        + [whole(value) for value in small],
        out_specs=[
            chan_block(hidden, rows, cols),
            pl.BlockSpec((rows, chans, cols), lambda i, j: (i, 0, j)),
        ]
        + [whole(value) for value in grads],
        out_shape=[
            jax.ShapeDtypeStruct((hidden, count, crop), BF16),
            jax.ShapeDtypeStruct((count, chans, crop), BF16),
        ]
        + grads,
        scratch_shapes=[pltpu.VMEM((cols // 128, rows * hidden, 128), F32)],
        compiler_params=params(2),
        name="middle",
    )(x, d, p, *small)


def last_kernel(
    x_ref, mask_ref, ga_ref, gb_ref, gate_ref, gain_ref, bias_ref, wt_ref, wcat_ref,
    out_ref, gw_ref, sa_ref, sb_ref,
):
    rows, cols, chans = x_ref.shape
    hidden = ga_ref.shape[0]

    @pl.when((pl.program_id(0) == 0) & (pl.program_id(1) == 0))
    def _():
        gw_ref[...] = jnp.zeros_like(gw_ref)

    spread_in(ga_ref, sa_ref)
    spread_in(gb_ref, sb_ref)

    @pl.loop(0, rows)
    def _(row):
        z_hat, inv_in = stats(turned(x_ref, row))
        normed = (z_hat * gain_ref[...] + bias_ref[...]).astype(BF16)
        mask = mask_ref[pl.ds(row, 1), :]
        proj = dot(wt_ref[...], normed)
        sides = []
        for side, ref in enumerate((sa_ref, sb_ref)):
            value = proj[2 * side * hidden : (2 * side + 1) * hidden]
            sig = sigmoid(proj[(2 * side + 1) * hidden : (2 * side + 2) * hidden])
            to_value = load_rows(ref, row, rows) * mask * sig
            sides += [to_value.astype(BF16), (to_value * value * (1.0 - sig)).astype(BF16)]
        grad_proj = jnp.concatenate(sides, axis=0)
        every = jnp.concatenate([grad_proj, gate_ref[row]], axis=0)
        upstream = dot(wcat_ref[...], every) * gain_ref[...]
        out_ref[row] = norm_back(upstream, z_hat, inv_in).T.astype(BF16)
        gw_ref[...] += dot(normed, grad_proj, NT)


def make_last(x, mask, grad_a, grad_b, gate_back, gain, bias, w_t, w_cat, rows, cols):
    count, crop, chans = x.shape
    hidden = w_t.shape[0] // 4
    grad = jax.ShapeDtypeStruct((chans, 4 * hidden), F32)
    small = [gain, bias, w_t, w_cat]
    return pl.pallas_call(
        last_kernel,
        grid=(count // rows, crop // cols),
        in_specs=[
            row_block(rows, cols, chans),
            pl.BlockSpec((rows, cols), lambda i, j: (i, j)),
            chan_block(hidden, rows, cols),
            chan_block(hidden, rows, cols),
            pl.BlockSpec((rows, chans, cols), lambda i, j: (i, 0, j)),
        ]
        + [whole(value) for value in small],
        out_specs=[row_block(rows, cols, chans), whole(grad)],
        out_shape=[jax.ShapeDtypeStruct(x.shape, BF16), grad],
        scratch_shapes=[pltpu.VMEM((cols // 128, rows * hidden, 128), F32)] * 2,
        compiler_params=params(2),
        name="last",
    )(x, mask, grad_a, grad_b, gate_back, *small)


def swap(array):
    return lax.all_to_all(array, "tile", split_axis=0, concat_axis=0, tiled=True)


def tile_sum(array, tiles):
    chans, width = array.shape
    parts = swap(array.astype(BF16)).reshape(tiles, chans // tiles, width)
    part = jnp.sum(parts.astype(F32), axis=0).astype(BF16)
    return swap(jnp.broadcast_to(part[None], (tiles,) + part.shape).reshape(chans, width)).astype(F32)


def body(
    tiles, x, d, token_mask, ln_in_gain, ln_in_bias, w_ab, w_gate, ln_out_gain, ln_out_bias, w_out
):
    count, crop, chans = x.shape
    hidden = w_out.shape[0]
    rows, cols = 16, 256
    valid = token_mask.astype(F32)
    own_valid = lax.dynamic_slice_in_dim(valid, lax.axis_index("tile") * count, count)
    mask = own_valid[:, None] * valid[None, :]
    gain, bias = ln_in_gain[:, None], ln_in_bias[:, None]
    out_gain, out_bias = ln_out_gain[:, None], ln_out_bias[:, None]
    w_t = w_ab.T
    w_cat = jnp.concatenate([w_ab, w_gate], axis=1)
    owned = (tiles, hidden // tiles, count, crop)

    factor_a, factor_b = make_factors(x, mask, gain, bias, w_t, rows, cols)
    owner_a = swap(factor_a).reshape(owned)
    owner_b = swap(factor_b).reshape(owned)
    owner_p = make_product(owner_a, owner_b)
    product = swap(owner_p.reshape(hidden, count, crop))
    grad_prod, gate_back, local_out, local_gate = make_middle(
        x, d, product, gain, bias, w_gate.T, out_gain, out_bias, w_out, w_out.T, rows, cols
    )
    owner_g = swap(grad_prod).reshape(owned)
    owner_da, owner_db = make_back(owner_g, owner_a, owner_b)
    grad_a = swap(owner_da.reshape(hidden, count, crop))
    grad_b = swap(owner_db.reshape(hidden, count, crop))
    pair_grad, local_ab = make_last(
        x, mask, grad_a, grad_b, gate_back, gain, bias, w_t, w_cat, rows, cols
    )
    local = jnp.concatenate([local_ab, local_gate, local_out], axis=1)
    total = tile_sum(local, tiles) / crop
    width = 4 * hidden
    return (pair_grad, total[:, :width], total[:, width : width + chans], total[:, width + chans :])


def solution(mesh):
    pairs = P(("crops", "tile"), None, None)
    return jax.shard_map(
        functools.partial(body, mesh.shape["tile"]),
        mesh=mesh,
        in_specs=(pairs, pairs, P("crops")) + (P(),) * 7,
        out_specs=(pairs,) + (P("crops", None),) * 3,
        check_vma=False,
    )
```

```python
import functools

import jax
import jax.numpy as jnp
from jax import lax
from jax.experimental import pallas as pl
from jax.experimental.pallas import tpu as pltpu
from jax.sharding import PartitionSpec as P

EPS = 1e-05
F32 = jnp.float32
BF16 = jnp.bfloat16
NN = (((1,), (0,)), ((), ()))
NT = (((1,), (1,)), ((), ()))
TN = (((0,), (0,)), ((), ()))


def params(steps):
    return pltpu.CompilerParams(
        dimension_semantics=("arbitrary",) * steps, vmem_limit_bytes=50 * 1024 * 1024
    )


def dot(left, right, form=NN):
    return lax.dot_general(left, right, form, preferred_element_type=F32)


def sigmoid(value):
    return 0.5 * jnp.tanh(0.5 * value) + 0.5


def col_mean(value):
    return jnp.mean(value, axis=0, keepdims=True)


def stats(value):
    centered = value - col_mean(value)
    inv_std = lax.rsqrt(col_mean(centered * centered) + EPS)
    return centered * inv_std, inv_std


def norm_back(upstream, scaled, inv_std):
    return inv_std * (upstream - col_mean(upstream) - scaled * col_mean(upstream * scaled))


def turned(ref, row, count):
    block = ref[pl.ds(row, count)]
    return block.reshape(-1, block.shape[-1]).astype(F32).T


def lane_parts(scratch, count):
    return [(at, lane) for at in range(count) for lane in range(scratch.shape[0])]


def store_rows(scratch, row, count, rows, value):
    hidden = value.shape[0]
    for part, (at, lane) in enumerate(lane_parts(scratch, count)):
        scratch[lane, pl.ds(row + at, hidden, stride=rows), :] = value[:, part * 128 : (part + 1) * 128]


def load_rows(scratch, row, count, rows):
    hidden = scratch.shape[1] // rows
    return jnp.concatenate(
        [
            scratch[lane, pl.ds(row + at, hidden, stride=rows), :]
            for at, lane in lane_parts(scratch, count)
        ],
        axis=1,
    )


def gather_out(scratch, out_ref):
    hidden, rows, cols = out_ref.shape
    for lane in range(scratch.shape[0]):
        out_ref[:, :, lane * 128 : (lane + 1) * 128] = (
            scratch[lane].reshape(hidden, rows, 128).astype(BF16)
        )


def spread_in(in_ref, scratch):
    hidden, rows, cols = in_ref.shape
    for lane in range(scratch.shape[0]):
        scratch[lane] = (
            in_ref[:, :, lane * 128 : (lane + 1) * 128].astype(F32).reshape(hidden * rows, 128)
        )


def flat_rows(ref, row, count):
    return jnp.concatenate([ref[pl.ds(row + at, 1), :] for at in range(count)], axis=1)


def whole(array):
    return pl.BlockSpec(array.shape, lambda *_: (0,) * array.ndim)


class Plan:
    def __init__(self, tiles, count, crop):
        self.tiles, self.count, self.crop = tiles, count, crop
        self.half = tiles // 2
        self.subs = 2 if count % 32 == 0 else 1
        self.rows = count // self.subs
        self.width = self.half * self.rows
        self.blocks = crop // self.width
        self.step = max(1, 512 // self.width)
        self.groups = [
            [side * self.half + at for at in range(self.half)] for side in range(2)
        ]
        self.partner = [(at, (at + self.half) % tiles) for at in range(tiles)]

    def view(self, array):
        return array.reshape(self.count, self.tiles, self.subs, self.rows, array.shape[-1])

    def pair_spec(self, chans, index):
        return pl.BlockSpec((self.rows, self.half, 1, self.rows, chans), index)

    def scratch(self, hidden):
        return pltpu.VMEM((self.width // 128, self.rows * hidden, 128), F32)

    def swap(self, array):
        return lax.all_to_all(
            array, "tile", split_axis=0, concat_axis=0, axis_index_groups=self.groups, tiled=True
        )

    def exchange(self, array):
        return lax.ppermute(array, "tile", self.partner)


def factors_kernel(step, x_ref, mask_ref, gain_ref, bias_ref, w_ref, fa_ref, fb_ref, sa_ref, sb_ref):
    rows = x_ref.shape[0]
    hidden = fa_ref.shape[0]

    @pl.loop(0, rows // step)
    def _(turn):
        row = pl.multiple_of(turn * step, step)
        z_hat, _ = stats(turned(x_ref, row, step))
        normed = (z_hat * gain_ref[...] + bias_ref[...]).astype(BF16)
        mask = flat_rows(mask_ref, row, step)
        proj = dot(w_ref[...], normed)
        value_a, gate_a = proj[:hidden], proj[hidden : 2 * hidden]
        value_b, gate_b = proj[2 * hidden : 3 * hidden], proj[3 * hidden :]
        store_rows(sb_ref, row, step, rows, mask * sigmoid(gate_b) * value_b)
        store_rows(sa_ref, row, step, rows, mask * sigmoid(gate_a) * value_a)

    gather_out(sa_ref, fa_ref)
    gather_out(sb_ref, fb_ref)


def make_factors(plan, sub, x, mask, gain, bias, w_t):
    chans = x.shape[-1]
    hidden = w_t.shape[0] // 4
    out = jax.ShapeDtypeStruct((hidden, plan.rows, plan.crop), BF16)
    out_spec = pl.BlockSpec((hidden, plan.rows, plan.width), lambda j: (0, 0, j))
    return pl.pallas_call(
        functools.partial(factors_kernel, plan.step),
        grid=(plan.blocks,),
        in_specs=[
            plan.pair_spec(chans, lambda j: (sub, j % 2, j // 2, 0, 0)),
            pl.BlockSpec((plan.rows, plan.width), lambda j: (sub, j)),
            whole(gain),
            whole(bias),
            whole(w_t),
        ],
        out_specs=[out_spec] * 2,
        out_shape=[out, out],
        scratch_shapes=[plan.scratch(hidden)] * 2,
        compiler_params=params(1),
        name="factors",
    )(x, mask, gain, bias, w_t)


def matrix(refs):
    parts = [ref[...].reshape(-1, ref.shape[-1]) for ref in refs]
    return jnp.concatenate(parts, axis=0) if len(parts) > 1 else parts[0]


def by_sub(ref, subs):
    rows = ref.shape[2] // subs
    parts = [
        ref[:, 0, sub * rows : (sub + 1) * rows, :].reshape(-1, ref.shape[3]) for sub in range(subs)
    ]
    return jnp.concatenate(parts, axis=0) if subs > 1 else parts[0]


def to_subs(ref, value, subs):
    tiles, _, rows, cols = ref.shape
    part = value.shape[0] // subs
    for sub in range(subs):
        ref[:, 0, sub * (rows // subs) : (sub + 1) * (rows // subs), :] = value[
            sub * part : (sub + 1) * part
        ].astype(BF16).reshape(tiles, rows // subs, cols)


def own_spec(array):
    src, _, rows, cols = array.shape
    return pl.BlockSpec((src, 1, rows, cols), lambda h: (0, h, 0, 0))


def product_kernel(subs, count, *refs):
    a, b, p_ref = refs[:subs], refs[subs : subs + count], refs[subs + count]
    to_subs(p_ref, dot(matrix(a), matrix(b), NT), subs)


def make_product(plan, a, b):
    tiles, chans, rows, _ = a[0].shape
    out = jax.ShapeDtypeStruct((tiles, chans, plan.count, len(b) * plan.width), BF16)
    return pl.pallas_call(
        functools.partial(product_kernel, plan.subs, len(b)),
        grid=(chans,),
        in_specs=[own_spec(value) for value in (*a, *b)],
        out_specs=own_spec(out),
        out_shape=out,
        compiler_params=params(1),
        name="product",
    )(*a, *b)


def grad_b_kernel(subs, g_ref, *refs):
    a, outs = refs[:subs], refs[subs:]
    grad = dot(by_sub(g_ref, subs), matrix(a), TN).astype(BF16)
    size = grad.shape[0] // len(outs)
    for at, out in enumerate(outs):
        out[...] = grad[at * size : (at + 1) * size].reshape(out.shape)


def make_grad_b(plan, g, a):
    outs = g.shape[-1] // plan.width
    return pl.pallas_call(
        functools.partial(grad_b_kernel, plan.subs),
        grid=(g.shape[1],),
        in_specs=[own_spec(value) for value in (g, *a)],
        out_specs=[own_spec(a[0])] * outs,
        out_shape=[jax.ShapeDtypeStruct(a[0].shape, BF16)] * outs,
        compiler_params=params(1),
        name="grad_b",
    )(g, *a)


def grad_a_kernel(subs, count, *refs):
    g, b, out = refs[:count], refs[count:-1], refs[-1]
    rows = jnp.concatenate([by_sub(ref, subs) for ref in g], axis=1)
    to_subs(out, dot(rows, matrix(b)), subs)


def make_grad_a(plan, g, b):
    tiles, chans, _, _ = b[0].shape
    out = jax.ShapeDtypeStruct((tiles, chans, plan.count, plan.crop), BF16)
    return pl.pallas_call(
        functools.partial(grad_a_kernel, plan.subs, len(g)),
        grid=(chans,),
        in_specs=[own_spec(value) for value in (*g, *b)],
        out_specs=own_spec(out),
        out_shape=out,
        compiler_params=params(1),
        name="grad_a",
    )(*g, *b)


def middle_kernel(
    step, _, x_ref, d_ref, p_ref, gain_ref, bias_ref, wg_ref, og_ref, ob_ref, wo_ref, wot_ref, *refs
):
    g_ref, gb_ref, gwo_ref, gwg_ref, s_ref = refs[-5:]
    rows = x_ref.shape[0]
    width = gb_ref.shape[-1]

    @pl.when((pl.program_id(0) == 0) & (pl.program_id(1) == 0))
    def _():
        gwo_ref[...] = jnp.zeros_like(gwo_ref)
        gwg_ref[...] = jnp.zeros_like(gwg_ref)

    spread_in(p_ref, s_ref)

    @pl.loop(0, rows // step)
    def _(turn):
        row = pl.multiple_of(turn * step, step)
        z_hat, _ = stats(turned(x_ref, row, step))
        normed = (z_hat * gain_ref[...] + bias_ref[...]).astype(BF16)
        gate = sigmoid(dot(wg_ref[...], normed))
        x_hat, inv_std = stats(load_rows(s_ref, row, step, rows))
        x_norm = (x_hat * og_ref[...] + ob_ref[...]).astype(BF16)
        out_lin = dot(wot_ref[...], x_norm)
        lin = turned(d_ref, row, step) * gate
        grad_lin = lin.astype(BF16)
        gate_back = (lin * out_lin * (1.0 - gate)).astype(BF16)
        upstream = dot(wo_ref[...], grad_lin) * og_ref[...]
        store_rows(s_ref, row, step, rows, norm_back(upstream, x_hat, inv_std))
        for at in range(step):
            gb_ref[row + at] = gate_back[:, at * width : (at + 1) * width]
        gwo_ref[...] += dot(x_norm, grad_lin, NT)
        gwg_ref[...] += dot(normed, gate_back, NT)

    gather_out(s_ref, g_ref)


def make_middle(plan, table, before, x, d, p, small):
    chans = x.shape[-1]
    hidden = p.shape[0]
    cut = table.shape[0]
    grads = [jax.ShapeDtypeStruct((hidden, chans), F32), jax.ShapeDtypeStruct((chans, chans), F32)]
    pairs = plan.pair_spec(chans, lambda i, j, at: (i, at[j, 0], at[j, 1], 0, 0))
    channel = pl.BlockSpec((hidden, plan.rows, plan.width), lambda i, j, at: (0, i, j))
    kept = [] if before is None else [before]
    return pl.pallas_call(
        functools.partial(middle_kernel, plan.step),
        grid_spec=pltpu.PrefetchScalarGridSpec(
            num_scalar_prefetch=1,
            grid=(plan.subs, cut),
            in_specs=[pairs, pairs, channel]
            + [whole(value) for value in small]
            + [pl.BlockSpec(memory_space=pl.ANY) for _ in kept],
            out_specs=[
                channel,
                pl.BlockSpec(
                    (plan.rows, chans, plan.width),
                    lambda i, j, at: (i, 0, at[j, 1] * 2 + at[j, 0]),
                ),
            ]
            + [whole(value) for value in grads],
            scratch_shapes=[plan.scratch(hidden)],
        ),
        out_shape=[
            jax.ShapeDtypeStruct(p.shape, BF16),
            jax.ShapeDtypeStruct((plan.count, chans, plan.crop), BF16),
        ]
        + grads,
        input_output_aliases={4 + len(small): 1} if kept else {},
        compiler_params=params(2),
        name="middle",
    )(table, x, d, p, *small, *kept)


def last_kernel(
    step, x_ref, mask_ref, ga_ref, gb_ref, gate_ref, gain_ref, bias_ref, wt_ref, wcat_ref, *refs
):
    out_ref, gw_ref, sa_ref, sb_ref = refs[-4:]
    rows = x_ref.shape[0]
    hidden = ga_ref.shape[0]

    @pl.when(pl.program_id(0) == 0)
    def _():
        gw_ref[...] = jnp.zeros_like(gw_ref)

    spread_in(ga_ref, sa_ref)
    spread_in(gb_ref, sb_ref)

    @pl.loop(0, rows // step)
    def _(turn):
        row = pl.multiple_of(turn * step, step)
        z_hat, inv_in = stats(turned(x_ref, row, step))
        normed = (z_hat * gain_ref[...] + bias_ref[...]).astype(BF16)
        mask = flat_rows(mask_ref, row, step)
        proj = dot(wt_ref[...], normed)
        sides = []
        for side, ref in enumerate((sa_ref, sb_ref)):
            value = proj[2 * side * hidden : (2 * side + 1) * hidden]
            sig = sigmoid(proj[(2 * side + 1) * hidden : (2 * side + 2) * hidden])
            to_value = load_rows(ref, row, step, rows) * mask * sig
            sides += [to_value.astype(BF16), (to_value * value * (1.0 - sig)).astype(BF16)]
        grad_proj = jnp.concatenate(sides, axis=0)
        gate_back = jnp.concatenate([gate_ref[row + at] for at in range(step)], axis=1)
        every = jnp.concatenate([grad_proj, gate_back], axis=0)
        upstream = dot(wcat_ref[...], every) * gain_ref[...]
        grad = norm_back(upstream, z_hat, inv_in).T.astype(BF16)
        out_ref[pl.ds(row, step)] = grad.reshape((step,) + out_ref.shape[1:])
        gw_ref[...] += dot(normed, grad_proj, NT)


def make_last(plan, sub, before, x, mask, grad_a, grad_b, gate_back, small):
    chans = x.shape[-1]
    hidden = grad_a.shape[0]
    grad = jax.ShapeDtypeStruct((chans, 4 * hidden), F32)
    pairs = plan.pair_spec(chans, lambda j: (sub, j % 2, j // 2, 0, 0))
    channel = (hidden, plan.rows, plan.width)
    kept = [] if before is None else [before]
    return pl.pallas_call(
        functools.partial(last_kernel, plan.step),
        grid=(plan.blocks,),
        in_specs=[
            pairs,
            pl.BlockSpec((plan.rows, plan.width), lambda j: (sub, j)),
            pl.BlockSpec(channel, lambda j: (0, sub, j)),
            pl.BlockSpec(channel, lambda j: (0, 0, j)),
            pl.BlockSpec((plan.rows, chans, plan.width), lambda j: (sub, 0, j)),
        ]
        + [whole(value) for value in small]
        + [pl.BlockSpec(memory_space=pl.ANY) for _ in kept],
        out_specs=[pairs, whole(grad)],
        out_shape=[jax.ShapeDtypeStruct(x.shape, BF16), grad],
        scratch_shapes=[plan.scratch(hidden)] * 2,
        input_output_aliases={5 + len(small): 0} if kept else {},
        compiler_params=params(1),
        name="last",
    )(x, mask, grad_a, grad_b, gate_back, *small, *kept)


def swap_all(array):
    return lax.all_to_all(array, "tile", split_axis=0, concat_axis=0, tiled=True)


def tile_sum(array, tiles):
    chans, width = array.shape
    parts = swap_all(array.astype(BF16)).reshape(tiles, chans // tiles, width)
    part = jnp.sum(parts.astype(F32), axis=0).astype(BF16)
    spread = jnp.broadcast_to(part[None], (tiles,) + part.shape).reshape(chans, width)
    return swap_all(spread).astype(F32)


def body(
    tiles, x, d, token_mask, ln_in_gain, ln_in_bias, w_ab, w_gate, ln_out_gain, ln_out_bias, w_out
):
    count, crop, chans = x.shape
    hidden = w_out.shape[0]
    plan = Plan(tiles, count, crop)
    me = lax.axis_index("tile")
    side = (me // plan.half).astype(jnp.int32)
    valid = token_mask.astype(F32)
    own_valid = lax.dynamic_slice_in_dim(valid, me * count, count)
    turned_valid = valid.reshape(tiles, plan.subs, plan.rows).transpose(1, 0, 2).reshape(crop)
    mask = own_valid[:, None] * turned_valid[None, :]
    gain, bias = ln_in_gain[:, None], ln_in_bias[:, None]
    w_t = w_ab.T
    w_cat = jnp.concatenate([w_ab, w_gate], axis=1)
    mid = [gain, bias, w_gate.T, ln_out_gain[:, None], ln_out_bias[:, None], w_out, w_out.T]
    x, d = plan.view(x), plan.view(d)
    owned = lambda array: array.reshape(plan.half, hidden // plan.half, *array.shape[1:])
    joined = lambda array: array.reshape(hidden, *array.shape[2:])
    every = range(plan.subs)

    own_a, own_b, other_b = [], [], []
    for sub in every:
        factor_a, factor_b = make_factors(plan, sub, x, mask, gain, bias, w_t)
        own_b.append(owned(plan.swap(factor_b)))
        other_b.append(plan.exchange(own_b[sub]))
        own_a.append(owned(plan.swap(factor_a)))

    gate_back, local_mid, owner_g, grad_own, grad_other = None, [], [], [], []
    turns = [([sub], [(1 - side, sub)], [other_b[sub]]) for sub in every]
    turns += [(list(every), [(side, sub) for sub in every], own_b)]
    for which, (subs, at, b) in enumerate(turns):
        table = jnp.stack([jnp.stack([half, jnp.int32(sub)]) for half, sub in at])
        product = plan.swap(joined(make_product(plan, own_a, b)))
        grad_prod, gate_back, *local = make_middle(plan, table, gate_back, x, d, product, mid)
        local_mid.append(jnp.concatenate(local[::-1], axis=1))
        owner_g.append(owned(plan.swap(grad_prod)))
        grads = make_grad_b(plan, owner_g[which], own_a)
        if which < plan.subs:
            grad_other.append(plan.exchange(grads[0]))
        else:
            grad_own = grads
    sum_mid = tile_sum(sum(local_mid), tiles) / crop
    grad_a = plan.swap(joined(make_grad_a(plan, owner_g, other_b + own_b)))
    pair_grad, local_ab = None, []
    for sub in every:
        whole_b = (grad_own[sub].astype(F32) + grad_other[sub].astype(F32)).astype(BF16)
        grad_b = plan.swap(joined(whole_b))
        pair_grad, local = make_last(
            plan, sub, pair_grad, x, mask, grad_a, grad_b, gate_back, [gain, bias, w_t, w_cat]
        )
        local_ab.append(local)
    sum_ab = tile_sum(sum(local_ab), tiles) / crop
    return (pair_grad.reshape(count, crop, chans), sum_ab, sum_mid[:, :chans], sum_mid[:, chans:])


def solution(mesh):
    pairs = P(("crops", "tile"), None, None)
    return jax.shard_map(
        functools.partial(body, mesh.shape["tile"]),
        mesh=mesh,
        in_specs=(pairs, pairs, P("crops")) + (P(),) * 7,
        out_specs=(pairs,) + (P("crops", None),) * 3,
        check_vma=False,
    )
```

```python
import functools

import jax
import jax.numpy as jnp
from jax import lax
from jax.experimental import pallas as pl
from jax.experimental.pallas import tpu as pltpu
from jax.sharding import PartitionSpec as P

EPS = 1e-05
CHANS = 4
F32 = jnp.float32
BF16 = jnp.bfloat16
NN = (((1,), (0,)), ((), ()))
NT = (((1,), (1,)), ((), ()))
TN = (((0,), (0,)), ((), ()))


def params(steps):
    return pltpu.CompilerParams(
        dimension_semantics=("arbitrary",) * steps, vmem_limit_bytes=50 * 1024 * 1024
    )


def cost(micros):
    return pl.CostEstimate(
        flops=int(micros * 1.0e9), bytes_accessed=int(micros * 3.0e6), transcendentals=0
    )


def dot(left, right, form=NN):
    return lax.dot_general(left, right, form, preferred_element_type=F32)


def sigmoid(value):
    return 0.5 * jnp.tanh(0.5 * value) + 0.5


def col_mean(value):
    return jnp.mean(value, axis=0, keepdims=True)


def stats(value):
    centered = value - col_mean(value)
    inv_std = lax.rsqrt(col_mean(centered * centered) + EPS)
    return centered * inv_std, inv_std


def norm_back(upstream, scaled, inv_std):
    return inv_std * (upstream - col_mean(upstream) - scaled * col_mean(upstream * scaled))


def turned(ref, row, count):
    block = ref[pl.ds(row, count)]
    return block.reshape(-1, block.shape[-1]).astype(F32).T


def lane_parts(scratch, count):
    return [(at, lane) for at in range(count) for lane in range(scratch.shape[0])]


def store_rows(scratch, row, count, rows, value):
    hidden = value.shape[0]
    for part, (at, lane) in enumerate(lane_parts(scratch, count)):
        scratch[lane, pl.ds(row + at, hidden, stride=rows), :] = value[:, part * 128 : (part + 1) * 128]


def load_rows(scratch, row, count, rows):
    hidden = scratch.shape[1] // rows
    return jnp.concatenate(
        [
            scratch[lane, pl.ds(row + at, hidden, stride=rows), :]
            for at, lane in lane_parts(scratch, count)
        ],
        axis=1,
    )


def gather_out(scratch, out_ref):
    hidden, rows, cols = out_ref.shape
    for lane in range(scratch.shape[0]):
        out_ref[:, :, lane * 128 : (lane + 1) * 128] = (
            scratch[lane].reshape(hidden, rows, 128).astype(BF16)
        )


def spread_in(in_ref, scratch):
    hidden, rows, cols = in_ref.shape
    for lane in range(scratch.shape[0]):
        scratch[lane] = (
            in_ref[:, :, lane * 128 : (lane + 1) * 128].astype(F32).reshape(hidden * rows, 128)
        )


def flat_rows(ref, row, count):
    return jnp.concatenate([ref[pl.ds(row + at, 1), :] for at in range(count)], axis=1)


def whole(array):
    return pl.BlockSpec(array.shape, lambda *_: (0,) * array.ndim)


class Plan:
    def __init__(self, tiles, count, crop):
        self.tiles, self.count, self.crop = tiles, count, crop
        self.half = tiles // 2
        self.subs = 2 if count % 32 == 0 else 1
        self.rows = count // self.subs
        self.width = self.half * self.rows
        self.blocks = crop // self.width
        self.step = max(1, 512 // self.width)
        self.groups = [
            [side * self.half + at for at in range(self.half)] for side in range(2)
        ]
        self.partner = [(at, (at + self.half) % tiles) for at in range(tiles)]

    def view(self, array):
        return array.reshape(self.count, self.tiles, self.subs, self.rows, array.shape[-1])

    def pair_spec(self, chans, index):
        return pl.BlockSpec((self.rows, self.half, 1, self.rows, chans), index)

    def scratch(self, hidden):
        return pltpu.VMEM((self.width // 128, self.rows * hidden, 128), F32)

    def swap(self, array):
        return lax.all_to_all(
            array, "tile", split_axis=0, concat_axis=0, axis_index_groups=self.groups, tiled=True
        )

    def exchange(self, array):
        return lax.ppermute(array, "tile", self.partner)


def factors_kernel(step, x_ref, mask_ref, gain_ref, bias_ref, w_ref, fa_ref, fb_ref, sa_ref, sb_ref):
    rows = x_ref.shape[0]
    hidden = fa_ref.shape[0]

    @pl.loop(0, rows // step)
    def _(turn):
        row = pl.multiple_of(turn * step, step)
        z_hat, _ = stats(turned(x_ref, row, step))
        normed = (z_hat * gain_ref[...] + bias_ref[...]).astype(BF16)
        mask = flat_rows(mask_ref, row, step)
        proj = dot(w_ref[...], normed)
        value_a, gate_a = proj[:hidden], proj[hidden : 2 * hidden]
        value_b, gate_b = proj[2 * hidden : 3 * hidden], proj[3 * hidden :]
        store_rows(sb_ref, row, step, rows, mask * sigmoid(gate_b) * value_b)
        store_rows(sa_ref, row, step, rows, mask * sigmoid(gate_a) * value_a)

    gather_out(sa_ref, fa_ref)
    gather_out(sb_ref, fb_ref)


def make_factors(plan, sub, x, mask, gain, bias, w_t):
    chans = x.shape[-1]
    hidden = w_t.shape[0] // 4
    out = jax.ShapeDtypeStruct((hidden, plan.rows, plan.crop), BF16)
    out_spec = pl.BlockSpec((hidden, plan.rows, plan.width), lambda j: (0, 0, j))
    return pl.pallas_call(
        functools.partial(factors_kernel, plan.step),
        grid=(plan.blocks,),
        in_specs=[
            plan.pair_spec(chans, lambda j: (sub, j % 2, j // 2, 0, 0)),
            pl.BlockSpec((plan.rows, plan.width), lambda j: (sub, j)),
            whole(gain),
            whole(bias),
            whole(w_t),
        ],
        out_specs=[out_spec] * 2,
        out_shape=[out, out],
        scratch_shapes=[plan.scratch(hidden)] * 2,
        compiler_params=params(1),
        cost_estimate=cost(12),
        name="factors",
    )(x, mask, gain, bias, w_t)


def matrix(refs, chan):
    parts = [ref[:, chan].reshape(-1, ref.shape[-1]) for ref in refs]
    return jnp.concatenate(parts, axis=0) if len(parts) > 1 else parts[0]


def by_sub(ref, chan, subs):
    rows = ref.shape[2] // subs
    parts = [
        ref[:, chan, sub * rows : (sub + 1) * rows, :].reshape(-1, ref.shape[3])
        for sub in range(subs)
    ]
    return jnp.concatenate(parts, axis=0) if subs > 1 else parts[0]


def to_subs(ref, chan, value, subs):
    tiles, _, rows, cols = ref.shape
    part = value.shape[0] // subs
    for sub in range(subs):
        ref[:, chan, sub * (rows // subs) : (sub + 1) * (rows // subs), :] = value[
            sub * part : (sub + 1) * part
        ].astype(BF16).reshape(tiles, rows // subs, cols)


def own_spec(array):
    src, _, rows, cols = array.shape
    return pl.BlockSpec((src, CHANS, rows, cols), lambda h: (0, h, 0, 0))


def product_kernel(subs, count, *refs):
    a, b, p_ref = refs[:subs], refs[subs : subs + count], refs[subs + count]
    for chan in range(CHANS):
        to_subs(p_ref, chan, dot(matrix(a, chan), matrix(b, chan), NT), subs)


def make_product(plan, a, b):
    tiles, chans, rows, _ = a[0].shape
    out = jax.ShapeDtypeStruct((tiles, chans, plan.count, len(b) * plan.width), BF16)
    return pl.pallas_call(
        functools.partial(product_kernel, plan.subs, len(b)),
        grid=(chans // CHANS,),
        in_specs=[own_spec(value) for value in (*a, *b)],
        out_specs=own_spec(out),
        out_shape=out,
        compiler_params=params(1),
        cost_estimate=cost(6),
        name="product",
    )(*a, *b)


def grad_b_kernel(subs, g_ref, *refs):
    a, outs = refs[:subs], refs[subs:]
    for chan in range(CHANS):
        grad = dot(by_sub(g_ref, chan, subs), matrix(a, chan), TN).astype(BF16)
        size = grad.shape[0] // len(outs)
        for at, out in enumerate(outs):
            part = grad[at * size : (at + 1) * size]
            out[:, chan] = part.reshape(out.shape[0], *out.shape[2:])


def make_grad_b(plan, g, a):
    outs = g.shape[-1] // plan.width
    return pl.pallas_call(
        functools.partial(grad_b_kernel, plan.subs),
        grid=(g.shape[1] // CHANS,),
        in_specs=[own_spec(value) for value in (g, *a)],
        out_specs=[own_spec(a[0])] * outs,
        out_shape=[jax.ShapeDtypeStruct(a[0].shape, BF16)] * outs,
        compiler_params=params(1),
        cost_estimate=cost(8),
        name="grad_b",
    )(g, *a)


def grad_a_kernel(subs, count, *refs):
    g, b, out = refs[:count], refs[count:-1], refs[-1]
    for chan in range(CHANS):
        rows = jnp.concatenate([by_sub(ref, chan, subs) for ref in g], axis=1)
        to_subs(out, chan, dot(rows, matrix(b, chan)), subs)


def make_grad_a(plan, g, b):
    tiles, chans, _, _ = b[0].shape
    out = jax.ShapeDtypeStruct((tiles, chans, plan.count, plan.crop), BF16)
    return pl.pallas_call(
        functools.partial(grad_a_kernel, plan.subs, len(g)),
        grid=(chans // CHANS,),
        in_specs=[own_spec(value) for value in (*g, *b)],
        out_specs=own_spec(out),
        out_shape=out,
        compiler_params=params(1),
        cost_estimate=cost(10),
        name="grad_a",
    )(*g, *b)


def middle_kernel(
    step, _, x_ref, d_ref, p_ref, gain_ref, bias_ref, wg_ref, og_ref, ob_ref, wo_ref, wot_ref, *refs
):
    g_ref, gb_ref, gwo_ref, gwg_ref, s_ref = refs[-5:]
    rows = x_ref.shape[0]
    width = gb_ref.shape[-1]

    @pl.when((pl.program_id(0) == 0) & (pl.program_id(1) == 0))
    def _():
        gwo_ref[...] = jnp.zeros_like(gwo_ref)
        gwg_ref[...] = jnp.zeros_like(gwg_ref)

    spread_in(p_ref, s_ref)

    @pl.loop(0, rows // step)
    def _(turn):
        row = pl.multiple_of(turn * step, step)
        z_hat, _ = stats(turned(x_ref, row, step))
        normed = (z_hat * gain_ref[...] + bias_ref[...]).astype(BF16)
        gate = sigmoid(dot(wg_ref[...], normed))
        x_hat, inv_std = stats(load_rows(s_ref, row, step, rows))
        x_norm = (x_hat * og_ref[...] + ob_ref[...]).astype(BF16)
        out_lin = dot(wot_ref[...], x_norm)
        lin = turned(d_ref, row, step) * gate
        grad_lin = lin.astype(BF16)
        gate_back = (lin * out_lin * (1.0 - gate)).astype(BF16)
        upstream = dot(wo_ref[...], grad_lin) * og_ref[...]
        store_rows(s_ref, row, step, rows, norm_back(upstream, x_hat, inv_std))
        for at in range(step):
            gb_ref[row + at] = gate_back[:, at * width : (at + 1) * width]
        gwo_ref[...] += dot(x_norm, grad_lin, NT)
        gwg_ref[...] += dot(normed, gate_back, NT)

    gather_out(s_ref, g_ref)


def make_middle(plan, table, before, x, d, p, small):
    chans = x.shape[-1]
    hidden = p.shape[0]
    cut = table.shape[0]
    grads = [jax.ShapeDtypeStruct((hidden, chans), F32), jax.ShapeDtypeStruct((chans, chans), F32)]
    pairs = plan.pair_spec(chans, lambda i, j, at: (i, at[j, 0], at[j, 1], 0, 0))
    channel = pl.BlockSpec((hidden, plan.rows, plan.width), lambda i, j, at: (0, i, j))
    kept = list(before)
    return pl.pallas_call(
        functools.partial(middle_kernel, plan.step),
        grid_spec=pltpu.PrefetchScalarGridSpec(
            num_scalar_prefetch=1,
            grid=(plan.subs, cut),
            in_specs=[pairs, pairs, channel]
            + [whole(value) for value in small]
            + [pl.BlockSpec(memory_space=pl.ANY) for _ in kept],
            out_specs=[
                channel,
                pl.BlockSpec(
                    (plan.rows, chans, plan.width),
                    lambda i, j, at: (i, 0, at[j, 1] * 2 + at[j, 0]),
                ),
            ]
            + [whole(value) for value in grads],
            scratch_shapes=[plan.scratch(hidden)],
        ),
        out_shape=[
            jax.ShapeDtypeStruct(p.shape, BF16),
            jax.ShapeDtypeStruct((plan.count, chans, plan.crop), BF16),
        ]
        + grads,
        input_output_aliases={4 + len(small): 1} if kept else {},
        compiler_params=params(2),
        cost_estimate=cost(10 * cut),
        name="middle",
    )(table, x, d, p, *small, *kept)


def last_kernel(
    step, x_ref, mask_ref, ga_ref, gb_ref, gate_ref, gain_ref, bias_ref, wt_ref, wcat_ref, *refs
):
    out_ref, gw_ref, sa_ref, sb_ref = refs[-4:]
    rows = x_ref.shape[0]
    hidden = ga_ref.shape[0]

    @pl.when(pl.program_id(0) == 0)
    def _():
        gw_ref[...] = jnp.zeros_like(gw_ref)

    spread_in(ga_ref, sa_ref)
    spread_in(gb_ref, sb_ref)

    @pl.loop(0, rows // step)
    def _(turn):
        row = pl.multiple_of(turn * step, step)
        z_hat, inv_in = stats(turned(x_ref, row, step))
        normed = (z_hat * gain_ref[...] + bias_ref[...]).astype(BF16)
        mask = flat_rows(mask_ref, row, step)
        proj = dot(wt_ref[...], normed)
        sides = []
        for side, ref in enumerate((sa_ref, sb_ref)):
            value = proj[2 * side * hidden : (2 * side + 1) * hidden]
            sig = sigmoid(proj[(2 * side + 1) * hidden : (2 * side + 2) * hidden])
            to_value = load_rows(ref, row, step, rows) * mask * sig
            sides += [to_value.astype(BF16), (to_value * value * (1.0 - sig)).astype(BF16)]
        grad_proj = jnp.concatenate(sides, axis=0)
        gate_back = jnp.concatenate([gate_ref[row + at] for at in range(step)], axis=1)
        every = jnp.concatenate([grad_proj, gate_back], axis=0)
        upstream = dot(wcat_ref[...], every) * gain_ref[...]
        grad = norm_back(upstream, z_hat, inv_in).T.astype(BF16)
        out_ref[pl.ds(row, step)] = grad.reshape((step,) + out_ref.shape[1:])
        gw_ref[...] += dot(normed, grad_proj, NT)


def make_last(plan, sub, before, ready, x, mask, grad_a, grad_b, gate_back, small):
    chans = x.shape[-1]
    hidden = grad_a.shape[0]
    grad = jax.ShapeDtypeStruct((chans, 4 * hidden), F32)
    pairs = plan.pair_spec(chans, lambda j: (sub, j % 2, j // 2, 0, 0))
    channel = (hidden, plan.rows, plan.width)
    kept = [ready] if before is None else [before]
    return pl.pallas_call(
        functools.partial(last_kernel, plan.step),
        grid=(plan.blocks,),
        in_specs=[
            pairs,
            pl.BlockSpec((plan.rows, plan.width), lambda j: (sub, j)),
            pl.BlockSpec(channel, lambda j: (0, sub, j)),
            pl.BlockSpec(channel, lambda j: (0, 0, j)),
            pl.BlockSpec((plan.rows, chans, plan.width), lambda j: (sub, 0, j)),
        ]
        + [whole(value) for value in small]
        + [pl.BlockSpec(memory_space=pl.ANY) for _ in kept],
        out_specs=[pairs, whole(grad)],
        out_shape=[jax.ShapeDtypeStruct(x.shape, BF16), grad],
        scratch_shapes=[plan.scratch(hidden)] * 2,
        input_output_aliases={} if before is None else {5 + len(small): 0},
        compiler_params=params(1),
        cost_estimate=cost(20),
        name="last",
    )(x, mask, grad_a, grad_b, gate_back, *small, *kept)


def swap_all(array):
    return lax.all_to_all(array, "tile", split_axis=0, concat_axis=0, tiled=True)


def tile_sum(array, tiles):
    chans, width = array.shape
    parts = swap_all(array.astype(BF16)).reshape(tiles, chans // tiles, width)
    part = jnp.sum(parts.astype(F32), axis=0).astype(BF16)
    spread = jnp.broadcast_to(part[None], (tiles,) + part.shape).reshape(chans, width)
    return swap_all(spread).astype(F32)


def body(
    tiles, x, d, token_mask, ln_in_gain, ln_in_bias, w_ab, w_gate, ln_out_gain, ln_out_bias, w_out
):
    count, crop, chans = x.shape
    hidden = w_out.shape[0]
    plan = Plan(tiles, count, crop)
    me = lax.axis_index("tile")
    side = (me // plan.half).astype(jnp.int32)
    valid = token_mask.astype(F32)
    own_valid = lax.dynamic_slice_in_dim(valid, me * count, count)
    turned_valid = valid.reshape(tiles, plan.subs, plan.rows).transpose(1, 0, 2).reshape(crop)
    mask = own_valid[:, None] * turned_valid[None, :]
    gain, bias = ln_in_gain[:, None], ln_in_bias[:, None]
    w_t = w_ab.T
    w_cat = jnp.concatenate([w_ab, w_gate], axis=1)
    mid = [gain, bias, w_gate.T, ln_out_gain[:, None], ln_out_bias[:, None], w_out, w_out.T]
    x, d = plan.view(x), plan.view(d)
    owned = lambda array: array.reshape(plan.half, hidden // plan.half, *array.shape[1:])
    joined = lambda array: array.reshape(hidden, *array.shape[2:])
    every = range(plan.subs)

    own_a, own_b, other_b = [], [], []
    for sub in every:
        factor_a, factor_b = make_factors(plan, sub, x, mask, gain, bias, w_t)
        own_b.append(owned(plan.swap(factor_b)))
        other_b.append(owned(plan.swap(plan.exchange(factor_b))))
        own_a.append(owned(plan.swap(factor_a)))

    before, local_mid, owner_g, grad_own, grad_other = (), [], [], [], []
    turns = [([sub], [(1 - side, sub)], [other_b[sub]]) for sub in every]
    turns += [(list(every), [(side, sub) for sub in every], own_b)]
    for which, (subs, at, b) in enumerate(turns):
        table = jnp.stack([jnp.stack([half, jnp.int32(sub)]) for half, sub in at])
        product = plan.swap(joined(make_product(plan, own_a, b)))
        grad_prod, gate_back, *local = make_middle(plan, table, before, x, d, product, mid)
        local_mid.append(jnp.concatenate(local[::-1], axis=1))
        owner_g.append(owned(plan.swap(grad_prod)))
        grads = make_grad_b(plan, owner_g[which], own_a)
        before = (gate_back, grads[0])
        if which < plan.subs:
            grad_other.append(plan.exchange(grads[0]))
        else:
            grad_own = grads
    sum_mid = tile_sum(sum(local_mid), tiles) / crop
    grad_a = plan.swap(joined(make_grad_a(plan, owner_g, other_b + own_b)))
    pair_grad, local_ab = None, []
    for sub in every:
        whole_b = (grad_own[sub].astype(F32) + grad_other[sub].astype(F32)).astype(BF16)
        grad_b = plan.swap(joined(whole_b))
        pair_grad, local = make_last(
            plan, sub, pair_grad, sum_mid, x, mask, grad_a, grad_b, gate_back, [gain, bias, w_t, w_cat]
        )
        local_ab.append(local)
    sum_ab = tile_sum(sum(local_ab), tiles) / crop
    return (pair_grad.reshape(count, crop, chans), sum_ab, sum_mid[:, :chans], sum_mid[:, chans:])


def solution(mesh):
    pairs = P(("crops", "tile"), None, None)
    return jax.shard_map(
        functools.partial(body, mesh.shape["tile"]),
        mesh=mesh,
        in_specs=(pairs, pairs, P("crops")) + (P(),) * 7,
        out_specs=(pairs,) + (P("crops", None),) * 3,
        check_vma=False,
    )
```

```python
import functools

import jax
import jax.numpy as jnp
from jax import lax
from jax.experimental import pallas as pl
from jax.experimental.pallas import tpu as pltpu
from jax.sharding import PartitionSpec as P

HELD = pl.BlockSpec(memory_space=pl.ANY)
EPS = 1e-05
CHANS = 4
F32 = jnp.float32
BF16 = jnp.bfloat16
NN = (((1,), (0,)), ((), ()))
NT = (((1,), (1,)), ((), ()))
TN = (((0,), (0,)), ((), ()))


def params(steps):
    return pltpu.CompilerParams(
        dimension_semantics=("arbitrary",) * steps, vmem_limit_bytes=50 * 1024 * 1024
    )


def cost(micros):
    return pl.CostEstimate(
        flops=int(micros * 1.0e9), bytes_accessed=int(micros * 3.0e6), transcendentals=0
    )


def dot(left, right, form=NN):
    return lax.dot_general(left, right, form, preferred_element_type=F32)


def sigmoid(value):
    return 0.5 * jnp.tanh(0.5 * value) + 0.5


def col_mean(value):
    return jnp.mean(value, axis=0, keepdims=True)


def stats(value):
    centered = value - col_mean(value)
    inv_std = lax.rsqrt(col_mean(centered * centered) + EPS)
    return centered * inv_std, inv_std


def norm_back(upstream, scaled, inv_std):
    return inv_std * (upstream - col_mean(upstream) - scaled * col_mean(upstream * scaled))


def turned(ref, row, count):
    block = ref[pl.ds(row, count)]
    return block.reshape(-1, block.shape[-1]).astype(F32).T


def lane_parts(scratch, count):
    return [(at, lane) for at in range(count) for lane in range(scratch.shape[0])]


def store_rows(scratch, row, count, rows, value):
    hidden = value.shape[0]
    for part, (at, lane) in enumerate(lane_parts(scratch, count)):
        scratch[lane, pl.ds(row + at, hidden, stride=rows), :] = value[:, part * 128 : (part + 1) * 128]


def load_rows(scratch, row, count, rows):
    hidden = scratch.shape[1] // rows
    return jnp.concatenate(
        [
            scratch[lane, pl.ds(row + at, hidden, stride=rows), :]
            for at, lane in lane_parts(scratch, count)
        ],
        axis=1,
    )


def gather_out(scratch, out_ref):
    hidden, rows, cols = out_ref.shape
    for lane in range(scratch.shape[0]):
        out_ref[:, :, lane * 128 : (lane + 1) * 128] = (
            scratch[lane].reshape(hidden, rows, 128).astype(BF16)
        )


def spread_in(in_ref, scratch):
    hidden, rows, cols = in_ref.shape
    for lane in range(scratch.shape[0]):
        scratch[lane] = (
            in_ref[:, :, lane * 128 : (lane + 1) * 128].astype(F32).reshape(hidden * rows, 128)
        )


def flat_rows(ref, row, count):
    return jnp.concatenate([ref[pl.ds(row + at, 1), :] for at in range(count)], axis=1)


def whole(array):
    return pl.BlockSpec(array.shape, lambda *_: (0,) * array.ndim)


class Plan:
    def __init__(self, tiles, count, crop):
        self.tiles, self.count, self.crop = tiles, count, crop
        self.half = tiles // 2
        self.subs = 2 if count % 32 == 0 else 1
        self.rows = count // self.subs
        self.width = self.half * self.rows
        self.blocks = crop // self.width
        self.step = max(1, 512 // self.width)
        self.groups = [
            [side * self.half + at for at in range(self.half)] for side in range(2)
        ]
        self.partner = [(at, (at + self.half) % tiles) for at in range(tiles)]

    def view(self, array):
        return array.reshape(self.count, self.tiles, self.subs, self.rows, array.shape[-1])

    def pair_spec(self, chans, index):
        return pl.BlockSpec((self.rows, self.half, 1, self.rows, chans), index)

    def scratch(self, hidden):
        return pltpu.VMEM((self.width // 128, self.rows * hidden, 128), F32)

    def swap(self, array):
        return lax.all_to_all(
            array, "tile", split_axis=0, concat_axis=0, axis_index_groups=self.groups, tiled=True
        )

    def cut(self, *eighths):
        return [max(1, self.half * share // 8) for share in eighths]

    def pieces(self, array, counts):
        ends = [sum(counts[: at + 1]) for at in range(len(counts))]
        return [array[end - size : end] for size, end in zip(counts, ends)]

    def exchange(self, array):
        return lax.ppermute(array, "tile", self.partner)


def after_kernel(*refs):
    del refs


def after(value, *others):
    return pl.pallas_call(
        after_kernel,
        in_specs=[HELD] * (1 + len(others)),
        out_specs=HELD,
        out_shape=jax.ShapeDtypeStruct(value.shape, value.dtype),
        input_output_aliases={0: 0},
        compiler_params=params(0),
        cost_estimate=cost(0.1),
        name="after",
    )(value, *others)


def factors_kernel(step, x_ref, mask_ref, gain_ref, bias_ref, w_ref, *refs):
    fa_ref, fb_ref, sa_ref, sb_ref = refs[-4:]
    rows = x_ref.shape[0]
    hidden = fa_ref.shape[0]

    @pl.loop(0, rows // step)
    def _(turn):
        row = pl.multiple_of(turn * step, step)
        z_hat, _ = stats(turned(x_ref, row, step))
        normed = (z_hat * gain_ref[...] + bias_ref[...]).astype(BF16)
        mask = flat_rows(mask_ref, row, step)
        proj = dot(w_ref[...], normed)
        value_a, gate_a = proj[:hidden], proj[hidden : 2 * hidden]
        value_b, gate_b = proj[2 * hidden : 3 * hidden], proj[3 * hidden :]
        store_rows(sb_ref, row, step, rows, mask * sigmoid(gate_b) * value_b)
        store_rows(sa_ref, row, step, rows, mask * sigmoid(gate_a) * value_a)

    gather_out(sa_ref, fa_ref)
    gather_out(sb_ref, fb_ref)


def make_factors(plan, sub, before, x, mask, gain, bias, w_t):
    chans = x.shape[-1]
    hidden = w_t.shape[0] // 4
    block = (hidden, plan.rows, plan.width)
    return pl.pallas_call(
        functools.partial(factors_kernel, plan.step),
        grid=(plan.blocks,),
        in_specs=[
            plan.pair_spec(chans, lambda j: (sub, j % 2, j // 2, 0, 0)),
            pl.BlockSpec((plan.rows, plan.width), lambda j: (sub, j)),
            whole(gain),
            whole(bias),
            whole(w_t),
        ]
        + [HELD for _ in before],
        out_specs=[
            pl.BlockSpec(block, lambda j: (0, sub, j)),
            pl.BlockSpec(block, lambda j: (0, 0, j)),
        ],
        out_shape=[
            jax.ShapeDtypeStruct((hidden, plan.count, plan.crop), BF16),
            jax.ShapeDtypeStruct((hidden, plan.rows, plan.crop), BF16),
        ],
        input_output_aliases={5: 0} if before else {},
        scratch_shapes=[plan.scratch(hidden)] * 2,
        compiler_params=params(1),
        cost_estimate=cost(0.2),
        name="factors",
    )(x, mask, gain, bias, w_t, *before)


def matrix(refs, chan):
    parts = [ref[:, chan].reshape(-1, ref.shape[-1]) for ref in refs]
    return jnp.concatenate(parts, axis=0) if len(parts) > 1 else parts[0]


def by_sub(ref, chan, subs):
    rows = ref.shape[2] // subs
    parts = [
        ref[:, chan, sub * rows : (sub + 1) * rows, :].reshape(-1, ref.shape[3])
        for sub in range(subs)
    ]
    return jnp.concatenate(parts, axis=0) if subs > 1 else parts[0]


def to_subs(ref, chan, value, subs):
    tiles, _, rows, cols = ref.shape
    part = value.shape[0] // subs
    for sub in range(subs):
        ref[:, chan, sub * (rows // subs) : (sub + 1) * (rows // subs), :] = value[
            sub * part : (sub + 1) * part
        ].astype(BF16).reshape(tiles, rows // subs, cols)


def own_spec(array):
    src, _, rows, cols = array.shape
    return pl.BlockSpec((src, CHANS, rows, cols), lambda h: (0, h, 0, 0))


def product_kernel(subs, a_ref, *refs):
    b, p_ref = refs[:-1], refs[-1]
    for chan in range(CHANS):
        to_subs(p_ref, chan, dot(by_sub(a_ref, chan, subs), matrix(b, chan), NT), subs)


def make_product(plan, a, b):
    tiles, chans, _, _ = a.shape
    cols = sum(value.shape[0] for value in b) * plan.rows
    out = jax.ShapeDtypeStruct((tiles, chans, plan.count, cols), BF16)
    return pl.pallas_call(
        functools.partial(product_kernel, plan.subs),
        grid=(chans // CHANS,),
        in_specs=[own_spec(value) for value in (a, *b)],
        out_specs=own_spec(out),
        out_shape=out,
        compiler_params=params(1),
        cost_estimate=cost(0.2),
        name="product",
    )(a, *b)


def grad_b_kernel(subs, g_ref, a_ref, *outs):
    for chan in range(CHANS):
        grad = dot(by_sub(g_ref, chan, subs), by_sub(a_ref, chan, subs), TN).astype(BF16)
        at = 0
        for out in outs:
            size = out.shape[0] * out.shape[2]
            out[:, chan] = grad[at : at + size].reshape(out.shape[0], *out.shape[2:])
            at += size


def make_grad_b(plan, g, a, tiles):
    outs = [
        jax.ShapeDtypeStruct((count, a.shape[1], plan.rows, plan.crop), BF16) for count in tiles
    ]
    return pl.pallas_call(
        functools.partial(grad_b_kernel, plan.subs),
        grid=(g.shape[1] // CHANS,),
        in_specs=[own_spec(value) for value in (g, a)],
        out_specs=[own_spec(value) for value in outs],
        out_shape=outs,
        compiler_params=params(1),
        cost_estimate=cost(0.2),
        name="grad_b",
    )(g, a)


def grad_a_kernel(subs, count, *refs):
    g, b, out = refs[:count], refs[count:-1], refs[-1]
    for chan in range(CHANS):
        rows = jnp.concatenate([by_sub(ref, chan, subs) for ref in g], axis=1)
        to_subs(out, chan, dot(rows, matrix(b, chan)), subs)


def make_grad_a(plan, g, b):
    chans = b[0].shape[1]
    out = jax.ShapeDtypeStruct((plan.half, chans, plan.count, plan.crop), BF16)
    return pl.pallas_call(
        functools.partial(grad_a_kernel, plan.subs, len(g)),
        grid=(chans // CHANS,),
        in_specs=[own_spec(value) for value in (*g, *b)],
        out_specs=own_spec(out),
        out_shape=out,
        compiler_params=params(1),
        cost_estimate=cost(0.2),
        name="grad_a",
    )(*g, *b)


def middle_kernel(
    step, _, x_ref, d_ref, p_ref, gain_ref, bias_ref, wg_ref, og_ref, ob_ref, wo_ref, wot_ref, *refs
):
    g_ref, gb_ref, gwo_ref, gwg_ref, s_ref = refs[-5:]
    rows = x_ref.shape[0]
    width = gb_ref.shape[-1]

    @pl.when((pl.program_id(0) == 0) & (pl.program_id(1) == 0))
    def _():
        gwo_ref[...] = jnp.zeros_like(gwo_ref)
        gwg_ref[...] = jnp.zeros_like(gwg_ref)

    spread_in(p_ref, s_ref)

    @pl.loop(0, rows // step)
    def _(turn):
        row = pl.multiple_of(turn * step, step)
        z_hat, _ = stats(turned(x_ref, row, step))
        normed = (z_hat * gain_ref[...] + bias_ref[...]).astype(BF16)
        gate = sigmoid(dot(wg_ref[...], normed))
        x_hat, inv_std = stats(load_rows(s_ref, row, step, rows))
        x_norm = (x_hat * og_ref[...] + ob_ref[...]).astype(BF16)
        out_lin = dot(wot_ref[...], x_norm)
        lin = turned(d_ref, row, step) * gate
        grad_lin = lin.astype(BF16)
        gate_back = (lin * out_lin * (1.0 - gate)).astype(BF16)
        upstream = dot(wo_ref[...], grad_lin) * og_ref[...]
        store_rows(s_ref, row, step, rows, norm_back(upstream, x_hat, inv_std))
        for at in range(step):
            gb_ref[row + at] = gate_back[:, at * width : (at + 1) * width]
        gwo_ref[...] += dot(x_norm, grad_lin, NT)
        gwg_ref[...] += dot(normed, gate_back, NT)

    gather_out(s_ref, g_ref)


def make_middle(plan, table, before, x, d, p, small):
    chans = x.shape[-1]
    hidden = p.shape[0]
    cut = table.shape[0]
    grads = [jax.ShapeDtypeStruct((hidden, chans), F32), jax.ShapeDtypeStruct((chans, chans), F32)]
    pairs = plan.pair_spec(chans, lambda i, j, at: (i, at[j, 0], at[j, 1], 0, 0))
    channel = pl.BlockSpec((hidden, plan.rows, plan.width), lambda i, j, at: (0, i, j))
    kept = list(before)
    return pl.pallas_call(
        functools.partial(middle_kernel, plan.step),
        grid_spec=pltpu.PrefetchScalarGridSpec(
            num_scalar_prefetch=1,
            grid=(plan.subs, cut),
            in_specs=[pairs, pairs, channel]
            + [whole(value) for value in small]
            + [HELD for _ in kept],
            out_specs=[
                channel,
                pl.BlockSpec(
                    (plan.rows, chans, plan.width),
                    lambda i, j, at: (i, 0, at[j, 1] * 2 + at[j, 0]),
                ),
            ]
            + [whole(value) for value in grads],
            scratch_shapes=[plan.scratch(hidden)],
        ),
        out_shape=[
            jax.ShapeDtypeStruct(p.shape, BF16),
            jax.ShapeDtypeStruct((plan.count, chans, plan.crop), BF16),
        ]
        + grads,
        input_output_aliases={4 + len(small): 1} if kept else {},
        compiler_params=params(2),
        cost_estimate=cost(0.2),
        name="middle",
    )(table, x, d, p, *small, *kept)


def last_kernel(
    step, x_ref, mask_ref, ga_ref, gb_ref, gate_ref, gain_ref, bias_ref, wt_ref, wcat_ref, *refs
):
    out_ref, gw_ref, sa_ref, sb_ref = refs[-4:]
    rows = x_ref.shape[0]
    hidden = ga_ref.shape[0]

    @pl.when(pl.program_id(0) == 0)
    def _():
        gw_ref[...] = jnp.zeros_like(gw_ref)

    spread_in(ga_ref, sa_ref)
    spread_in(gb_ref, sb_ref)

    @pl.loop(0, rows // step)
    def _(turn):
        row = pl.multiple_of(turn * step, step)
        z_hat, inv_in = stats(turned(x_ref, row, step))
        normed = (z_hat * gain_ref[...] + bias_ref[...]).astype(BF16)
        mask = flat_rows(mask_ref, row, step)
        proj = dot(wt_ref[...], normed)
        sides = []
        for side, ref in enumerate((sa_ref, sb_ref)):
            value = proj[2 * side * hidden : (2 * side + 1) * hidden]
            sig = sigmoid(proj[(2 * side + 1) * hidden : (2 * side + 2) * hidden])
            to_value = load_rows(ref, row, step, rows) * mask * sig
            sides += [to_value.astype(BF16), (to_value * value * (1.0 - sig)).astype(BF16)]
        grad_proj = jnp.concatenate(sides, axis=0)
        gate_back = jnp.concatenate([gate_ref[row + at] for at in range(step)], axis=1)
        every = jnp.concatenate([grad_proj, gate_back], axis=0)
        upstream = dot(wcat_ref[...], every) * gain_ref[...]
        grad = norm_back(upstream, z_hat, inv_in).T.astype(BF16)
        out_ref[pl.ds(row, step)] = grad.reshape((step,) + out_ref.shape[1:])
        gw_ref[...] += dot(normed, grad_proj, NT)


def make_last(plan, sub, before, ready, x, mask, grad_a, grad_b, gate_back, small):
    chans = x.shape[-1]
    hidden = grad_a.shape[0]
    grad = jax.ShapeDtypeStruct((chans, 4 * hidden), F32)
    pairs = plan.pair_spec(chans, lambda j: (sub, j % 2, j // 2, 0, 0))
    channel = (hidden, plan.rows, plan.width)
    kept = list(ready) if before is None else [before]
    return pl.pallas_call(
        functools.partial(last_kernel, plan.step),
        grid=(plan.blocks,),
        in_specs=[
            pairs,
            pl.BlockSpec((plan.rows, plan.width), lambda j: (sub, j)),
            pl.BlockSpec(channel, lambda j: (0, sub, j)),
            pl.BlockSpec(channel, lambda j: (0, 0, j)),
            pl.BlockSpec((plan.rows, chans, plan.width), lambda j: (sub, 0, j)),
        ]
        + [whole(value) for value in small]
        + [HELD for _ in kept],
        out_specs=[pairs, whole(grad)],
        out_shape=[jax.ShapeDtypeStruct(x.shape, BF16), grad],
        scratch_shapes=[plan.scratch(hidden)] * 2,
        input_output_aliases={} if before is None else {5 + len(small): 0},
        compiler_params=params(1),
        cost_estimate=cost(0.2),
        name="last",
    )(x, mask, grad_a, grad_b, gate_back, *small, *kept)


def swap_all(array):
    return lax.all_to_all(array, "tile", split_axis=0, concat_axis=0, tiled=True)


def tile_sum(array, tiles):
    chans, width = array.shape
    parts = swap_all(array.astype(BF16)).reshape(tiles, chans // tiles, width)
    part = jnp.sum(parts.astype(F32), axis=0).astype(BF16)
    spread = jnp.broadcast_to(part[None], (tiles,) + part.shape).reshape(chans, width)
    return swap_all(spread).astype(F32)


def body(
    tiles, x, d, token_mask, ln_in_gain, ln_in_bias, w_ab, w_gate, ln_out_gain, ln_out_bias, w_out
):
    count, crop, chans = x.shape
    hidden = w_out.shape[0]
    plan = Plan(tiles, count, crop)
    me = lax.axis_index("tile")
    side = (me // plan.half).astype(jnp.int32)
    valid = token_mask.astype(F32)
    own_valid = lax.dynamic_slice_in_dim(valid, me * count, count)
    turned_valid = valid.reshape(tiles, plan.subs, plan.rows).transpose(1, 0, 2).reshape(crop)
    mask = own_valid[:, None] * turned_valid[None, :]
    gain, bias = ln_in_gain[:, None], ln_in_bias[:, None]
    w_t = w_ab.T
    w_cat = jnp.concatenate([w_ab, w_gate], axis=1)
    mid = [gain, bias, w_gate.T, ln_out_gain[:, None], ln_out_bias[:, None], w_out, w_out.T]
    x, d = plan.view(x), plan.view(d)
    owned = lambda array: array.reshape(plan.half, hidden // plan.half, *array.shape[1:])
    joined = lambda array: array.reshape(hidden, *array.shape[2:])
    every = range(plan.subs)

    plan_cut = plan.cut
    two = plan.subs == 2
    cut_a, cut_b = plan_cut(5, 3), plan_cut(2, 2, 2, 2)
    back_a, back_b = plan_cut(2, 1, 2, 3), plan_cut(2, 3, 3)

    def middle(at, before, product):
        table = jnp.stack([jnp.stack([half, jnp.int32(sub)]) for half, sub in at])
        g, kept, *local = make_middle(plan, table, before, x, d, product, mid)
        return g, kept, jnp.concatenate(local[::-1], axis=1)

    def product_of(b):
        return joined(make_product(plan, own_a, b))

    factor_a, factor_b0 = make_factors(plan, 0, (), x, mask, gain, bias, w_t)
    own_b = [owned(plan.swap(factor_b0))]
    if two:
        factor_a, factor_b1 = make_factors(plan, 1, (factor_a,), x, mask, gain, bias, w_t)
    sent = plan.pieces(own_b[0], cut_a)
    got_a = [plan.exchange(sent[0])]
    own_a = owned(plan.swap(after(factor_a, own_b[0])))
    got_a.append(plan.exchange(sent[1]))
    if two:
        own_b.append(owned(plan.swap(after(factor_b1, own_a, got_a[0]))))
        sent = plan.pieces(own_b[1], cut_b)
        got_b = [plan.exchange(piece) for piece in sent]
    else:
        got_b = [own_a] * 4
    product = plan.swap(after(product_of(got_a), own_b[-1]))
    grad, kept, local_0 = middle([(1 - side, 0)], (), product)
    product_own = plan.swap(after(product_of(own_b), product, got_b[0]))
    owner_g = [owned(plan.swap(after(grad, product_own, got_b[1])))]
    grad_own, kept, local_own = middle([(side, sub) for sub in every], (kept, grad), product_own)
    grad_b0 = make_grad_b(plan, owner_g[0], own_a, back_a)
    owner_own = owned(plan.swap(after(grad_own, owner_g[0], got_b[2], grad_b0[0])))
    grad_b_own = make_grad_b(plan, owner_own, own_a, [plan.half] * plan.subs)
    back_0 = [plan.exchange(piece) for piece in grad_b0]
    local_mid = local_0 + local_own
    back_1, b_other = [], [got_a]
    if two:
        product = plan.swap(after(product_of(got_b), owner_own, grad_b_own[0]))
        grad, kept, local_1 = middle([(1 - side, 1)], (kept, back_0[0]), product)
        local_mid += local_1
        owner_g.append(owned(plan.swap(after(grad, back_0[1]))))
        grad_b1 = make_grad_b(plan, owner_g[1], own_a, back_b)
        back_1 = [plan.exchange(piece) for piece in grad_b1]
        b_other.append(got_b)
    grad_a = joined(
        make_grad_a(plan, owner_g + [owner_own], [v for got in b_other for v in got] + own_b)
    )
    grad_a = plan.swap(after(grad_a, back_0[2], *(grad_b1[:1] if two else [])))

    def summed(own, back):
        return joined(
            (own.astype(F32) + jnp.concatenate(back, axis=0).astype(F32)).astype(BF16)
        )

    waits = (grad_a, *back_1[:1])
    grad_b = plan.swap(after(summed(grad_b_own[0], back_0), *waits))
    sum_mid = tile_sum(after(local_mid, grad_b, *back_1[1:2]), tiles) / crop
    small = [gain, bias, w_t, w_cat]
    pair_grad, local_ab = make_last(
        plan, 0, None, (grad_b,), x, mask, grad_a, grad_b, kept, small
    )
    if two:
        grad_b = plan.swap(after(summed(grad_b_own[1], back_1), sum_mid))
        pair_grad, local = make_last(plan, 1, pair_grad, (), x, mask, grad_a, grad_b, kept, small)
        local_ab += local
    sum_ab = tile_sum(local_ab, tiles) / crop
    return (pair_grad.reshape(count, crop, chans), sum_ab, sum_mid[:, :chans], sum_mid[:, chans:])


def solution(mesh):
    pairs = P(("crops", "tile"), None, None)
    return jax.shard_map(
        functools.partial(body, mesh.shape["tile"]),
        mesh=mesh,
        in_specs=(pairs, pairs, P("crops")) + (P(),) * 7,
        out_specs=(pairs,) + (P("crops", None),) * 3,
        check_vma=False,
    )
```

```python
import functools

import jax
import jax.numpy as jnp
from jax import lax
from jax.experimental import pallas as pl
from jax.experimental.pallas import tpu as pltpu
from jax.sharding import PartitionSpec as P

HELD = pl.BlockSpec(memory_space=pl.ANY)
EPS = 1e-05
CHANS = 4
F32 = jnp.float32
BF16 = jnp.bfloat16
NN = (((1,), (0,)), ((), ()))
NT = (((1,), (1,)), ((), ()))
TN = (((0,), (0,)), ((), ()))


def params(steps):
    return pltpu.CompilerParams(
        dimension_semantics=("arbitrary",) * steps, vmem_limit_bytes=50 * 1024 * 1024
    )


def cost(micros):
    return pl.CostEstimate(
        flops=int(micros * 1.0e9), bytes_accessed=int(micros * 3.0e6), transcendentals=0
    )


def dot(left, right, form=NN):
    return lax.dot_general(left, right, form, preferred_element_type=F32)


def sigmoid(value):
    return 0.5 * jnp.tanh(0.5 * value) + 0.5


def col_mean(value):
    return jnp.mean(value, axis=0, keepdims=True)


def stats(value):
    centered = value - col_mean(value)
    inv_std = lax.rsqrt(col_mean(centered * centered) + EPS)
    return centered * inv_std, inv_std


def norm_back(upstream, scaled, inv_std):
    return inv_std * (upstream - col_mean(upstream) - scaled * col_mean(upstream * scaled))


def turned(ref, row, count):
    block = ref[pl.ds(row, count)]
    return block.reshape(-1, block.shape[-1]).astype(F32).T


def lane_parts(scratch, count):
    return [(at, lane) for at in range(count) for lane in range(scratch.shape[0])]


def store_rows(scratch, row, count, rows, value):
    hidden = value.shape[0]
    for part, (at, lane) in enumerate(lane_parts(scratch, count)):
        scratch[lane, pl.ds(row + at, hidden, stride=rows), :] = value[:, part * 128 : (part + 1) * 128]


def load_rows(scratch, row, count, rows):
    hidden = scratch.shape[1] // rows
    return jnp.concatenate(
        [
            scratch[lane, pl.ds(row + at, hidden, stride=rows), :]
            for at, lane in lane_parts(scratch, count)
        ],
        axis=1,
    )


def gather_out(scratch, out_ref):
    hidden, rows, cols = out_ref.shape
    for lane in range(scratch.shape[0]):
        out_ref[:, :, lane * 128 : (lane + 1) * 128] = (
            scratch[lane].reshape(hidden, rows, 128).astype(BF16)
        )


def spread_in(in_ref, scratch):
    hidden, rows, cols = in_ref.shape
    for lane in range(scratch.shape[0]):
        scratch[lane] = (
            in_ref[:, :, lane * 128 : (lane + 1) * 128].astype(F32).reshape(hidden * rows, 128)
        )


def flat_rows(ref, row, count):
    return jnp.concatenate([ref[pl.ds(row + at, 1), :] for at in range(count)], axis=1)


def whole(array):
    return pl.BlockSpec(array.shape, lambda *_: (0,) * array.ndim)


class Plan:
    def __init__(self, tiles, count, crop):
        self.tiles, self.count, self.crop = tiles, count, crop
        self.half = tiles // 2
        self.subs = 2 if count % 32 == 0 else 1
        self.rows = count // self.subs
        self.width = self.half * self.rows
        self.blocks = crop // self.width
        self.step = max(1, 512 // self.width)
        self.groups = [
            [side * self.half + at for at in range(self.half)] for side in range(2)
        ]
        self.partner = [(at, (at + self.half) % tiles) for at in range(tiles)]

    def view(self, array):
        return array.reshape(self.count, self.tiles, self.subs, self.rows, array.shape[-1])

    def pair_spec(self, chans, index):
        return pl.BlockSpec((self.rows, self.half, 1, self.rows, chans), index)

    def scratch(self, hidden):
        return pltpu.VMEM((self.width // 128, self.rows * hidden, 128), F32)

    def swap(self, array):
        return lax.all_to_all(
            array, "tile", split_axis=0, concat_axis=0, axis_index_groups=self.groups, tiled=True
        )

    def cut(self, *eighths):
        return [max(1, self.half * share // 8) for share in eighths]

    def pieces(self, array, counts):
        ends = [sum(counts[: at + 1]) for at in range(len(counts))]
        return [array[end - size : end] for size, end in zip(counts, ends)]

    def exchange(self, array):
        return lax.ppermute(array, "tile", self.partner)


def after_kernel(*refs):
    del refs


def after(value, *others):
    return pl.pallas_call(
        after_kernel,
        in_specs=[HELD] * (1 + len(others)),
        out_specs=HELD,
        out_shape=jax.ShapeDtypeStruct(value.shape, value.dtype),
        input_output_aliases={0: 0},
        compiler_params=params(0),
        cost_estimate=cost(0.1),
        name="after",
    )(value, *others)


def factors_kernel(step, x_ref, mask_ref, gain_ref, bias_ref, w_ref, *refs):
    fa_ref, fb_ref, sa_ref, sb_ref = refs[-4:]
    rows = x_ref.shape[0]
    hidden = fa_ref.shape[0]

    @pl.loop(0, rows // step, unroll=min(2, rows // step))
    def _(turn):
        row = pl.multiple_of(turn * step, step)
        z_hat, _ = stats(turned(x_ref, row, step))
        normed = (z_hat * gain_ref[...] + bias_ref[...]).astype(BF16)
        mask = flat_rows(mask_ref, row, step)
        proj = dot(w_ref[...], normed)
        value_a, gate_a = proj[:hidden], proj[hidden : 2 * hidden]
        value_b, gate_b = proj[2 * hidden : 3 * hidden], proj[3 * hidden :]
        store_rows(sb_ref, row, step, rows, mask * sigmoid(gate_b) * value_b)
        store_rows(sa_ref, row, step, rows, mask * sigmoid(gate_a) * value_a)

    gather_out(sa_ref, fa_ref)
    gather_out(sb_ref, fb_ref)


def make_factors(plan, sub, before, x, mask, gain, bias, w_t):
    chans = x.shape[-1]
    hidden = w_t.shape[0] // 4
    block = (hidden, plan.rows, plan.width)
    return pl.pallas_call(
        functools.partial(factors_kernel, plan.step),
        grid=(plan.blocks,),
        in_specs=[
            plan.pair_spec(chans, lambda j: (sub, j % 2, j // 2, 0, 0)),
            pl.BlockSpec((plan.rows, plan.width), lambda j: (sub, j)),
            whole(gain),
            whole(bias),
            whole(w_t),
        ]
        + [HELD for _ in before],
        out_specs=[
            pl.BlockSpec(block, lambda j: (0, sub, j)),
            pl.BlockSpec(block, lambda j: (0, 0, j)),
        ],
        out_shape=[
            jax.ShapeDtypeStruct((hidden, plan.count, plan.crop), BF16),
            jax.ShapeDtypeStruct((hidden, plan.rows, plan.crop), BF16),
        ],
        input_output_aliases={5: 0} if before else {},
        scratch_shapes=[plan.scratch(hidden)] * 2,
        compiler_params=params(1),
        cost_estimate=cost(0.2),
        name="factors",
    )(x, mask, gain, bias, w_t, *before)


def matrix(refs, chan):
    parts = [ref[:, chan].reshape(-1, ref.shape[-1]) for ref in refs]
    return jnp.concatenate(parts, axis=0) if len(parts) > 1 else parts[0]


def by_sub(ref, chan, subs):
    rows = ref.shape[2] // subs
    parts = [
        ref[:, chan, sub * rows : (sub + 1) * rows, :].reshape(-1, ref.shape[3])
        for sub in range(subs)
    ]
    return jnp.concatenate(parts, axis=0) if subs > 1 else parts[0]


def to_subs(ref, chan, value, subs):
    tiles, _, rows, cols = ref.shape
    part = value.shape[0] // subs
    for sub in range(subs):
        ref[:, chan, sub * (rows // subs) : (sub + 1) * (rows // subs), :] = value[
            sub * part : (sub + 1) * part
        ].astype(BF16).reshape(tiles, rows // subs, cols)


def own_spec(array):
    src, _, rows, cols = array.shape
    return pl.BlockSpec((src, CHANS, rows, cols), lambda h: (0, h, 0, 0))


def product_kernel(subs, a_ref, *refs):
    b, p_ref = refs[:-1], refs[-1]
    for chan in range(CHANS):
        to_subs(p_ref, chan, dot(by_sub(a_ref, chan, subs), matrix(b, chan), NT), subs)


def make_product(plan, a, b):
    tiles, chans, _, _ = a.shape
    cols = sum(value.shape[0] for value in b) * plan.rows
    out = jax.ShapeDtypeStruct((tiles, chans, plan.count, cols), BF16)
    return pl.pallas_call(
        functools.partial(product_kernel, plan.subs),
        grid=(chans // CHANS,),
        in_specs=[own_spec(value) for value in (a, *b)],
        out_specs=own_spec(out),
        out_shape=out,
        compiler_params=params(1),
        cost_estimate=cost(0.2),
        name="product",
    )(a, *b)


def grad_b_kernel(subs, g_ref, a_ref, *outs):
    for chan in range(CHANS):
        grad = dot(by_sub(g_ref, chan, subs), by_sub(a_ref, chan, subs), TN).astype(BF16)
        at = 0
        for out in outs:
            size = out.shape[0] * out.shape[2]
            out[:, chan] = grad[at : at + size].reshape(out.shape[0], *out.shape[2:])
            at += size


def make_grad_b(plan, g, a, tiles):
    outs = [
        jax.ShapeDtypeStruct((count, a.shape[1], plan.rows, plan.crop), BF16) for count in tiles
    ]
    return pl.pallas_call(
        functools.partial(grad_b_kernel, plan.subs),
        grid=(g.shape[1] // CHANS,),
        in_specs=[own_spec(value) for value in (g, a)],
        out_specs=[own_spec(value) for value in outs],
        out_shape=outs,
        compiler_params=params(1),
        cost_estimate=cost(0.2),
        name="grad_b",
    )(g, a)


def grad_a_kernel(subs, count, *refs):
    g, b, out = refs[:count], refs[count:-1], refs[-1]
    for chan in range(CHANS):
        rows = jnp.concatenate([by_sub(ref, chan, subs) for ref in g], axis=1)
        to_subs(out, chan, dot(rows, matrix(b, chan)), subs)


def make_grad_a(plan, g, b):
    chans = b[0].shape[1]
    out = jax.ShapeDtypeStruct((plan.half, chans, plan.count, plan.crop), BF16)
    return pl.pallas_call(
        functools.partial(grad_a_kernel, plan.subs, len(g)),
        grid=(chans // CHANS,),
        in_specs=[own_spec(value) for value in (*g, *b)],
        out_specs=own_spec(out),
        out_shape=out,
        compiler_params=params(1),
        cost_estimate=cost(0.2),
        name="grad_a",
    )(*g, *b)


def middle_kernel(
    step, _, x_ref, d_ref, p_ref, gain_ref, bias_ref, wg_ref, og_ref, ob_ref, wo_ref, wot_ref, *refs
):
    g_ref, gb_ref, gwo_ref, gwg_ref, s_ref = refs[-5:]
    rows = x_ref.shape[0]
    width = gb_ref.shape[-1]

    @pl.when((pl.program_id(0) == 0) & (pl.program_id(1) == 0))
    def _():
        gwo_ref[...] = jnp.zeros_like(gwo_ref)
        gwg_ref[...] = jnp.zeros_like(gwg_ref)

    spread_in(p_ref, s_ref)

    @pl.loop(0, rows // step, unroll=min(2, rows // step))
    def _(turn):
        row = pl.multiple_of(turn * step, step)
        z_hat, _ = stats(turned(x_ref, row, step))
        normed = (z_hat * gain_ref[...] + bias_ref[...]).astype(BF16)
        gate = sigmoid(dot(wg_ref[...], normed))
        x_hat, inv_std = stats(load_rows(s_ref, row, step, rows))
        x_norm = (x_hat * og_ref[...] + ob_ref[...]).astype(BF16)
        out_lin = dot(wot_ref[...], x_norm)
        lin = turned(d_ref, row, step) * gate
        grad_lin = lin.astype(BF16)
        gate_back = (lin * out_lin * (1.0 - gate)).astype(BF16)
        upstream = dot(wo_ref[...], grad_lin) * og_ref[...]
        store_rows(s_ref, row, step, rows, norm_back(upstream, x_hat, inv_std))
        for at in range(step):
            gb_ref[row + at] = gate_back[:, at * width : (at + 1) * width]
        gwo_ref[...] += dot(x_norm, grad_lin, NT)
        gwg_ref[...] += dot(normed, gate_back, NT)

    gather_out(s_ref, g_ref)


def make_middle(plan, table, before, ready, x, d, p, small):
    chans = x.shape[-1]
    hidden = p.shape[0]
    cut = table.shape[0]
    grads = [jax.ShapeDtypeStruct((hidden, chans), F32), jax.ShapeDtypeStruct((chans, chans), F32)]
    pairs = plan.pair_spec(chans, lambda i, j, at: (i, at[j, 0], at[j, 1], 0, 0))
    channel = pl.BlockSpec((hidden, plan.rows, plan.width), lambda i, j, at: (0, i, j))
    kept = [*before, *ready]
    return pl.pallas_call(
        functools.partial(middle_kernel, plan.step),
        grid_spec=pltpu.PrefetchScalarGridSpec(
            num_scalar_prefetch=1,
            grid=(plan.subs, cut),
            in_specs=[pairs, pairs, channel]
            + [whole(value) for value in small]
            + [HELD for _ in kept],
            out_specs=[
                channel,
                pl.BlockSpec(
                    (plan.rows, chans, plan.width),
                    lambda i, j, at: (i, 0, at[j, 1] * 2 + at[j, 0]),
                ),
            ]
            + [whole(value) for value in grads],
            scratch_shapes=[plan.scratch(hidden)],
        ),
        out_shape=[
            jax.ShapeDtypeStruct(p.shape, BF16),
            jax.ShapeDtypeStruct((plan.count, chans, plan.crop), BF16),
        ]
        + grads,
        input_output_aliases={4 + len(small): 1} if before else {},
        compiler_params=params(2),
        cost_estimate=cost(0.2),
        name="middle",
    )(table, x, d, p, *small, *kept)


def last_kernel(
    step, x_ref, mask_ref, ga_ref, gb_ref, gate_ref, gain_ref, bias_ref, wt_ref, wcat_ref, *refs
):
    out_ref, gw_ref, sa_ref, sb_ref = refs[-4:]
    rows = x_ref.shape[0]
    hidden = ga_ref.shape[0]

    @pl.when(pl.program_id(0) == 0)
    def _():
        gw_ref[...] = jnp.zeros_like(gw_ref)

    spread_in(ga_ref, sa_ref)
    spread_in(gb_ref, sb_ref)

    @pl.loop(0, rows // step, unroll=min(2, rows // step))
    def _(turn):
        row = pl.multiple_of(turn * step, step)
        z_hat, inv_in = stats(turned(x_ref, row, step))
        normed = (z_hat * gain_ref[...] + bias_ref[...]).astype(BF16)
        mask = flat_rows(mask_ref, row, step)
        proj = dot(wt_ref[...], normed)
        sides = []
        for side, ref in enumerate((sa_ref, sb_ref)):
            value = proj[2 * side * hidden : (2 * side + 1) * hidden]
            sig = sigmoid(proj[(2 * side + 1) * hidden : (2 * side + 2) * hidden])
            to_value = load_rows(ref, row, step, rows) * mask * sig
            sides += [to_value.astype(BF16), (to_value * value * (1.0 - sig)).astype(BF16)]
        grad_proj = jnp.concatenate(sides, axis=0)
        gate_back = jnp.concatenate([gate_ref[row + at] for at in range(step)], axis=1)
        every = jnp.concatenate([grad_proj, gate_back], axis=0)
        upstream = dot(wcat_ref[...], every) * gain_ref[...]
        grad = norm_back(upstream, z_hat, inv_in).T.astype(BF16)
        out_ref[pl.ds(row, step)] = grad.reshape((step,) + out_ref.shape[1:])
        gw_ref[...] += dot(normed, grad_proj, NT)


def make_last(plan, sub, before, ready, x, mask, grad_a, grad_b, gate_back, small):
    chans = x.shape[-1]
    hidden = grad_a.shape[0]
    grad = jax.ShapeDtypeStruct((chans, 4 * hidden), F32)
    pairs = plan.pair_spec(chans, lambda j: (sub, j % 2, j // 2, 0, 0))
    channel = (hidden, plan.rows, plan.width)
    kept = list(ready) if before is None else [before]
    return pl.pallas_call(
        functools.partial(last_kernel, plan.step),
        grid=(plan.blocks,),
        in_specs=[
            pairs,
            pl.BlockSpec((plan.rows, plan.width), lambda j: (sub, j)),
            pl.BlockSpec(channel, lambda j: (0, sub, j)),
            pl.BlockSpec(channel, lambda j: (0, 0, j)),
            pl.BlockSpec((plan.rows, chans, plan.width), lambda j: (sub, 0, j)),
        ]
        + [whole(value) for value in small]
        + [HELD for _ in kept],
        out_specs=[pairs, whole(grad)],
        out_shape=[jax.ShapeDtypeStruct(x.shape, BF16), grad],
        scratch_shapes=[plan.scratch(hidden)] * 2,
        input_output_aliases={} if before is None else {5 + len(small): 0},
        compiler_params=params(1),
        cost_estimate=cost(0.2),
        name="last",
    )(x, mask, grad_a, grad_b, gate_back, *small, *kept)


def swap_all(array):
    return lax.all_to_all(array, "tile", split_axis=0, concat_axis=0, tiled=True)


def tile_sum(array, tiles):
    chans, width = array.shape
    parts = swap_all(array.astype(BF16)).reshape(tiles, chans // tiles, width)
    part = jnp.sum(parts.astype(F32), axis=0).astype(BF16)
    spread = jnp.broadcast_to(part[None], (tiles,) + part.shape).reshape(chans, width)
    return swap_all(spread).astype(F32)


def body(
    tiles, x, d, token_mask, ln_in_gain, ln_in_bias, w_ab, w_gate, ln_out_gain, ln_out_bias, w_out
):
    count, crop, chans = x.shape
    hidden = w_out.shape[0]
    plan = Plan(tiles, count, crop)
    me = lax.axis_index("tile")
    side = (me // plan.half).astype(jnp.int32)
    valid = token_mask.astype(F32)
    own_valid = lax.dynamic_slice_in_dim(valid, me * count, count)
    turned_valid = valid.reshape(tiles, plan.subs, plan.rows).transpose(1, 0, 2).reshape(crop)
    mask = own_valid[:, None] * turned_valid[None, :]
    gain, bias = ln_in_gain[:, None], ln_in_bias[:, None]
    w_t = w_ab.T
    w_cat = jnp.concatenate([w_ab, w_gate], axis=1)
    mid = [gain, bias, w_gate.T, ln_out_gain[:, None], ln_out_bias[:, None], w_out, w_out.T]
    x, d = plan.view(x), plan.view(d)
    owned = lambda array: array.reshape(plan.half, hidden // plan.half, *array.shape[1:])
    joined = lambda array: array.reshape(hidden, *array.shape[2:])
    every = range(plan.subs)

    plan_cut = plan.cut
    two = plan.subs == 2
    cut_a, cut_b = plan_cut(5, 3), plan_cut(3, 2, 3)
    back_a, back_b = plan_cut(3, 1, 4), plan_cut(2, 4, 2)
    small = [gain, bias, w_t, w_cat]

    def middle(at, before, ready, product):
        table = jnp.stack([jnp.stack([half, jnp.int32(sub)]) for half, sub in at])
        g, kept, *local = make_middle(plan, table, before, ready, x, d, product, mid)
        return g, kept, jnp.concatenate(local[::-1], axis=1)

    def summed(own, back):
        return joined(
            (own.astype(F32) + jnp.concatenate(back, axis=0).astype(F32)).astype(BF16)
        )

    def last(sub, before, ready, grad_b):
        return make_last(plan, sub, before, ready, x, mask, grad_a, grad_b, kept, small)

    factor_a, factor_b0 = make_factors(plan, 0, (), x, mask, gain, bias, w_t)
    own_b = [owned(plan.swap(factor_b0))]
    if two:
        factor_a, factor_b1 = make_factors(plan, 1, (factor_a,), x, mask, gain, bias, w_t)
    sent = plan.pieces(own_b[0], cut_a)
    got_a = [plan.exchange(sent[0])]
    own_a = owned(plan.swap(after(factor_a, own_b[0])))
    got_a.append(plan.exchange(sent[1]))
    got_b = []
    if two:
        own_b.append(owned(plan.swap(after(factor_b1, own_a, got_a[0]))))
        sent = plan.pieces(own_b[1], cut_b)
        got_b = [plan.exchange(piece) for piece in sent]
    product = plan.swap(joined(make_product(plan, own_a, got_a + own_b)))
    places = [(1 - side, 0)] + [(side, sub) for sub in every]
    grad, kept, local_mid = middle(places, (), got_b[:1], product)
    owner_g = [owned(plan.swap(after(grad, *got_b[1:2])))]
    parts = make_grad_b(plan, owner_g[0], own_a, back_a + [plan.half] * plan.subs)
    grad_b0, grad_b_own = parts[: len(back_a)], parts[len(back_a) :]
    back_0 = [plan.exchange(piece) for piece in grad_b0]
    other_b, held = got_a + own_b, ()
    if two:
        product = plan.swap(after(joined(make_product(plan, own_a, got_b)), grad_b0[0]))
        grad, kept, local_1 = middle([(1 - side, 1)], (kept,), back_0[:1], product)
        local_mid += local_1
        owner_g.append(owned(plan.swap(after(grad, back_0[1]))))
        held = (owner_g[1],)
    grad_b = plan.swap(after(summed(grad_b_own[0], back_0), *held))
    if two:
        grad_b1 = make_grad_b(plan, owner_g[1], own_a, back_b)
        back_1 = [plan.exchange(piece) for piece in grad_b1]
        other_b, held = other_b + got_b, (grad_b1[0], back_1[0])
    grad_a = joined(make_grad_a(plan, owner_g, other_b))
    grad_a = plan.swap(after(grad_a, grad_b, *held))
    pair_grad, local_ab = last(0, None, (back_1[1],) if two else (grad_b,), grad_b)
    if two:
        grad_b = plan.swap(after(summed(grad_b_own[1], back_1), local_ab))
        pair_grad, local = last(1, pair_grad, (), grad_b)
        local_ab += local
    total = tile_sum(jnp.concatenate([local_ab, local_mid], axis=1), tiles) / crop
    wide = 4 * hidden
    return (
        pair_grad.reshape(count, crop, chans),
        total[:, :wide],
        total[:, wide : wide + chans],
        total[:, wide + chans :],
    )


def solution(mesh):
    pairs = P(("crops", "tile"), None, None)
    return jax.shard_map(
        functools.partial(body, mesh.shape["tile"]),
        mesh=mesh,
        in_specs=(pairs, pairs, P("crops")) + (P(),) * 7,
        out_specs=(pairs,) + (P("crops", None),) * 3,
        check_vma=False,
    )
```

```python
import functools

import jax
import jax.numpy as jnp
from jax import lax
from jax.experimental import pallas as pl
from jax.experimental.pallas import tpu as pltpu
from jax.sharding import PartitionSpec as P

HELD = pl.BlockSpec(memory_space=pl.ANY)
EPS = 1e-05
CHANS = 4
F32 = jnp.float32
BF16 = jnp.bfloat16
NN = (((1,), (0,)), ((), ()))
NT = (((1,), (1,)), ((), ()))
TN = (((0,), (0,)), ((), ()))


def params(steps):
    return pltpu.CompilerParams(
        dimension_semantics=("arbitrary",) * steps, vmem_limit_bytes=50 * 1024 * 1024
    )


def cost(micros):
    return pl.CostEstimate(
        flops=int(micros * 1.0e9), bytes_accessed=int(micros * 3.0e6), transcendentals=0
    )


def dot(left, right, form=NN):
    return lax.dot_general(left, right, form, preferred_element_type=F32)


def sigmoid(value):
    return 0.5 * jnp.tanh(0.5 * value) + 0.5


def col_mean(value):
    return jnp.mean(value, axis=0, keepdims=True)


def stats(value):
    centered = value - col_mean(value)
    inv_std = lax.rsqrt(col_mean(centered * centered) + EPS)
    return centered * inv_std, inv_std


def norm_back(upstream, scaled, inv_std):
    return inv_std * (upstream - col_mean(upstream) - scaled * col_mean(upstream * scaled))


def turned(ref, row, count):
    block = ref[pl.ds(row, count)]
    return block.reshape(-1, block.shape[-1]).astype(F32).T


def lane_parts(scratch, count):
    return [(at, lane) for at in range(count) for lane in range(scratch.shape[0])]


def store_rows(scratch, row, count, rows, value):
    hidden = value.shape[0]
    for part, (at, lane) in enumerate(lane_parts(scratch, count)):
        scratch[lane, pl.ds(row + at, hidden, stride=rows), :] = value[:, part * 128 : (part + 1) * 128]


def load_rows(scratch, row, count, rows):
    hidden = scratch.shape[1] // rows
    return jnp.concatenate(
        [
            scratch[lane, pl.ds(row + at, hidden, stride=rows), :]
            for at, lane in lane_parts(scratch, count)
        ],
        axis=1,
    )


def gather_out(scratch, out_ref):
    hidden, rows, cols = out_ref.shape
    for lane in range(scratch.shape[0]):
        out_ref[:, :, lane * 128 : (lane + 1) * 128] = (
            scratch[lane].reshape(hidden, rows, 128).astype(BF16)
        )


def spread_in(in_ref, scratch):
    hidden, rows, cols = in_ref.shape
    for lane in range(scratch.shape[0]):
        scratch[lane] = (
            in_ref[:, :, lane * 128 : (lane + 1) * 128].astype(F32).reshape(hidden * rows, 128)
        )


def flat_rows(ref, row, count):
    return jnp.concatenate([ref[pl.ds(row + at, 1), :] for at in range(count)], axis=1)


def whole(array):
    return pl.BlockSpec(array.shape, lambda *_: (0,) * array.ndim)


class Plan:
    def __init__(self, tiles, count, crop):
        self.tiles, self.count, self.crop = tiles, count, crop
        self.half = tiles // 2
        self.subs = 2 if count % 32 == 0 else 1
        self.rows = count // self.subs
        self.width = self.half * self.rows
        self.blocks = crop // self.width
        self.step = max(1, 512 // self.width)
        self.groups = [
            [side * self.half + at for at in range(self.half)] for side in range(2)
        ]
        self.partner = [(at, (at + self.half) % tiles) for at in range(tiles)]

    def view(self, array):
        return array.reshape(self.count, self.tiles, self.subs, self.rows, array.shape[-1])

    def pair_spec(self, chans, index):
        return pl.BlockSpec((self.rows, self.half, 1, self.rows, chans), index)

    def scratch(self, hidden):
        return pltpu.VMEM((self.width // 128, self.rows * hidden, 128), F32)

    def swap(self, array):
        return lax.all_to_all(
            array, "tile", split_axis=0, concat_axis=0, axis_index_groups=self.groups, tiled=True
        )

    def cut(self, *eighths):
        return [max(1, self.half * share // 8) for share in eighths]

    def pieces(self, array, counts):
        ends = [sum(counts[: at + 1]) for at in range(len(counts))]
        return [array[end - size : end] for size, end in zip(counts, ends)]

    def exchange(self, array):
        return lax.ppermute(array, "tile", self.partner)


def after_kernel(*refs):
    del refs


def after(value, *others):
    return pl.pallas_call(
        after_kernel,
        in_specs=[HELD] * (1 + len(others)),
        out_specs=HELD,
        out_shape=jax.ShapeDtypeStruct(value.shape, value.dtype),
        input_output_aliases={0: 0},
        compiler_params=params(0),
        cost_estimate=cost(0.1),
        name="after",
    )(value, *others)


def factors_kernel(step, x_ref, mask_ref, gain_ref, bias_ref, w_ref, *refs):
    fa_ref, fb_ref, sa_ref, sb_ref = refs[-4:]
    rows = x_ref.shape[0]
    hidden = fa_ref.shape[0]

    @pl.loop(0, rows // step, unroll=min(4, rows // step))
    def _(turn):
        row = pl.multiple_of(turn * step, step)
        z_hat, _ = stats(turned(x_ref, row, step))
        normed = (z_hat * gain_ref[...] + bias_ref[...]).astype(BF16)
        mask = flat_rows(mask_ref, row, step)
        proj = dot(w_ref[...], normed)
        value_a, gate_a = proj[:hidden], proj[hidden : 2 * hidden]
        value_b, gate_b = proj[2 * hidden : 3 * hidden], proj[3 * hidden :]
        store_rows(sb_ref, row, step, rows, mask * sigmoid(gate_b) * value_b)
        store_rows(sa_ref, row, step, rows, mask * sigmoid(gate_a) * value_a)

    gather_out(sa_ref, fa_ref)
    gather_out(sb_ref, fb_ref)


def make_factors(plan, sub, before, x, mask, gain, bias, w_t):
    chans = x.shape[-1]
    hidden = w_t.shape[0] // 4
    block = (hidden, plan.rows, plan.width)
    return pl.pallas_call(
        functools.partial(factors_kernel, plan.step),
        grid=(plan.blocks,),
        in_specs=[
            plan.pair_spec(chans, lambda j: (sub, j % 2, j // 2, 0, 0)),
            pl.BlockSpec((plan.rows, plan.width), lambda j: (sub, j)),
            whole(gain),
            whole(bias),
            whole(w_t),
        ]
        + [HELD for _ in before],
        out_specs=[
            pl.BlockSpec(block, lambda j: (0, sub, j)),
            pl.BlockSpec(block, lambda j: (0, 0, j)),
        ],
        out_shape=[
            jax.ShapeDtypeStruct((hidden, plan.count, plan.crop), BF16),
            jax.ShapeDtypeStruct((hidden, plan.rows, plan.crop), BF16),
        ],
        input_output_aliases={5: 0} if before else {},
        scratch_shapes=[plan.scratch(hidden)] * 2,
        compiler_params=params(1),
        cost_estimate=cost(0.2),
        name="factors",
    )(x, mask, gain, bias, w_t, *before)


def matrix(refs, chan):
    parts = [ref[:, chan].reshape(-1, ref.shape[-1]) for ref in refs]
    return jnp.concatenate(parts, axis=0) if len(parts) > 1 else parts[0]


def by_sub(ref, chan, subs):
    rows = ref.shape[2] // subs
    parts = [
        ref[:, chan, sub * rows : (sub + 1) * rows, :].reshape(-1, ref.shape[3])
        for sub in range(subs)
    ]
    return jnp.concatenate(parts, axis=0) if subs > 1 else parts[0]


def to_subs(ref, chan, value, subs):
    tiles, _, rows, cols = ref.shape
    part = value.shape[0] // subs
    for sub in range(subs):
        ref[:, chan, sub * (rows // subs) : (sub + 1) * (rows // subs), :] = value[
            sub * part : (sub + 1) * part
        ].astype(BF16).reshape(tiles, rows // subs, cols)


def own_spec(array):
    src, _, rows, cols = array.shape
    return pl.BlockSpec((src, CHANS, rows, cols), lambda h: (0, h, 0, 0))


def product_kernel(subs, a_ref, *refs):
    b, p_ref = refs[:-1], refs[-1]
    for chan in range(CHANS):
        to_subs(p_ref, chan, dot(by_sub(a_ref, chan, subs), matrix(b, chan), NT), subs)


def make_product(plan, a, b):
    tiles, chans, _, _ = a.shape
    cols = sum(value.shape[0] for value in b) * plan.rows
    out = jax.ShapeDtypeStruct((tiles, chans, plan.count, cols), BF16)
    return pl.pallas_call(
        functools.partial(product_kernel, plan.subs),
        grid=(chans // CHANS,),
        in_specs=[own_spec(value) for value in (a, *b)],
        out_specs=own_spec(out),
        out_shape=out,
        compiler_params=params(1),
        cost_estimate=cost(0.2),
        name="product",
    )(a, *b)


def grad_b_kernel(subs, g_ref, a_ref, *outs):
    for chan in range(CHANS):
        grad = dot(by_sub(g_ref, chan, subs), by_sub(a_ref, chan, subs), TN).astype(BF16)
        at = 0
        for out in outs:
            size = out.shape[0] * out.shape[2]
            out[:, chan] = grad[at : at + size].reshape(out.shape[0], *out.shape[2:])
            at += size


def make_grad_b(plan, g, a, tiles):
    outs = [
        jax.ShapeDtypeStruct((count, a.shape[1], plan.rows, plan.crop), BF16) for count in tiles
    ]
    return pl.pallas_call(
        functools.partial(grad_b_kernel, plan.subs),
        grid=(g.shape[1] // CHANS,),
        in_specs=[own_spec(value) for value in (g, a)],
        out_specs=[own_spec(value) for value in outs],
        out_shape=outs,
        compiler_params=params(1),
        cost_estimate=cost(0.2),
        name="grad_b",
    )(g, a)


def grad_a_kernel(subs, count, *refs):
    g, b, out = refs[:count], refs[count:-1], refs[-1]
    for chan in range(CHANS):
        rows = jnp.concatenate([by_sub(ref, chan, subs) for ref in g], axis=1)
        to_subs(out, chan, dot(rows, matrix(b, chan)), subs)


def make_grad_a(plan, g, b):
    chans = b[0].shape[1]
    out = jax.ShapeDtypeStruct((plan.half, chans, plan.count, plan.crop), BF16)
    return pl.pallas_call(
        functools.partial(grad_a_kernel, plan.subs, len(g)),
        grid=(chans // CHANS,),
        in_specs=[own_spec(value) for value in (*g, *b)],
        out_specs=own_spec(out),
        out_shape=out,
        compiler_params=params(1),
        cost_estimate=cost(0.2),
        name="grad_a",
    )(*g, *b)


def middle_kernel(
    step, _, x_ref, d_ref, p_ref, gain_ref, bias_ref, wg_ref, og_ref, ob_ref, wo_ref, wot_ref, *refs
):
    g_ref, gb_ref, gwo_ref, gwg_ref, s_ref = refs[-5:]
    rows = x_ref.shape[0]
    width = gb_ref.shape[-1]

    @pl.when((pl.program_id(0) == 0) & (pl.program_id(1) == 0))
    def _():
        gwo_ref[...] = jnp.zeros_like(gwo_ref)
        gwg_ref[...] = jnp.zeros_like(gwg_ref)

    spread_in(p_ref, s_ref)

    @pl.loop(0, rows // step, unroll=min(4, rows // step))
    def _(turn):
        row = pl.multiple_of(turn * step, step)
        z_hat, _ = stats(turned(x_ref, row, step))
        normed = (z_hat * gain_ref[...] + bias_ref[...]).astype(BF16)
        gate = sigmoid(dot(wg_ref[...], normed))
        x_hat, inv_std = stats(load_rows(s_ref, row, step, rows))
        x_norm = (x_hat * og_ref[...] + ob_ref[...]).astype(BF16)
        out_lin = dot(wot_ref[...], x_norm)
        lin = turned(d_ref, row, step) * gate
        grad_lin = lin.astype(BF16)
        gate_back = (lin * out_lin * (1.0 - gate)).astype(BF16)
        upstream = dot(wo_ref[...], grad_lin) * og_ref[...]
        store_rows(s_ref, row, step, rows, norm_back(upstream, x_hat, inv_std))
        for at in range(step):
            gb_ref[row + at] = gate_back[:, at * width : (at + 1) * width]
        gwo_ref[...] += dot(x_norm, grad_lin, NT)
        gwg_ref[...] += dot(normed, gate_back, NT)

    gather_out(s_ref, g_ref)


def make_middle(plan, table, before, ready, x, d, p, small):
    chans = x.shape[-1]
    hidden = p.shape[0]
    cut = table.shape[0]
    grads = [jax.ShapeDtypeStruct((hidden, chans), F32), jax.ShapeDtypeStruct((chans, chans), F32)]
    pairs = plan.pair_spec(chans, lambda i, j, at: (i, at[j, 0], at[j, 1], 0, 0))
    channel = pl.BlockSpec((hidden, plan.rows, plan.width), lambda i, j, at: (0, i, j))
    kept = [*before, *ready]
    return pl.pallas_call(
        functools.partial(middle_kernel, plan.step),
        grid_spec=pltpu.PrefetchScalarGridSpec(
            num_scalar_prefetch=1,
            grid=(plan.subs, cut),
            in_specs=[pairs, pairs, channel]
            + [whole(value) for value in small]
            + [HELD for _ in kept],
            out_specs=[
                channel,
                pl.BlockSpec(
                    (plan.rows, chans, plan.width),
                    lambda i, j, at: (i, 0, at[j, 1] * 2 + at[j, 0]),
                ),
            ]
            + [whole(value) for value in grads],
            scratch_shapes=[plan.scratch(hidden)],
        ),
        out_shape=[
            jax.ShapeDtypeStruct(p.shape, BF16),
            jax.ShapeDtypeStruct((plan.count, chans, plan.crop), BF16),
        ]
        + grads,
        input_output_aliases={4 + len(small): 1} if before else {},
        compiler_params=params(2),
        cost_estimate=cost(0.2),
        name="middle",
    )(table, x, d, p, *small, *kept)


def last_kernel(
    step, x_ref, mask_ref, ga_ref, gb_ref, gate_ref, gain_ref, bias_ref, wt_ref, wcat_ref, *refs
):
    out_ref, gw_ref, sa_ref, sb_ref = refs[-4:]
    rows = x_ref.shape[0]
    hidden = ga_ref.shape[0]

    @pl.when(pl.program_id(0) == 0)
    def _():
        gw_ref[...] = jnp.zeros_like(gw_ref)

    spread_in(ga_ref, sa_ref)
    spread_in(gb_ref, sb_ref)

    @pl.loop(0, rows // step, unroll=min(4, rows // step))
    def _(turn):
        row = pl.multiple_of(turn * step, step)
        z_hat, inv_in = stats(turned(x_ref, row, step))
        normed = (z_hat * gain_ref[...] + bias_ref[...]).astype(BF16)
        mask = flat_rows(mask_ref, row, step)
        proj = dot(wt_ref[...], normed)
        sides = []
        for side, ref in enumerate((sa_ref, sb_ref)):
            value = proj[2 * side * hidden : (2 * side + 1) * hidden]
            sig = sigmoid(proj[(2 * side + 1) * hidden : (2 * side + 2) * hidden])
            to_value = load_rows(ref, row, step, rows) * mask * sig
            sides += [to_value.astype(BF16), (to_value * value * (1.0 - sig)).astype(BF16)]
        grad_proj = jnp.concatenate(sides, axis=0)
        gate_back = jnp.concatenate([gate_ref[row + at] for at in range(step)], axis=1)
        every = jnp.concatenate([grad_proj, gate_back], axis=0)
        upstream = dot(wcat_ref[...], every) * gain_ref[...]
        grad = norm_back(upstream, z_hat, inv_in).T.astype(BF16)
        out_ref[pl.ds(row, step)] = grad.reshape((step,) + out_ref.shape[1:])
        gw_ref[...] += dot(normed, grad_proj, NT)


def make_last(plan, sub, before, ready, x, mask, grad_a, grad_b, gate_back, small):
    chans = x.shape[-1]
    hidden = grad_a.shape[0]
    grad = jax.ShapeDtypeStruct((chans, 4 * hidden), F32)
    pairs = plan.pair_spec(chans, lambda j: (sub, j % 2, j // 2, 0, 0))
    channel = (hidden, plan.rows, plan.width)
    kept = list(ready) if before is None else [before]
    return pl.pallas_call(
        functools.partial(last_kernel, plan.step),
        grid=(plan.blocks,),
        in_specs=[
            pairs,
            pl.BlockSpec((plan.rows, plan.width), lambda j: (sub, j)),
            pl.BlockSpec(channel, lambda j: (0, sub, j)),
            pl.BlockSpec(channel, lambda j: (0, 0, j)),
            pl.BlockSpec((plan.rows, chans, plan.width), lambda j: (sub, 0, j)),
        ]
        + [whole(value) for value in small]
        + [HELD for _ in kept],
        out_specs=[pairs, whole(grad)],
        out_shape=[jax.ShapeDtypeStruct(x.shape, BF16), grad],
        scratch_shapes=[plan.scratch(hidden)] * 2,
        input_output_aliases={} if before is None else {5 + len(small): 0},
        compiler_params=params(1),
        cost_estimate=cost(0.2),
        name="last",
    )(x, mask, grad_a, grad_b, gate_back, *small, *kept)


def swap_all(array):
    return lax.all_to_all(array, "tile", split_axis=0, concat_axis=0, tiled=True)


def tile_sum(array, tiles):
    chans, width = array.shape
    parts = swap_all(array.astype(BF16)).reshape(tiles, chans // tiles, width)
    part = jnp.sum(parts.astype(F32), axis=0).astype(BF16)
    spread = jnp.broadcast_to(part[None], (tiles,) + part.shape).reshape(chans, width)
    return swap_all(spread).astype(F32)


def body(
    tiles, x, d, token_mask, ln_in_gain, ln_in_bias, w_ab, w_gate, ln_out_gain, ln_out_bias, w_out
):
    count, crop, chans = x.shape
    hidden = w_out.shape[0]
    plan = Plan(tiles, count, crop)
    me = lax.axis_index("tile")
    side = (me // plan.half).astype(jnp.int32)
    valid = token_mask.astype(F32)
    own_valid = lax.dynamic_slice_in_dim(valid, me * count, count)
    turned_valid = valid.reshape(tiles, plan.subs, plan.rows).transpose(1, 0, 2).reshape(crop)
    mask = own_valid[:, None] * turned_valid[None, :]
    gain, bias = ln_in_gain[:, None], ln_in_bias[:, None]
    w_t = w_ab.T
    w_cat = jnp.concatenate([w_ab, w_gate], axis=1)
    mid = [gain, bias, w_gate.T, ln_out_gain[:, None], ln_out_bias[:, None], w_out, w_out.T]
    x, d = plan.view(x), plan.view(d)
    owned = lambda array: array.reshape(plan.half, hidden // plan.half, *array.shape[1:])
    joined = lambda array: array.reshape(hidden, *array.shape[2:])
    every = range(plan.subs)

    plan_cut = plan.cut
    two = plan.subs == 2
    cut_a, cut_b = plan_cut(5, 3), plan_cut(4, 4)
    back_a, back_b = plan_cut(3, 2, 3), plan_cut(2, 3, 3)
    small = [gain, bias, w_t, w_cat]

    def middle(at, before, ready, product):
        table = jnp.stack([jnp.stack([half, jnp.int32(sub)]) for half, sub in at])
        g, kept, *local = make_middle(plan, table, before, ready, x, d, product, mid)
        return g, kept, jnp.concatenate(local[::-1], axis=1)

    def summed(own, back):
        return joined(
            (own.astype(F32) + jnp.concatenate(back, axis=0).astype(F32)).astype(BF16)
        )

    def last(sub, before, ready, grad_b):
        return make_last(plan, sub, before, ready, x, mask, grad_a, grad_b, kept, small)

    factor_a, factor_b0 = make_factors(plan, 0, (), x, mask, gain, bias, w_t)
    own_b = [owned(plan.swap(factor_b0))]
    if two:
        factor_a, factor_b1 = make_factors(plan, 1, (factor_a,), x, mask, gain, bias, w_t)
    sent = plan.pieces(own_b[0], cut_a)
    got_a = [plan.exchange(sent[0])]
    own_a = owned(plan.swap(after(factor_a, own_b[0])))
    got_a.append(plan.exchange(sent[1]))
    got_b = []
    if two:
        own_b.append(owned(plan.swap(after(factor_b1, own_a, got_a[0]))))
        sent = plan.pieces(own_b[1], cut_b)
        got_b = [plan.exchange(piece) for piece in sent]
    product = plan.swap(joined(make_product(plan, own_a, got_a + own_b)))
    places = [(1 - side, 0)] + [(side, sub) for sub in every]
    grad, kept, local_mid = middle(places, (), got_b[:1], product)
    owner_g = [owned(plan.swap(after(grad, *got_b[1:2])))]
    parts = make_grad_b(plan, owner_g[0], own_a, back_a + [plan.half] * plan.subs)
    grad_b0, grad_b_own = parts[: len(back_a)], parts[len(back_a) :]
    back_0 = [plan.exchange(piece) for piece in grad_b0]
    other_b, held = got_a + own_b, ()
    if two:
        got_b[0] = after(got_b[0], grad_b0[0])
        product = plan.swap(joined(make_product(plan, own_a, got_b)))
        grad, kept, local_1 = middle([(1 - side, 1)], (kept,), (), product)
        local_mid += local_1
        owner_g.append(after(owned(plan.swap(after(grad, back_0[0]))), back_0[1]))
        grad_b1 = make_grad_b(plan, owner_g[1], own_a, back_b)
        back_1 = [plan.exchange(piece) for piece in grad_b1]
        other_b, held = other_b + got_b, (grad_b1[0],)
    grad_a = joined(make_grad_a(plan, owner_g, other_b))
    grad_a = plan.swap(after(grad_a, *held))
    held = (grad_a, back_1[0]) if two else (grad_a,)
    grad_b = plan.swap(after(summed(grad_b_own[0], back_0), *held))
    pair_grad, local_ab = last(0, None, (back_1[1],) if two else (grad_b,), grad_b)
    if two:
        grad_b = plan.swap(after(summed(grad_b_own[1], back_1), local_ab))
        pair_grad, local = last(1, pair_grad, (), grad_b)
        local_ab += local
    total = tile_sum(jnp.concatenate([local_ab, local_mid], axis=1), tiles) / crop
    wide = 4 * hidden
    return (
        pair_grad.reshape(count, crop, chans),
        total[:, :wide],
        total[:, wide : wide + chans],
        total[:, wide + chans :],
    )


def solution(mesh):
    pairs = P(("crops", "tile"), None, None)
    return jax.shard_map(
        functools.partial(body, mesh.shape["tile"]),
        mesh=mesh,
        in_specs=(pairs, pairs, P("crops")) + (P(),) * 7,
        out_specs=(pairs,) + (P("crops", None),) * 3,
        check_vma=False,
    )
```

```python
import functools

import jax
import jax.numpy as jnp
from jax import lax
from jax.experimental import pallas as pl
from jax.experimental.pallas import tpu as pltpu
from jax.sharding import PartitionSpec as P

HELD = pl.BlockSpec(memory_space=pl.ANY)
EPS = 1e-05
CHANS = 4
F32 = jnp.float32
BF16 = jnp.bfloat16
NN = (((1,), (0,)), ((), ()))
NT = (((1,), (1,)), ((), ()))
TN = (((0,), (0,)), ((), ()))


def params(steps):
    return pltpu.CompilerParams(
        dimension_semantics=("arbitrary",) * steps, vmem_limit_bytes=50 * 1024 * 1024
    )


def cost(micros):
    return pl.CostEstimate(
        flops=int(micros * 1.0e9), bytes_accessed=int(micros * 3.0e6), transcendentals=0
    )


def dot(left, right, form=NN):
    return lax.dot_general(left, right, form, preferred_element_type=F32)


def sigmoid(value):
    return 0.5 * jnp.tanh(0.5 * value) + 0.5


def col_mean(value):
    return jnp.mean(value, axis=0, keepdims=True)


def stats(value):
    centered = value - col_mean(value)
    inv_std = lax.rsqrt(col_mean(centered * centered) + EPS)
    return centered * inv_std, inv_std


def norm_back(upstream, scaled, inv_std):
    return inv_std * (upstream - col_mean(upstream) - scaled * col_mean(upstream * scaled))


def turned(ref, row, count):
    block = ref[pl.ds(row, count)]
    return block.reshape(-1, block.shape[-1]).astype(F32).T


def lane_parts(scratch, count):
    return [(at, lane) for at in range(count) for lane in range(scratch.shape[0])]


def store_rows(scratch, row, count, rows, value):
    hidden = value.shape[0]
    for part, (at, lane) in enumerate(lane_parts(scratch, count)):
        scratch[lane, pl.ds(row + at, hidden, stride=rows), :] = value[:, part * 128 : (part + 1) * 128]


def load_rows(scratch, row, count, rows):
    hidden = scratch.shape[1] // rows
    return jnp.concatenate(
        [
            scratch[lane, pl.ds(row + at, hidden, stride=rows), :]
            for at, lane in lane_parts(scratch, count)
        ],
        axis=1,
    )


def gather_out(scratch, out_ref, rows, at=0):
    hidden = out_ref.shape[0]
    for lane in range(scratch.shape[0]):
        out_ref[:, at : at + rows, lane * 128 : (lane + 1) * 128] = (
            scratch[lane].reshape(hidden, rows, 128).astype(BF16)
        )


def spread_in(in_ref, scratch):
    hidden, rows, cols = in_ref.shape
    for lane in range(scratch.shape[0]):
        scratch[lane] = (
            in_ref[:, :, lane * 128 : (lane + 1) * 128].astype(F32).reshape(hidden * rows, 128)
        )


def flat_rows(ref, row, count):
    return jnp.concatenate([ref[pl.ds(row + at, 1), :] for at in range(count)], axis=1)


def whole(array):
    return pl.BlockSpec(array.shape, lambda *_: (0,) * array.ndim)


class Plan:
    def __init__(self, tiles, count, crop):
        self.tiles, self.count, self.crop = tiles, count, crop
        self.half = tiles // 2
        self.subs = 2 if count % 32 == 0 else 1
        self.rows = count // self.subs
        self.width = self.half * self.rows
        self.blocks = crop // self.width
        self.step = max(1, 512 // self.width)
        self.groups = [
            [side * self.half + at for at in range(self.half)] for side in range(2)
        ]
        self.partner = [(at, (at + self.half) % tiles) for at in range(tiles)]

    def view(self, array):
        return array.reshape(self.count, self.tiles, self.subs, self.rows, array.shape[-1])

    def pair_spec(self, chans, index):
        return pl.BlockSpec((self.rows, self.half, 1, self.rows, chans), index)

    def scratch(self, hidden):
        return pltpu.VMEM((self.width // 128, self.rows * hidden, 128), F32)

    def swap(self, array):
        return lax.all_to_all(
            array, "tile", split_axis=0, concat_axis=0, axis_index_groups=self.groups, tiled=True
        )

    def cut(self, *eighths):
        return [max(1, self.half * share // 8) for share in eighths]

    def pieces(self, array, counts):
        ends = [sum(counts[: at + 1]) for at in range(len(counts))]
        return [array[end - size : end] for size, end in zip(counts, ends)]

    def exchange(self, array):
        return lax.ppermute(array, "tile", self.partner)


def after_kernel(*refs):
    del refs


def after(value, *others):
    return pl.pallas_call(
        after_kernel,
        in_specs=[HELD] * (1 + len(others)),
        out_specs=HELD,
        out_shape=jax.ShapeDtypeStruct(value.shape, value.dtype),
        input_output_aliases={0: 0},
        compiler_params=params(0),
        cost_estimate=cost(0.1),
        name="after",
    )(value, *others)


def factors_kernel(step, joint, x_ref, mask_ref, gain_ref, bias_ref, w_ref, *refs):
    sa_ref, sb_ref = refs[-2:]
    rows = x_ref.shape[0]
    hidden = w_ref.shape[0] // 4

    @pl.loop(0, rows // step, unroll=min(4, rows // step))
    def _(turn):
        row = pl.multiple_of(turn * step, step)
        z_hat, _ = stats(turned(x_ref, row, step))
        normed = (z_hat * gain_ref[...] + bias_ref[...]).astype(BF16)
        mask = flat_rows(mask_ref, row, step)
        proj = dot(w_ref[...], normed)
        value_a, gate_a = proj[:hidden], proj[hidden : 2 * hidden]
        value_b, gate_b = proj[2 * hidden : 3 * hidden], proj[3 * hidden :]
        store_rows(sb_ref, row, step, rows, mask * sigmoid(gate_b) * value_b)
        store_rows(sa_ref, row, step, rows, mask * sigmoid(gate_a) * value_a)

    if joint:
        gather_out(sa_ref, refs[-3], rows)
        gather_out(sb_ref, refs[-3], rows, rows)
    else:
        gather_out(sa_ref, refs[-4], rows)
        gather_out(sb_ref, refs[-3], rows)


def make_factors(plan, sub, before, x, mask, gain, bias, w_t):
    chans = x.shape[-1]
    hidden = w_t.shape[0] // 4
    block = (hidden, plan.rows, plan.width)
    held = plan.rows * (3 if plan.subs == 2 else 1)
    out_specs = [
        pl.BlockSpec(block, lambda j: (0, 2 * (plan.subs - 1), j)),
        pl.BlockSpec(block, lambda j: (0, 0, j)),
    ]
    out_shape = [
        jax.ShapeDtypeStruct((hidden, held, plan.crop), BF16),
        jax.ShapeDtypeStruct((hidden, plan.rows, plan.crop), BF16),
    ]
    if before:
        out_specs = [pl.BlockSpec((hidden, 2 * plan.rows, plan.width), lambda j: (0, 0, j))]
        out_shape = out_shape[:1]
    return pl.pallas_call(
        functools.partial(factors_kernel, plan.step, bool(before)),
        grid=(plan.blocks,),
        in_specs=[
            plan.pair_spec(chans, lambda j: (sub, j % 2, j // 2, 0, 0)),
            pl.BlockSpec((plan.rows, plan.width), lambda j: (sub, j)),
            whole(gain),
            whole(bias),
            whole(w_t),
        ]
        + [HELD for _ in before],
        out_specs=out_specs,
        out_shape=out_shape,
        input_output_aliases={5: 0} if before else {},
        scratch_shapes=[plan.scratch(hidden)] * 2,
        compiler_params=params(1),
        cost_estimate=cost(0.2),
        name="factors",
    )(x, mask, gain, bias, w_t, *before)


def matrix(refs, chan):
    parts = [ref[:, chan].reshape(-1, ref.shape[-1]) for ref in refs]
    return jnp.concatenate(parts, axis=0) if len(parts) > 1 else parts[0]


def by_sub(ref, chan, subs):
    rows = ref.shape[2] // subs
    parts = [
        ref[:, chan, sub * rows : (sub + 1) * rows, :].reshape(-1, ref.shape[3])
        for sub in range(subs)
    ]
    return jnp.concatenate(parts, axis=0) if subs > 1 else parts[0]


def to_subs(ref, chan, value, subs, rows):
    part = value.shape[0] // subs
    for sub in range(subs):
        ref[:, chan, sub * rows : (sub + 1) * rows, :] = value[
            sub * part : (sub + 1) * part
        ].astype(BF16).reshape(ref.shape[0], rows, ref.shape[3])


def own_spec(array):
    src, _, rows, cols = array.shape
    return pl.BlockSpec((src, CHANS, rows, cols), lambda h: (0, h, 0, 0))


def view_spec(plan, view):
    array, at = view
    return pl.BlockSpec((array.shape[0], CHANS, plan.rows, array.shape[3]), lambda h: (0, h, at, 0))


def arrays(views):
    return [array for array, _ in views]


def product_kernel(subs, rows, *refs):
    a, b, p_ref = refs[:subs], refs[subs:-1], refs[-1]
    for chan in range(CHANS):
        to_subs(p_ref, chan, dot(matrix(a, chan), matrix(b, chan), NT), subs, rows)


def make_product(plan, a, b):
    tiles, chans = a[0][0].shape[:2]
    cols = sum(array.shape[0] for array in arrays(b)) * plan.rows
    out = jax.ShapeDtypeStruct((tiles, chans, plan.count, cols), BF16)
    return pl.pallas_call(
        functools.partial(product_kernel, plan.subs, plan.rows),
        grid=(chans // CHANS,),
        in_specs=[view_spec(plan, view) for view in (*a, *b)],
        out_specs=own_spec(out),
        out_shape=out,
        compiler_params=params(1),
        cost_estimate=cost(0.2),
        name="product",
    )(*arrays(a), *arrays(b))


def grad_b_kernel(subs, g_ref, *refs):
    a, outs = refs[:subs], refs[subs:]
    for chan in range(CHANS):
        grad = dot(by_sub(g_ref, chan, subs), matrix(a, chan), TN).astype(BF16)
        at = 0
        for out in outs:
            size = out.shape[0] * out.shape[2]
            out[:, chan] = grad[at : at + size].reshape(out.shape[0], *out.shape[2:])
            at += size


def make_grad_b(plan, g, a, tiles):
    outs = [
        jax.ShapeDtypeStruct((count, g.shape[1], plan.rows, plan.crop), BF16) for count in tiles
    ]
    return pl.pallas_call(
        functools.partial(grad_b_kernel, plan.subs),
        grid=(g.shape[1] // CHANS,),
        in_specs=[own_spec(g)] + [view_spec(plan, view) for view in a],
        out_specs=[own_spec(value) for value in outs],
        out_shape=outs,
        compiler_params=params(1),
        cost_estimate=cost(0.2),
        name="grad_b",
    )(g, *arrays(a))


def grad_a_kernel(subs, rows, counts, *refs):
    g, b = refs[: counts[0]], refs[counts[0] : counts[0] + counts[1]]
    own, back, out = refs[counts[0] + counts[1]], refs[counts[0] + counts[1] + 1 : -1], refs[-1]
    for chan in range(CHANS):
        left = jnp.concatenate([by_sub(ref, chan, subs) for ref in g], axis=1)
        to_subs(out, chan, dot(left, matrix(b, chan)), subs, rows)
        at = 0
        for piece in back:
            end = at + piece.shape[0]
            added = own[at:end, chan].astype(F32) + piece[:, chan].astype(F32)
            out[at:end, chan, subs * rows :, :] = added.astype(BF16)
            at = end


def make_grad_a(plan, g, b, own, back):
    chans = own.shape[1]
    out = jax.ShapeDtypeStruct((plan.half, chans, plan.count + plan.rows, plan.crop), BF16)
    return pl.pallas_call(
        functools.partial(grad_a_kernel, plan.subs, plan.rows, (len(g), len(b))),
        grid=(chans // CHANS,),
        in_specs=[own_spec(value) for value in g]
        + [view_spec(plan, view) for view in b]
        + [own_spec(value) for value in (own, *back)],
        out_specs=own_spec(out),
        out_shape=out,
        compiler_params=params(1),
        cost_estimate=cost(0.2),
        name="grad_a",
    )(*g, *arrays(b), own, *back)


def middle_kernel(
    step, _, x_ref, d_ref, p_ref, gain_ref, bias_ref, wg_ref, og_ref, ob_ref, wo_ref, wot_ref, *refs
):
    g_ref, gb_ref, gwo_ref, gwg_ref, s_ref = refs[-5:]
    rows = x_ref.shape[0]
    width = gb_ref.shape[-1]

    @pl.when((pl.program_id(0) == 0) & (pl.program_id(1) == 0))
    def _():
        gwo_ref[...] = jnp.zeros_like(gwo_ref)
        gwg_ref[...] = jnp.zeros_like(gwg_ref)

    spread_in(p_ref, s_ref)

    @pl.loop(0, rows // step, unroll=min(4, rows // step))
    def _(turn):
        row = pl.multiple_of(turn * step, step)
        z_hat, _ = stats(turned(x_ref, row, step))
        normed = (z_hat * gain_ref[...] + bias_ref[...]).astype(BF16)
        gate = sigmoid(dot(wg_ref[...], normed))
        x_hat, inv_std = stats(load_rows(s_ref, row, step, rows))
        x_norm = (x_hat * og_ref[...] + ob_ref[...]).astype(BF16)
        out_lin = dot(wot_ref[...], x_norm)
        lin = turned(d_ref, row, step) * gate
        grad_lin = lin.astype(BF16)
        gate_back = (lin * out_lin * (1.0 - gate)).astype(BF16)
        upstream = dot(wo_ref[...], grad_lin) * og_ref[...]
        store_rows(s_ref, row, step, rows, norm_back(upstream, x_hat, inv_std))
        for at in range(step):
            gb_ref[row + at] = gate_back[:, at * width : (at + 1) * width]
        gwo_ref[...] += dot(x_norm, grad_lin, NT)
        gwg_ref[...] += dot(normed, gate_back, NT)

    gather_out(s_ref, g_ref, rows)


def make_middle(plan, table, before, ready, x, d, p, small):
    chans = x.shape[-1]
    hidden = p.shape[0]
    cut = table.shape[0]
    grads = [jax.ShapeDtypeStruct((hidden, chans), F32), jax.ShapeDtypeStruct((chans, chans), F32)]
    pairs = plan.pair_spec(chans, lambda i, j, at: (i, at[j, 0], at[j, 1], 0, 0))
    channel = pl.BlockSpec((hidden, plan.rows, plan.width), lambda i, j, at: (0, i, j))
    kept = [*before, *ready]
    return pl.pallas_call(
        functools.partial(middle_kernel, plan.step),
        grid_spec=pltpu.PrefetchScalarGridSpec(
            num_scalar_prefetch=1,
            grid=(plan.subs, cut),
            in_specs=[pairs, pairs, channel]
            + [whole(value) for value in small]
            + [HELD for _ in kept],
            out_specs=[
                channel,
                pl.BlockSpec(
                    (plan.rows, chans, plan.width),
                    lambda i, j, at: (i, 0, at[j, 1] * 2 + at[j, 0]),
                ),
            ]
            + [whole(value) for value in grads],
            scratch_shapes=[plan.scratch(hidden)],
        ),
        out_shape=[
            jax.ShapeDtypeStruct(p.shape, BF16),
            jax.ShapeDtypeStruct((plan.count, chans, plan.crop), BF16),
        ]
        + grads,
        input_output_aliases={4 + len(small): 1} if before else {},
        compiler_params=params(2),
        cost_estimate=cost(0.2),
        name="middle",
    )(table, x, d, p, *small, *kept)


def last_kernel(
    step, x_ref, mask_ref, ga_ref, gb_ref, gate_ref, gain_ref, bias_ref, wt_ref, wcat_ref, *refs
):
    out_ref, gw_ref, sa_ref, sb_ref = refs[-4:]
    rows = x_ref.shape[0]
    hidden = ga_ref.shape[0]

    @pl.when(pl.program_id(0) == 0)
    def _():
        gw_ref[...] = jnp.zeros_like(gw_ref)

    spread_in(ga_ref, sa_ref)
    spread_in(gb_ref, sb_ref)

    @pl.loop(0, rows // step, unroll=min(4, rows // step))
    def _(turn):
        row = pl.multiple_of(turn * step, step)
        z_hat, inv_in = stats(turned(x_ref, row, step))
        normed = (z_hat * gain_ref[...] + bias_ref[...]).astype(BF16)
        mask = flat_rows(mask_ref, row, step)
        proj = dot(wt_ref[...], normed)
        sides = []
        for side, ref in enumerate((sa_ref, sb_ref)):
            value = proj[2 * side * hidden : (2 * side + 1) * hidden]
            sig = sigmoid(proj[(2 * side + 1) * hidden : (2 * side + 2) * hidden])
            to_value = load_rows(ref, row, step, rows) * mask * sig
            sides += [to_value.astype(BF16), (to_value * value * (1.0 - sig)).astype(BF16)]
        grad_proj = jnp.concatenate(sides, axis=0)
        gate_back = jnp.concatenate([gate_ref[row + at] for at in range(step)], axis=1)
        every = jnp.concatenate([grad_proj, gate_back], axis=0)
        upstream = dot(wcat_ref[...], every) * gain_ref[...]
        grad = norm_back(upstream, z_hat, inv_in).T.astype(BF16)
        out_ref[pl.ds(row, step)] = grad.reshape((step,) + out_ref.shape[1:])
        gw_ref[...] += dot(normed, grad_proj, NT)


def make_last(plan, sub, before, x, mask, grad_a, grad_b, at, gate_back, small):
    chans = x.shape[-1]
    hidden = grad_a.shape[0]
    grad = jax.ShapeDtypeStruct((chans, 4 * hidden), F32)
    pairs = plan.pair_spec(chans, lambda j: (sub, j % 2, j // 2, 0, 0))
    channel = (hidden, plan.rows, plan.width)
    kept = [] if before is None else [before]
    return pl.pallas_call(
        functools.partial(last_kernel, plan.step),
        grid=(plan.blocks,),
        in_specs=[
            pairs,
            pl.BlockSpec((plan.rows, plan.width), lambda j: (sub, j)),
            pl.BlockSpec(channel, lambda j: (0, sub, j)),
            pl.BlockSpec(channel, lambda j: (0, at, j)),
            pl.BlockSpec((plan.rows, chans, plan.width), lambda j: (sub, 0, j)),
        ]
        + [whole(value) for value in small]
        + [HELD for _ in kept],
        out_specs=[pairs, whole(grad)],
        out_shape=[jax.ShapeDtypeStruct(x.shape, BF16), grad],
        scratch_shapes=[plan.scratch(hidden)] * 2,
        input_output_aliases={} if before is None else {5 + len(small): 0},
        compiler_params=params(1),
        cost_estimate=cost(0.2),
        name="last",
    )(x, mask, grad_a, grad_b, gate_back, *small, *kept)


def swap_all(array):
    return lax.all_to_all(array, "tile", split_axis=0, concat_axis=0, tiled=True)


def tile_sum(array, tiles):
    chans, width = array.shape
    parts = swap_all(array.astype(BF16)).reshape(tiles, chans // tiles, width)
    part = jnp.sum(parts.astype(F32), axis=0).astype(BF16)
    spread = jnp.broadcast_to(part[None], (tiles,) + part.shape).reshape(chans, width)
    return swap_all(spread).astype(F32)


def body(
    tiles, x, d, token_mask, ln_in_gain, ln_in_bias, w_ab, w_gate, ln_out_gain, ln_out_bias, w_out
):
    count, crop, chans = x.shape
    hidden = w_out.shape[0]
    plan = Plan(tiles, count, crop)
    me = lax.axis_index("tile")
    side = (me // plan.half).astype(jnp.int32)
    valid = token_mask.astype(F32)
    own_valid = lax.dynamic_slice_in_dim(valid, me * count, count)
    turned_valid = valid.reshape(tiles, plan.subs, plan.rows).transpose(1, 0, 2).reshape(crop)
    mask = own_valid[:, None] * turned_valid[None, :]
    gain, bias = ln_in_gain[:, None], ln_in_bias[:, None]
    w_t = w_ab.T
    w_cat = jnp.concatenate([w_ab, w_gate], axis=1)
    mid = [gain, bias, w_gate.T, ln_out_gain[:, None], ln_out_bias[:, None], w_out, w_out.T]
    x, d = plan.view(x), plan.view(d)
    owned = lambda array: array.reshape(plan.half, hidden // plan.half, *array.shape[1:])
    joined = lambda array: array.reshape(hidden, *array.shape[2:])
    every = range(plan.subs)

    plan_cut = plan.cut
    two = plan.subs == 2
    cut_b, back_a = plan_cut(4, 2, 2), plan_cut(4, 4)
    small = [gain, bias, w_t, w_cat]

    def middle(at, before, ready, product):
        table = jnp.stack([jnp.stack([half, jnp.int32(sub)]) for half, sub in at])
        g, kept, *local = make_middle(plan, table, before, ready, x, d, product, mid)
        return g, kept, jnp.concatenate(local[::-1], axis=1)

    def product_of(b):
        return plan.swap(joined(make_product(plan, own_a, b)))

    held, factor_b0 = make_factors(plan, 0, (), x, mask, gain, bias, w_t)
    own_b0 = owned(plan.swap(factor_b0))
    if two:
        (held,) = make_factors(plan, 1, (held,), x, mask, gain, bias, w_t)
    other_0 = plan.exchange(own_b0)
    own_ab = owned(plan.swap(after(held, own_b0)))
    own_a, own_b, got_b = [(own_ab, 0)], [(own_b0, 0)], []
    if two:
        own_a, own_b = [(own_ab, 2), (own_ab, 0)], [(own_b0, 0), (own_ab, 1)]
        sent = plan.pieces(own_ab[:, :, plan.rows : 2 * plan.rows], cut_b)
        got_b = [plan.exchange(sent[0])]
    b_first = [(other_0, 0)] + own_b
    product = product_of(b_first)
    if two:
        got_b.append(plan.exchange(after(sent[1], product)))
        got_b.append(plan.exchange(sent[2]))
    places = [(1 - side, 0)] + [(side, sub) for sub in every]
    grad, kept, local_mid = middle(places, (), got_b[:1], product)
    owner_g = [owned(plan.swap(after(grad, *got_b[1:2])))]
    parts = make_grad_b(plan, owner_g[0], own_a, back_a + [plan.half] * plan.subs)
    grad_b0, grad_b_own = parts[: len(back_a)], parts[len(back_a) :]
    back_0 = [plan.exchange(piece) for piece in grad_b0]
    if two:
        b_second = [(after(got_b[0], grad_b0[0]), 0)] + [(piece, 0) for piece in got_b[1:]]
        product = product_of(b_second)
        b_first = b_first + b_second
        grad, kept, local_1 = middle([(1 - side, 1)], (kept,), (), product)
        local_mid += local_1
        owner_g.append(owned(plan.swap(after(grad, back_0[0]))))
        (grad_b1,) = make_grad_b(plan, owner_g[1], own_a, [plan.half])
        back_1 = plan.exchange(grad_b1)
        back_0[1] = after(back_0[1], grad_b1)
    grads = plan.swap(joined(make_grad_a(plan, owner_g, b_first, grad_b_own[0], back_0)))
    pair_grad, local_ab = make_last(
        plan, 0, None, x, mask, grads, grads, plan.subs, kept, small
    )
    if two:
        grad_b = plan.swap(
            joined((grad_b_own[1].astype(F32) + back_1.astype(F32)).astype(BF16))
        )
        pair_grad, local = make_last(
            plan, 1, pair_grad, x, mask, grads, grad_b, 0, kept, small
        )
        local_ab += local
    total = tile_sum(jnp.concatenate([local_ab, local_mid], axis=1), tiles) / crop
    wide = 4 * hidden
    return (
        pair_grad.reshape(count, crop, chans),
        total[:, :wide],
        total[:, wide : wide + chans],
        total[:, wide + chans :],
    )


def solution(mesh):
    pairs = P(("crops", "tile"), None, None)
    return jax.shard_map(
        functools.partial(body, mesh.shape["tile"]),
        mesh=mesh,
        in_specs=(pairs, pairs, P("crops")) + (P(),) * 7,
        out_specs=(pairs,) + (P("crops", None),) * 3,
        check_vma=False,
    )
```

```python
import functools

import jax
import jax.numpy as jnp
from jax import lax
from jax.experimental import pallas as pl
from jax.experimental.pallas import tpu as pltpu
from jax.sharding import PartitionSpec as P

HELD = pl.BlockSpec(memory_space=pl.ANY)
EPS = 1e-05
CHANS = 4
F32 = jnp.float32
BF16 = jnp.bfloat16
NN = (((1,), (0,)), ((), ()))
NT = (((1,), (1,)), ((), ()))
TN = (((0,), (0,)), ((), ()))


def params(steps):
    return pltpu.CompilerParams(
        dimension_semantics=("arbitrary",) * steps, vmem_limit_bytes=50 * 1024 * 1024
    )


def cost(micros):
    return pl.CostEstimate(
        flops=int(micros * 1.0e9), bytes_accessed=int(micros * 3.0e6), transcendentals=0
    )


def dot(left, right, form=NN):
    return lax.dot_general(left, right, form, preferred_element_type=F32)


def sigmoid(value):
    return 0.5 * jnp.tanh(0.5 * value) + 0.5


def col_mean(value):
    return jnp.mean(value, axis=0, keepdims=True)


def stats(value):
    centered = value - col_mean(value)
    inv_std = lax.rsqrt(col_mean(centered * centered) + EPS)
    return centered * inv_std, inv_std


def norm_back(upstream, scaled, inv_std):
    return inv_std * (upstream - col_mean(upstream) - scaled * col_mean(upstream * scaled))


def turned(ref, row, count):
    block = ref[pl.ds(row, count)]
    return block.reshape(-1, block.shape[-1]).astype(F32).T


def lane_parts(scratch, count):
    return [(at, lane) for at in range(count) for lane in range(scratch.shape[0])]


def store_rows(scratch, row, count, rows, value):
    hidden = value.shape[0]
    for part, (at, lane) in enumerate(lane_parts(scratch, count)):
        scratch[lane, pl.ds(row + at, hidden, stride=rows), :] = value[:, part * 128 : (part + 1) * 128]


def load_rows(scratch, row, count, rows):
    hidden = scratch.shape[1] // rows
    return jnp.concatenate(
        [
            scratch[lane, pl.ds(row + at, hidden, stride=rows), :]
            for at, lane in lane_parts(scratch, count)
        ],
        axis=1,
    )


def gather_out(scratch, out_ref, rows, at=0):
    hidden = out_ref.shape[0]
    for lane in range(scratch.shape[0]):
        out_ref[:, at : at + rows, lane * 128 : (lane + 1) * 128] = (
            scratch[lane].reshape(hidden, rows, 128).astype(BF16)
        )


def spread_in(in_ref, scratch):
    hidden, rows, cols = in_ref.shape
    for lane in range(scratch.shape[0]):
        scratch[lane] = (
            in_ref[:, :, lane * 128 : (lane + 1) * 128].astype(F32).reshape(hidden * rows, 128)
        )


def flat_rows(ref, row, count):
    return jnp.concatenate([ref[pl.ds(row + at, 1), :] for at in range(count)], axis=1)


def whole(array):
    return pl.BlockSpec(array.shape, lambda *_: (0,) * array.ndim)


class Plan:
    def __init__(self, tiles, count, crop):
        self.tiles, self.count, self.crop = tiles, count, crop
        self.half = tiles // 2
        self.subs = 2 if count % 32 == 0 else 1
        self.rows = count // self.subs
        self.width = self.half * self.rows
        self.blocks = crop // self.width
        self.step = max(1, 512 // self.width)
        self.groups = [
            [side * self.half + at for at in range(self.half)] for side in range(2)
        ]
        self.partner = [(at, (at + self.half) % tiles) for at in range(tiles)]

    def view(self, array):
        return array.reshape(self.count, self.tiles, self.subs, self.rows, array.shape[-1])

    def pair_spec(self, chans, index):
        return pl.BlockSpec((self.rows, self.half, 1, self.rows, chans), index)

    def scratch(self, hidden):
        return pltpu.VMEM((self.width // 128, self.rows * hidden, 128), F32)

    def swap(self, array):
        return lax.all_to_all(
            array, "tile", split_axis=0, concat_axis=0, axis_index_groups=self.groups, tiled=True
        )

    def cut(self, *eighths):
        return [max(1, self.half * share // 8) for share in eighths]

    def pieces(self, array, counts):
        ends = [sum(counts[: at + 1]) for at in range(len(counts))]
        return [array[end - size : end] for size, end in zip(counts, ends)]

    def exchange(self, array):
        return lax.ppermute(array, "tile", self.partner)


def after_kernel(*refs):
    del refs


def after(value, *others):
    return pl.pallas_call(
        after_kernel,
        in_specs=[HELD] * (1 + len(others)),
        out_specs=HELD,
        out_shape=jax.ShapeDtypeStruct(value.shape, value.dtype),
        input_output_aliases={0: 0},
        compiler_params=params(0),
        cost_estimate=cost(0.1),
        name="after",
    )(value, *others)


def factors_kernel(step, joint, x_ref, mask_ref, gain_ref, bias_ref, w_ref, *refs):
    sa_ref, sb_ref = refs[-2:]
    rows = x_ref.shape[0]
    hidden = w_ref.shape[0] // 4

    @pl.loop(0, rows // step, unroll=min(4, rows // step))
    def _(turn):
        row = pl.multiple_of(turn * step, step)
        z_hat, _ = stats(turned(x_ref, row, step))
        normed = (z_hat * gain_ref[...] + bias_ref[...]).astype(BF16)
        mask = flat_rows(mask_ref, row, step)
        proj = dot(w_ref[...], normed)
        value_a, gate_a = proj[:hidden], proj[hidden : 2 * hidden]
        value_b, gate_b = proj[2 * hidden : 3 * hidden], proj[3 * hidden :]
        store_rows(sb_ref, row, step, rows, mask * sigmoid(gate_b) * value_b)
        store_rows(sa_ref, row, step, rows, mask * sigmoid(gate_a) * value_a)

    if joint:
        gather_out(sa_ref, refs[-3], rows)
        gather_out(sb_ref, refs[-3], rows, rows)
    else:
        gather_out(sa_ref, refs[-4], rows)
        gather_out(sb_ref, refs[-3], rows)


def make_factors(plan, sub, before, x, mask, gain, bias, w_t):
    chans = x.shape[-1]
    hidden = w_t.shape[0] // 4
    block = (hidden, plan.rows, plan.width)
    held = plan.rows * (3 if plan.subs == 2 else 1)
    out_specs = [
        pl.BlockSpec(block, lambda j: (0, 2 * (plan.subs - 1), j)),
        pl.BlockSpec(block, lambda j: (0, 0, j)),
    ]
    out_shape = [
        jax.ShapeDtypeStruct((hidden, held, plan.crop), BF16),
        jax.ShapeDtypeStruct((hidden, plan.rows, plan.crop), BF16),
    ]
    if before:
        out_specs = [pl.BlockSpec((hidden, 2 * plan.rows, plan.width), lambda j: (0, 0, j))]
        out_shape = out_shape[:1]
    return pl.pallas_call(
        functools.partial(factors_kernel, plan.step, bool(before)),
        grid=(plan.blocks,),
        in_specs=[
            plan.pair_spec(chans, lambda j: (sub, j % 2, j // 2, 0, 0)),
            pl.BlockSpec((plan.rows, plan.width), lambda j: (sub, j)),
            whole(gain),
            whole(bias),
            whole(w_t),
        ]
        + [HELD for _ in before],
        out_specs=out_specs,
        out_shape=out_shape,
        input_output_aliases={5: 0} if before else {},
        scratch_shapes=[plan.scratch(hidden)] * 2,
        compiler_params=params(1),
        cost_estimate=cost(0.2),
        name="factors",
    )(x, mask, gain, bias, w_t, *before)


def matrix(refs, chan):
    parts = [ref[:, chan].reshape(-1, ref.shape[-1]) for ref in refs]
    return jnp.concatenate(parts, axis=0) if len(parts) > 1 else parts[0]


def by_sub(ref, chan, subs):
    rows = ref.shape[2] // subs
    parts = [
        ref[:, chan, sub * rows : (sub + 1) * rows, :].reshape(-1, ref.shape[3])
        for sub in range(subs)
    ]
    return jnp.concatenate(parts, axis=0) if subs > 1 else parts[0]


def to_subs(ref, chan, value, subs, rows):
    part = value.shape[0] // subs
    for sub in range(subs):
        ref[:, chan, sub * rows : (sub + 1) * rows, :] = value[
            sub * part : (sub + 1) * part
        ].astype(BF16).reshape(ref.shape[0], rows, ref.shape[3])


def own_spec(array):
    src, _, rows, cols = array.shape
    return pl.BlockSpec((src, CHANS, rows, cols), lambda h: (0, h, 0, 0))


def view_spec(plan, view):
    array, at = view
    return pl.BlockSpec((array.shape[0], CHANS, plan.rows, array.shape[3]), lambda h: (0, h, at, 0))


def arrays(views):
    return [array for array, _ in views]


def product_kernel(subs, rows, *refs):
    a, b, p_ref = refs[:subs], refs[subs:-1], refs[-1]
    for chan in range(CHANS):
        to_subs(p_ref, chan, dot(matrix(a, chan), matrix(b, chan), NT), subs, rows)


def make_product(plan, a, b):
    tiles, chans = a[0][0].shape[:2]
    cols = sum(array.shape[0] for array in arrays(b)) * plan.rows
    out = jax.ShapeDtypeStruct((tiles, chans, plan.count, cols), BF16)
    return pl.pallas_call(
        functools.partial(product_kernel, plan.subs, plan.rows),
        grid=(chans // CHANS,),
        in_specs=[view_spec(plan, view) for view in (*a, *b)],
        out_specs=own_spec(out),
        out_shape=out,
        compiler_params=params(1),
        cost_estimate=cost(0.2),
        name="product",
    )(*arrays(a), *arrays(b))


def grad_b_kernel(subs, g_ref, *refs):
    a, outs = refs[:subs], refs[subs:]
    for chan in range(CHANS):
        grad = dot(by_sub(g_ref, chan, subs), matrix(a, chan), TN).astype(BF16)
        at = 0
        for out in outs:
            size = out.shape[0] * out.shape[2]
            out[:, chan] = grad[at : at + size].reshape(out.shape[0], *out.shape[2:])
            at += size


def make_grad_b(plan, g, a, tiles):
    outs = [
        jax.ShapeDtypeStruct((count, g.shape[1], plan.rows, plan.crop), BF16) for count in tiles
    ]
    return pl.pallas_call(
        functools.partial(grad_b_kernel, plan.subs),
        grid=(g.shape[1] // CHANS,),
        in_specs=[own_spec(g)] + [view_spec(plan, view) for view in a],
        out_specs=[own_spec(value) for value in outs],
        out_shape=outs,
        compiler_params=params(1),
        cost_estimate=cost(0.2),
        name="grad_b",
    )(g, *arrays(a))


def grad_a_kernel(subs, rows, counts, *refs):
    g, b = refs[: counts[0]], refs[counts[0] : counts[0] + counts[1]]
    own, back, out = refs[counts[0] + counts[1]], refs[counts[0] + counts[1] + 1 : -1], refs[-1]
    for chan in range(CHANS):
        left = jnp.concatenate([by_sub(ref, chan, subs) for ref in g], axis=1)
        to_subs(out, chan, dot(left, matrix(b, chan)), subs, rows)
        at = 0
        for piece in back:
            end = at + piece.shape[0]
            added = own[at:end, chan].astype(F32) + piece[:, chan].astype(F32)
            out[at:end, chan, subs * rows :, :] = added.astype(BF16)
            at = end


def make_grad_a(plan, g, b, own, back):
    chans = own.shape[1]
    out = jax.ShapeDtypeStruct((plan.half, chans, plan.count + plan.rows, plan.crop), BF16)
    return pl.pallas_call(
        functools.partial(grad_a_kernel, plan.subs, plan.rows, (len(g), len(b))),
        grid=(chans // CHANS,),
        in_specs=[own_spec(value) for value in g]
        + [view_spec(plan, view) for view in b]
        + [own_spec(value) for value in (own, *back)],
        out_specs=own_spec(out),
        out_shape=out,
        compiler_params=params(1),
        cost_estimate=cost(0.2),
        name="grad_a",
    )(*g, *arrays(b), own, *back)


def middle_kernel(
    step, _, x_ref, d_ref, p_ref, gain_ref, bias_ref, wg_ref, og_ref, ob_ref, wo_ref, wot_ref, *refs
):
    g_ref, gb_ref, gwo_ref, gwg_ref, s_ref = refs[-5:]
    rows = x_ref.shape[0]
    width = gb_ref.shape[-1]

    @pl.when((pl.program_id(0) == 0) & (pl.program_id(1) == 0))
    def _():
        gwo_ref[...] = jnp.zeros_like(gwo_ref)
        gwg_ref[...] = jnp.zeros_like(gwg_ref)

    spread_in(p_ref, s_ref)

    @pl.loop(0, rows // step, unroll=min(4, rows // step))
    def _(turn):
        row = pl.multiple_of(turn * step, step)
        z_hat, _ = stats(turned(x_ref, row, step))
        normed = (z_hat * gain_ref[...] + bias_ref[...]).astype(BF16)
        gate = sigmoid(dot(wg_ref[...], normed))
        x_hat, inv_std = stats(load_rows(s_ref, row, step, rows))
        x_norm = (x_hat * og_ref[...] + ob_ref[...]).astype(BF16)
        out_lin = dot(wot_ref[...], x_norm)
        lin = turned(d_ref, row, step) * gate
        grad_lin = lin.astype(BF16)
        gate_back = (lin * out_lin * (1.0 - gate)).astype(BF16)
        upstream = dot(wo_ref[...], grad_lin) * og_ref[...]
        store_rows(s_ref, row, step, rows, norm_back(upstream, x_hat, inv_std))
        for at in range(step):
            gb_ref[row + at] = gate_back[:, at * width : (at + 1) * width]
        gwo_ref[...] += dot(x_norm, grad_lin, NT)
        gwg_ref[...] += dot(normed, gate_back, NT)

    gather_out(s_ref, g_ref, rows)


def make_middle(plan, table, first, before, ready, x, d, p, small):
    chans = x.shape[-1]
    hidden = p.shape[0]
    cut = table.shape[0]
    grads = [jax.ShapeDtypeStruct((hidden, chans), F32), jax.ShapeDtypeStruct((chans, chans), F32)]
    pairs = plan.pair_spec(chans, lambda i, j, at: (i, at[j, 0], at[j, 1], 0, 0))
    channel = (hidden, plan.rows, plan.width)
    kept = [*before, *ready]
    return pl.pallas_call(
        functools.partial(middle_kernel, plan.step),
        grid_spec=pltpu.PrefetchScalarGridSpec(
            num_scalar_prefetch=1,
            grid=(plan.subs, cut),
            in_specs=[pairs, pairs, pl.BlockSpec(channel, lambda i, j, at: (0, i, first + j))]
            + [whole(value) for value in small]
            + [HELD for _ in kept],
            out_specs=[
                pl.BlockSpec(channel, lambda i, j, at: (0, i, j)),
                pl.BlockSpec(
                    (plan.rows, chans, plan.width),
                    lambda i, j, at: (i, 0, at[j, 1] * 2 + at[j, 0]),
                ),
            ]
            + [whole(value) for value in grads],
            scratch_shapes=[plan.scratch(hidden)],
        ),
        out_shape=[
            jax.ShapeDtypeStruct((hidden, plan.count, cut * plan.width), BF16),
            jax.ShapeDtypeStruct((plan.count, chans, plan.crop), BF16),
        ]
        + grads,
        input_output_aliases={4 + len(small): 1} if before else {},
        compiler_params=params(2),
        cost_estimate=cost(0.2),
        name="middle",
    )(table, x, d, p, *small, *kept)


def last_kernel(
    step, x_ref, mask_ref, ga_ref, gb_ref, gate_ref, gain_ref, bias_ref, wt_ref, wcat_ref, *refs
):
    out_ref, gw_ref, sa_ref, sb_ref = refs[-4:]
    rows = x_ref.shape[0]
    hidden = ga_ref.shape[0]

    @pl.when(pl.program_id(0) == 0)
    def _():
        gw_ref[...] = jnp.zeros_like(gw_ref)

    spread_in(ga_ref, sa_ref)
    spread_in(gb_ref, sb_ref)

    @pl.loop(0, rows // step, unroll=min(4, rows // step))
    def _(turn):
        row = pl.multiple_of(turn * step, step)
        z_hat, inv_in = stats(turned(x_ref, row, step))
        normed = (z_hat * gain_ref[...] + bias_ref[...]).astype(BF16)
        mask = flat_rows(mask_ref, row, step)
        proj = dot(wt_ref[...], normed)
        sides = []
        for side, ref in enumerate((sa_ref, sb_ref)):
            value = proj[2 * side * hidden : (2 * side + 1) * hidden]
            sig = sigmoid(proj[(2 * side + 1) * hidden : (2 * side + 2) * hidden])
            to_value = load_rows(ref, row, step, rows) * mask * sig
            sides += [to_value.astype(BF16), (to_value * value * (1.0 - sig)).astype(BF16)]
        grad_proj = jnp.concatenate(sides, axis=0)
        gate_back = jnp.concatenate([gate_ref[row + at] for at in range(step)], axis=1)
        every = jnp.concatenate([grad_proj, gate_back], axis=0)
        upstream = dot(wcat_ref[...], every) * gain_ref[...]
        grad = norm_back(upstream, z_hat, inv_in).T.astype(BF16)
        out_ref[pl.ds(row, step)] = grad.reshape((step,) + out_ref.shape[1:])
        gw_ref[...] += dot(normed, grad_proj, NT)


def make_last(plan, sub, before, x, mask, grad_a, grad_b, at, gate_back, small):
    chans = x.shape[-1]
    hidden = grad_a.shape[0]
    grad = jax.ShapeDtypeStruct((chans, 4 * hidden), F32)
    pairs = plan.pair_spec(chans, lambda j: (sub, j % 2, j // 2, 0, 0))
    channel = (hidden, plan.rows, plan.width)
    kept = [] if before is None else [before]
    return pl.pallas_call(
        functools.partial(last_kernel, plan.step),
        grid=(plan.blocks,),
        in_specs=[
            pairs,
            pl.BlockSpec((plan.rows, plan.width), lambda j: (sub, j)),
            pl.BlockSpec(channel, lambda j: (0, sub, j)),
            pl.BlockSpec(channel, lambda j: (0, at, j)),
            pl.BlockSpec((plan.rows, chans, plan.width), lambda j: (sub, 0, j)),
        ]
        + [whole(value) for value in small]
        + [HELD for _ in kept],
        out_specs=[pairs, whole(grad)],
        out_shape=[jax.ShapeDtypeStruct(x.shape, BF16), grad],
        scratch_shapes=[plan.scratch(hidden)] * 2,
        input_output_aliases={} if before is None else {5 + len(small): 0},
        compiler_params=params(1),
        cost_estimate=cost(0.2),
        name="last",
    )(x, mask, grad_a, grad_b, gate_back, *small, *kept)


def swap_all(array):
    return lax.all_to_all(array, "tile", split_axis=0, concat_axis=0, tiled=True)


def tile_sum(array, tiles):
    chans, width = array.shape
    parts = swap_all(array.astype(BF16)).reshape(tiles, chans // tiles, width)
    part = jnp.sum(parts.astype(F32), axis=0).astype(BF16)
    spread = jnp.broadcast_to(part[None], (tiles,) + part.shape).reshape(chans, width)
    return swap_all(spread).astype(F32)


def body(
    tiles, x, d, token_mask, ln_in_gain, ln_in_bias, w_ab, w_gate, ln_out_gain, ln_out_bias, w_out
):
    count, crop, chans = x.shape
    hidden = w_out.shape[0]
    plan = Plan(tiles, count, crop)
    me = lax.axis_index("tile")
    side = (me // plan.half).astype(jnp.int32)
    valid = token_mask.astype(F32)
    own_valid = lax.dynamic_slice_in_dim(valid, me * count, count)
    turned_valid = valid.reshape(tiles, plan.subs, plan.rows).transpose(1, 0, 2).reshape(crop)
    mask = own_valid[:, None] * turned_valid[None, :]
    gain, bias = ln_in_gain[:, None], ln_in_bias[:, None]
    w_t = w_ab.T
    w_cat = jnp.concatenate([w_ab, w_gate], axis=1)
    mid = [gain, bias, w_gate.T, ln_out_gain[:, None], ln_out_bias[:, None], w_out, w_out.T]
    x, d = plan.view(x), plan.view(d)
    owned = lambda array: array.reshape(plan.half, hidden // plan.half, *array.shape[1:])
    joined = lambda array: array.reshape(hidden, *array.shape[2:])
    every = range(plan.subs)

    plan_cut = plan.cut
    two = plan.subs == 2
    cut_b, back_a = plan_cut(4, 2, 2), plan_cut(3, 3, 2)
    small = [gain, bias, w_t, w_cat]

    def middle(at, first, before, ready, product):
        table = jnp.stack([jnp.stack([half, jnp.int32(sub)]) for half, sub in at])
        g, kept, *local = make_middle(plan, table, first, before, ready, x, d, product, mid)
        return g, kept, jnp.concatenate(local[::-1], axis=1)

    def product_of(b):
        return plan.swap(joined(make_product(plan, own_a, b)))

    held, factor_b0 = make_factors(plan, 0, (), x, mask, gain, bias, w_t)
    own_b0 = owned(plan.swap(factor_b0))
    if two:
        (held,) = make_factors(plan, 1, (held,), x, mask, gain, bias, w_t)
    other_0 = plan.exchange(own_b0)
    own_ab = owned(plan.swap(after(held, own_b0)))
    own_a, own_b, got_b = [(own_ab, 0)], [(own_b0, 0)], []
    if two:
        own_a, own_b = [(own_ab, 2), (own_ab, 0)], [(own_b0, 0), (own_ab, 1)]
        sent = plan.pieces(own_ab[:, :, plan.rows : 2 * plan.rows], cut_b)
        got_b = [plan.exchange(sent[0])]
    b_first = [(other_0, 0)] + own_b
    product = product_of(b_first)
    if two:
        got_b.append(plan.exchange(after(sent[1], product)))
        got_b.append(plan.exchange(sent[2]))
    grad, kept, local_mid = middle([(1 - side, 0)], 0, (), got_b[:1], product)
    owner_g = [owned(plan.swap(grad))]
    grad, kept, local = middle([(side, sub) for sub in every], 1, (kept,), (), product)
    local_mid += local
    grad_b0 = make_grad_b(plan, owner_g[0], own_a, back_a)
    back_0 = [plan.exchange(piece) for piece in grad_b0]
    waits = (owner_g[0], grad_b0[0], *got_b[1:2])
    owner_g.append(owned(plan.swap(after(grad, *waits))))
    grad_b_own = make_grad_b(plan, owner_g[1], own_a, [plan.half] * plan.subs)
    if two:
        b_second = [(piece, 0) for piece in got_b]
        b_first = b_first + b_second
        product = joined(make_product(plan, own_a, b_second))
        product = plan.swap(after(product, owner_g[1], back_0[0]))
        grad, kept, local = middle([(1 - side, 1)], 0, (kept,), grad_b_own[:1], product)
        local_mid += local
        owner_g.append(owned(plan.swap(after(grad, back_0[1]))))
        (grad_b1,) = make_grad_b(plan, owner_g[2], own_a, [plan.half])
        back_1 = plan.exchange(grad_b1)
        back_0[2] = after(back_0[2], grad_b1)
    grads = plan.swap(joined(make_grad_a(plan, owner_g, b_first, grad_b_own[0], back_0)))
    pair_grad, local_ab = make_last(
        plan, 0, None, x, mask, grads, grads, plan.subs, kept, small
    )
    if two:
        grad_b = plan.swap(
            joined((grad_b_own[1].astype(F32) + back_1.astype(F32)).astype(BF16))
        )
        pair_grad, local = make_last(
            plan, 1, pair_grad, x, mask, grads, grad_b, 0, kept, small
        )
        local_ab += local
    total = tile_sum(jnp.concatenate([local_ab, local_mid], axis=1), tiles) / crop
    wide = 4 * hidden
    return (
        pair_grad.reshape(count, crop, chans),
        total[:, :wide],
        total[:, wide : wide + chans],
        total[:, wide + chans :],
    )


def solution(mesh):
    pairs = P(("crops", "tile"), None, None)
    return jax.shard_map(
        functools.partial(body, mesh.shape["tile"]),
        mesh=mesh,
        in_specs=(pairs, pairs, P("crops")) + (P(),) * 7,
        out_specs=(pairs,) + (P("crops", None),) * 3,
        check_vma=False,
    )
```

```python
import functools

import jax
import jax.numpy as jnp
from jax import lax
from jax.experimental import pallas as pl
from jax.experimental.pallas import tpu as pltpu
from jax.sharding import PartitionSpec as P

HELD = pl.BlockSpec(memory_space=pl.ANY)
EPS = 1e-05
CHANS = 4
F32 = jnp.float32
BF16 = jnp.bfloat16
NN = (((1,), (0,)), ((), ()))
NT = (((1,), (1,)), ((), ()))
TN = (((0,), (0,)), ((), ()))


def params(steps):
    return pltpu.CompilerParams(
        dimension_semantics=("arbitrary",) * steps, vmem_limit_bytes=50 * 1024 * 1024
    )


def cost(micros):
    return pl.CostEstimate(
        flops=int(micros * 1.0e9), bytes_accessed=int(micros * 3.0e6), transcendentals=0
    )


def dot(left, right, form=NN):
    return lax.dot_general(left, right, form, preferred_element_type=F32)


def sigmoid(value):
    return 0.5 * jnp.tanh(0.5 * value) + 0.5


def col_mean(value):
    return jnp.mean(value, axis=0, keepdims=True)


def stats(value):
    centered = value - col_mean(value)
    inv_std = lax.rsqrt(col_mean(centered * centered) + EPS)
    return centered * inv_std, inv_std


def norm_back(upstream, scaled, inv_std):
    return inv_std * (upstream - col_mean(upstream) - scaled * col_mean(upstream * scaled))


def turned(ref, row, count):
    block = ref[pl.ds(row, count)]
    return block.reshape(-1, block.shape[-1]).astype(F32).T


def lane_parts(scratch, count):
    return [(at, lane) for at in range(count) for lane in range(scratch.shape[0])]


def store_rows(scratch, row, count, rows, value):
    hidden = value.shape[0]
    for part, (at, lane) in enumerate(lane_parts(scratch, count)):
        scratch[lane, pl.ds(row + at, hidden, stride=rows), :] = value[:, part * 128 : (part + 1) * 128]


def load_rows(scratch, row, count, rows):
    hidden = scratch.shape[1] // rows
    return jnp.concatenate(
        [
            scratch[lane, pl.ds(row + at, hidden, stride=rows), :]
            for at, lane in lane_parts(scratch, count)
        ],
        axis=1,
    )


def gather_out(scratch, out_ref, rows, at=0):
    hidden = out_ref.shape[0]
    for lane in range(scratch.shape[0]):
        out_ref[:, at : at + rows, lane * 128 : (lane + 1) * 128] = (
            scratch[lane].reshape(hidden, rows, 128).astype(BF16)
        )


def spread_in(in_ref, scratch):
    hidden, rows, cols = in_ref.shape
    for lane in range(scratch.shape[0]):
        scratch[lane] = (
            in_ref[:, :, lane * 128 : (lane + 1) * 128].astype(F32).reshape(hidden * rows, 128)
        )


def flat_rows(ref, row, count):
    return jnp.concatenate([ref[pl.ds(row + at, 1), :] for at in range(count)], axis=1)


def whole(array):
    return pl.BlockSpec(array.shape, lambda *_: (0,) * array.ndim)


class Plan:
    def __init__(self, tiles, count, crop):
        self.tiles, self.count, self.crop = tiles, count, crop
        self.half = tiles // 2
        self.subs = 2 if count % 32 == 0 else 1
        self.rows = count // self.subs
        self.width = self.half * self.rows
        self.blocks = crop // self.width
        self.step = max(1, 512 // self.width)
        self.groups = [
            [side * self.half + at for at in range(self.half)] for side in range(2)
        ]
        self.partner = [(at, (at + self.half) % tiles) for at in range(tiles)]

    def view(self, array):
        return array.reshape(self.count, self.tiles, self.subs, self.rows, array.shape[-1])

    def pair_spec(self, chans, index):
        return pl.BlockSpec((self.rows, self.half, 1, self.rows, chans), index)

    def scratch(self, hidden):
        return pltpu.VMEM((self.width // 128, self.rows * hidden, 128), F32)

    def swap(self, array):
        return lax.all_to_all(
            array, "tile", split_axis=0, concat_axis=0, axis_index_groups=self.groups, tiled=True
        )

    def cut(self, *eighths):
        return [max(1, self.half * share // 8) for share in eighths]

    def pieces(self, array, counts):
        ends = [sum(counts[: at + 1]) for at in range(len(counts))]
        return [array[end - size : end] for size, end in zip(counts, ends)]

    def exchange(self, array):
        return lax.ppermute(array, "tile", self.partner)


def after_kernel(*refs):
    del refs


def after(value, *others):
    return pl.pallas_call(
        after_kernel,
        in_specs=[HELD] * (1 + len(others)),
        out_specs=HELD,
        out_shape=jax.ShapeDtypeStruct(value.shape, value.dtype),
        input_output_aliases={0: 0},
        compiler_params=params(0),
        cost_estimate=cost(0.1),
        name="after",
    )(value, *others)


def factors_kernel(step, joint, x_ref, mask_ref, gain_ref, bias_ref, w_ref, *refs):
    sa_ref, sb_ref = refs[-2:]
    rows = x_ref.shape[0]
    hidden = w_ref.shape[0] // 4

    @pl.loop(0, rows // step, unroll=min(4, rows // step))
    def _(turn):
        row = pl.multiple_of(turn * step, step)
        z_hat, _ = stats(turned(x_ref, row, step))
        normed = (z_hat * gain_ref[...] + bias_ref[...]).astype(BF16)
        mask = flat_rows(mask_ref, row, step)
        proj = dot(w_ref[...], normed)
        value_a, gate_a = proj[:hidden], proj[hidden : 2 * hidden]
        value_b, gate_b = proj[2 * hidden : 3 * hidden], proj[3 * hidden :]
        store_rows(sb_ref, row, step, rows, mask * sigmoid(gate_b) * value_b)
        store_rows(sa_ref, row, step, rows, mask * sigmoid(gate_a) * value_a)

    if joint:
        gather_out(sa_ref, refs[-3], rows)
        gather_out(sb_ref, refs[-3], rows, rows)
    else:
        gather_out(sa_ref, refs[-4], rows)
        gather_out(sb_ref, refs[-3], rows)


def make_factors(plan, sub, before, x, mask, gain, bias, w_t):
    chans = x.shape[-1]
    hidden = w_t.shape[0] // 4
    block = (hidden, plan.rows, plan.width)
    held = plan.rows * (3 if plan.subs == 2 else 1)
    out_specs = [
        pl.BlockSpec(block, lambda j: (0, 2 * (plan.subs - 1), j)),
        pl.BlockSpec(block, lambda j: (0, 0, j)),
    ]
    out_shape = [
        jax.ShapeDtypeStruct((hidden, held, plan.crop), BF16),
        jax.ShapeDtypeStruct((hidden, plan.rows, plan.crop), BF16),
    ]
    if before:
        out_specs = [pl.BlockSpec((hidden, 2 * plan.rows, plan.width), lambda j: (0, 0, j))]
        out_shape = out_shape[:1]
    return pl.pallas_call(
        functools.partial(factors_kernel, plan.step, bool(before)),
        grid=(plan.blocks,),
        in_specs=[
            plan.pair_spec(chans, lambda j: (sub, j % 2, j // 2, 0, 0)),
            pl.BlockSpec((plan.rows, plan.width), lambda j: (sub, j)),
            whole(gain),
            whole(bias),
            whole(w_t),
        ]
        + [HELD for _ in before],
        out_specs=out_specs,
        out_shape=out_shape,
        input_output_aliases={5: 0} if before else {},
        scratch_shapes=[plan.scratch(hidden)] * 2,
        compiler_params=params(1),
        cost_estimate=cost(0.2),
        name="factors",
    )(x, mask, gain, bias, w_t, *before)


def matrix(refs, chan):
    parts = [ref[:, chan].reshape(-1, ref.shape[-1]) for ref in refs]
    return jnp.concatenate(parts, axis=0) if len(parts) > 1 else parts[0]


def by_sub(ref, chan, subs):
    rows = ref.shape[2] // subs
    parts = [
        ref[:, chan, sub * rows : (sub + 1) * rows, :].reshape(-1, ref.shape[3])
        for sub in range(subs)
    ]
    return jnp.concatenate(parts, axis=0) if subs > 1 else parts[0]


def to_subs(ref, chan, value, subs, rows):
    part = value.shape[0] // subs
    for sub in range(subs):
        ref[:, chan, sub * rows : (sub + 1) * rows, :] = value[
            sub * part : (sub + 1) * part
        ].astype(BF16).reshape(ref.shape[0], rows, ref.shape[3])


def own_spec(array):
    src, _, rows, cols = array.shape
    return pl.BlockSpec((src, CHANS, rows, cols), lambda h: (0, h, 0, 0))


def view_spec(plan, view):
    array, at = view
    return pl.BlockSpec((array.shape[0], CHANS, plan.rows, array.shape[3]), lambda h: (0, h, at, 0))


def arrays(views):
    return [array for array, _ in views]


def product_kernel(subs, rows, *refs):
    a, b, p_ref = refs[:subs], refs[subs:-1], refs[-1]
    for chan in range(CHANS):
        to_subs(p_ref, chan, dot(matrix(a, chan), matrix(b, chan), NT), subs, rows)


def make_product(plan, a, b):
    tiles, chans = a[0][0].shape[:2]
    cols = sum(array.shape[0] for array in arrays(b)) * plan.rows
    out = jax.ShapeDtypeStruct((tiles, chans, plan.count, cols), BF16)
    return pl.pallas_call(
        functools.partial(product_kernel, plan.subs, plan.rows),
        grid=(chans // CHANS,),
        in_specs=[view_spec(plan, view) for view in (*a, *b)],
        out_specs=own_spec(out),
        out_shape=out,
        compiler_params=params(1),
        cost_estimate=cost(0.2),
        name="product",
    )(*arrays(a), *arrays(b))


def grad_b_kernel(subs, g_ref, *refs):
    a, outs = refs[:subs], refs[subs:]
    for chan in range(CHANS):
        grad = dot(by_sub(g_ref, chan, subs), matrix(a, chan), TN).astype(BF16)
        at = 0
        for out in outs:
            size = out.shape[0] * out.shape[2]
            out[:, chan] = grad[at : at + size].reshape(out.shape[0], *out.shape[2:])
            at += size


def make_grad_b(plan, g, a, tiles):
    outs = [
        jax.ShapeDtypeStruct((count, g.shape[1], plan.rows, plan.crop), BF16) for count in tiles
    ]
    return pl.pallas_call(
        functools.partial(grad_b_kernel, plan.subs),
        grid=(g.shape[1] // CHANS,),
        in_specs=[own_spec(g)] + [view_spec(plan, view) for view in a],
        out_specs=[own_spec(value) for value in outs],
        out_shape=outs,
        compiler_params=params(1),
        cost_estimate=cost(0.2),
        name="grad_b",
    )(g, *arrays(a))


def grad_a_kernel(subs, rows, counts, *refs):
    g, b = refs[: counts[0]], refs[counts[0] : counts[0] + counts[1]]
    own, back, out = refs[counts[0] + counts[1]], refs[counts[0] + counts[1] + 1 : -1], refs[-1]
    for chan in range(CHANS):
        left = jnp.concatenate([by_sub(ref, chan, subs) for ref in g], axis=1)
        to_subs(out, chan, dot(left, matrix(b, chan)), subs, rows)
        at = 0
        for piece in back:
            end = at + piece.shape[0]
            added = own[at:end, chan].astype(F32) + piece[:, chan].astype(F32)
            out[at:end, chan, subs * rows :, :] = added.astype(BF16)
            at = end


def make_grad_a(plan, g, b, own, back):
    chans = own.shape[1]
    out = jax.ShapeDtypeStruct((plan.half, chans, plan.count + plan.rows, plan.crop), BF16)
    return pl.pallas_call(
        functools.partial(grad_a_kernel, plan.subs, plan.rows, (len(g), len(b))),
        grid=(chans // CHANS,),
        in_specs=[own_spec(value) for value in g]
        + [view_spec(plan, view) for view in b]
        + [own_spec(value) for value in (own, *back)],
        out_specs=own_spec(out),
        out_shape=out,
        compiler_params=params(1),
        cost_estimate=cost(0.2),
        name="grad_a",
    )(*g, *arrays(b), own, *back)


def middle_kernel(
    step, _, x_ref, d_ref, p_ref, gain_ref, bias_ref, wg_ref, og_ref, ob_ref, wo_ref, wot_ref, *refs
):
    g_ref, gb_ref, gwo_ref, gwg_ref, s_ref = refs[-5:]
    rows = x_ref.shape[0]
    width = gb_ref.shape[-1]

    @pl.when((pl.program_id(0) == 0) & (pl.program_id(1) == 0))
    def _():
        gwo_ref[...] = jnp.zeros_like(gwo_ref)
        gwg_ref[...] = jnp.zeros_like(gwg_ref)

    spread_in(p_ref, s_ref)

    @pl.loop(0, rows // step, unroll=min(4, rows // step))
    def _(turn):
        row = pl.multiple_of(turn * step, step)
        z_hat, _ = stats(turned(x_ref, row, step))
        normed = (z_hat * gain_ref[...] + bias_ref[...]).astype(BF16)
        gate = sigmoid(dot(wg_ref[...], normed))
        x_hat, inv_std = stats(load_rows(s_ref, row, step, rows))
        x_norm = (x_hat * og_ref[...] + ob_ref[...]).astype(BF16)
        out_lin = dot(wot_ref[...], x_norm)
        lin = turned(d_ref, row, step) * gate
        grad_lin = lin.astype(BF16)
        gate_back = (lin * out_lin * (1.0 - gate)).astype(BF16)
        upstream = dot(wo_ref[...], grad_lin) * og_ref[...]
        store_rows(s_ref, row, step, rows, norm_back(upstream, x_hat, inv_std))
        for at in range(step):
            gb_ref[row + at] = gate_back[:, at * width : (at + 1) * width]
        gwo_ref[...] += dot(x_norm, grad_lin, NT)
        gwg_ref[...] += dot(normed, gate_back, NT)

    gather_out(s_ref, g_ref, rows)


def make_middle(plan, table, first, before, ready, x, d, p, small):
    chans = x.shape[-1]
    hidden = p.shape[0]
    cut = table.shape[0]
    grads = [jax.ShapeDtypeStruct((hidden, chans), F32), jax.ShapeDtypeStruct((chans, chans), F32)]
    pairs = plan.pair_spec(chans, lambda i, j, at: (i, at[j, 0], at[j, 1], 0, 0))
    channel = (hidden, plan.rows, plan.width)
    kept = [*before, *ready]
    return pl.pallas_call(
        functools.partial(middle_kernel, plan.step),
        grid_spec=pltpu.PrefetchScalarGridSpec(
            num_scalar_prefetch=1,
            grid=(plan.subs, cut),
            in_specs=[pairs, pairs, pl.BlockSpec(channel, lambda i, j, at: (0, i, first + j))]
            + [whole(value) for value in small]
            + [HELD for _ in kept],
            out_specs=[
                pl.BlockSpec(channel, lambda i, j, at: (0, i, j)),
                pl.BlockSpec(
                    (plan.rows, chans, plan.width),
                    lambda i, j, at: (i, 0, at[j, 1] * 2 + at[j, 0]),
                ),
            ]
            + [whole(value) for value in grads],
            scratch_shapes=[plan.scratch(hidden)],
        ),
        out_shape=[
            jax.ShapeDtypeStruct((hidden, plan.count, cut * plan.width), BF16),
            jax.ShapeDtypeStruct((plan.count, chans, plan.crop), BF16),
        ]
        + grads,
        input_output_aliases={4 + len(small): 1} if before else {},
        compiler_params=params(2),
        cost_estimate=cost(0.2),
        name="middle",
    )(table, x, d, p, *small, *kept)


def last_kernel(step, mode, *refs):
    sides, gated, based, out_kind, summed = MODES[mode]
    scratches, rest = refs[-len(sides) :], iter(refs[: -len(sides)])
    x_ref, mask_ref = next(rest), next(rest)
    grads = [next(rest) for _ in sides]
    gate_ref = next(rest) if gated else None
    base_ref = next(rest) if based else None
    gain_ref, bias_ref, wt_ref, wcat_ref, *outs = rest
    gw_ref = outs[-1]
    out_ref = outs[-1 - summed] if out_kind else None
    rows, _, _, _, _ = x_ref.shape
    hidden = grads[0].shape[0]
    width = mask_ref.shape[1]

    if summed:

        @pl.when(pl.program_id(0) == 0)
        def _():
            gw_ref[...] = jnp.zeros_like(gw_ref)

    for ref, scratch in zip(grads, scratches):
        spread_in(ref, scratch)

    @pl.loop(0, rows // step, unroll=min(4, rows // step))
    def _(turn):
        row = pl.multiple_of(turn * step, step)
        z_hat, inv_in = stats(turned(x_ref, row, step))
        normed = (z_hat * gain_ref[...] + bias_ref[...]).astype(BF16)
        mask = flat_rows(mask_ref, row, step)
        proj = dot(wt_ref[...], normed)
        parts = []
        for side, scratch in enumerate(scratches):
            value = proj[2 * side * hidden : (2 * side + 1) * hidden]
            sig = sigmoid(proj[(2 * side + 1) * hidden : (2 * side + 2) * hidden])
            to_value = load_rows(scratch, row, step, rows) * mask * sig
            parts += [to_value.astype(BF16), (to_value * value * (1.0 - sig)).astype(BF16)]
        grad_proj = jnp.concatenate(parts, axis=0)
        if summed:
            gw_ref[...] += dot(normed, grad_proj, NT)
        if out_kind:
            every = grad_proj
            if gated:
                gate_back = jnp.concatenate([gate_ref[row + at] for at in range(step)], axis=1)
                every = jnp.concatenate([grad_proj, gate_back], axis=0)
            upstream = dot(wcat_ref[...], every)
            if based:
                upstream += jnp.concatenate(
                    [base_ref[row + at].astype(F32) for at in range(step)], axis=1
                )
            if out_kind == "pair":
                grad = norm_back(upstream * gain_ref[...], z_hat, inv_in).T.astype(BF16)
                out_ref[pl.ds(row, step)] = grad.reshape((step,) + out_ref.shape[1:])
            else:
                for at in range(step):
                    out_ref[row + at] = upstream[:, at * width : (at + 1) * width].astype(BF16)


MODES = {
    "both": ((0, 1), True, False, "pair", True),
    "a": ((0,), True, False, "base", True),
    "b_sum": ((1,), False, False, "", True),
    "b": ((1,), False, True, "pair", False),
}


def make_last(plan, mode, sub, before, x, mask, grads, extra, small):
    sides, gated, based, out_kind, summed = MODES[mode]
    chans = x.shape[-1]
    hidden = grads[0][0].shape[0]
    grad = jax.ShapeDtypeStruct((chans, 2 * len(sides) * hidden), F32)
    pairs = plan.pair_spec(chans, lambda j: (sub, j % 2, j // 2, 0, 0))
    channel = (hidden, plan.rows, plan.width)
    lines = (plan.rows, chans, plan.width)
    kept = [] if before is None else [before]
    in_specs = [pairs, pl.BlockSpec((plan.rows, plan.width), lambda j: (sub, j))]
    for _, at in grads:
        in_specs.append(pl.BlockSpec(channel, lambda j, at=at: (0, at, j)))
    if gated:
        in_specs.append(pl.BlockSpec(lines, lambda j: (sub, 0, j)))
    if based:
        in_specs.append(pl.BlockSpec(lines, lambda j: (0, 0, j)))
    out_specs, out_shape = [], []
    if out_kind == "pair":
        out_specs.append(pairs)
        out_shape.append(jax.ShapeDtypeStruct(x.shape, BF16))
    if out_kind == "base":
        out_specs.append(pl.BlockSpec(lines, lambda j: (0, 0, j)))
        out_shape.append(jax.ShapeDtypeStruct((plan.rows, chans, plan.crop), BF16))
    if summed:
        out_specs.append(whole(grad))
        out_shape.append(grad)
    operands = [x, mask, *arrays(grads), *extra, *small]
    in_specs += [whole(value) for value in small]
    return pl.pallas_call(
        functools.partial(last_kernel, plan.step, mode),
        grid=(plan.blocks,),
        in_specs=in_specs + [HELD for _ in kept],
        out_specs=out_specs,
        out_shape=out_shape,
        scratch_shapes=[plan.scratch(hidden)] * len(sides),
        input_output_aliases={len(operands): 0} if kept else {},
        compiler_params=params(1),
        cost_estimate=cost(0.2),
        name="last_" + mode,
    )(*operands, *kept)


def swap_all(array):
    return lax.all_to_all(array, "tile", split_axis=0, concat_axis=0, tiled=True)


def tile_sum(array, tiles):
    chans, width = array.shape
    parts = swap_all(array.astype(BF16)).reshape(tiles, chans // tiles, width)
    part = jnp.sum(parts.astype(F32), axis=0).astype(BF16)
    spread = jnp.broadcast_to(part[None], (tiles,) + part.shape).reshape(chans, width)
    return swap_all(spread).astype(F32)


def body(
    tiles, x, d, token_mask, ln_in_gain, ln_in_bias, w_ab, w_gate, ln_out_gain, ln_out_bias, w_out
):
    count, crop, chans = x.shape
    hidden = w_out.shape[0]
    plan = Plan(tiles, count, crop)
    me = lax.axis_index("tile")
    side = (me // plan.half).astype(jnp.int32)
    valid = token_mask.astype(F32)
    own_valid = lax.dynamic_slice_in_dim(valid, me * count, count)
    turned_valid = valid.reshape(tiles, plan.subs, plan.rows).transpose(1, 0, 2).reshape(crop)
    mask = own_valid[:, None] * turned_valid[None, :]
    gain, bias = ln_in_gain[:, None], ln_in_bias[:, None]
    w_t = w_ab.T
    w_cat = jnp.concatenate([w_ab, w_gate], axis=1)
    mid = [gain, bias, w_gate.T, ln_out_gain[:, None], ln_out_bias[:, None], w_out, w_out.T]
    x, d = plan.view(x), plan.view(d)
    owned = lambda array: array.reshape(plan.half, hidden // plan.half, *array.shape[1:])
    joined = lambda array: array.reshape(hidden, *array.shape[2:])
    every = range(plan.subs)

    plan_cut = plan.cut
    two = plan.subs == 2
    cut_b, back_a = plan_cut(6, 2), plan_cut(3, 3, 2)
    small = [gain, bias, w_t, w_cat]

    def middle(at, first, before, ready, product):
        table = jnp.stack([jnp.stack([half, jnp.int32(sub)]) for half, sub in at])
        g, kept, *local = make_middle(plan, table, first, before, ready, x, d, product, mid)
        return g, kept, jnp.concatenate(local[::-1], axis=1)

    def product_of(b):
        return plan.swap(joined(make_product(plan, own_a, b)))

    held, factor_b0 = make_factors(plan, 0, (), x, mask, gain, bias, w_t)
    own_b0 = owned(plan.swap(factor_b0))
    if two:
        (held,) = make_factors(plan, 1, (held,), x, mask, gain, bias, w_t)
    other_0 = plan.exchange(own_b0)
    own_ab = owned(plan.swap(after(held, own_b0)))
    own_a, own_b, got_b = [(own_ab, 0)], [(own_b0, 0)], []
    if two:
        own_a, own_b = [(own_ab, 2), (own_ab, 0)], [(own_b0, 0), (own_ab, 1)]
        sent = plan.pieces(own_ab[:, :, plan.rows : 2 * plan.rows], cut_b)
        got_b = [plan.exchange(sent[0])]
    b_first = [(other_0, 0)] + own_b
    product = product_of(b_first)
    if two:
        got_b.append(plan.exchange(after(sent[1], product)))
    grad, kept, local_mid = middle([(1 - side, 0)], 0, (), (), product)
    owner_g = [owned(plan.swap(after(grad, *got_b[:1])))]
    grad, kept, local = middle([(side, sub) for sub in every], 1, (kept,), (), product)
    local_mid += local
    grad_b0 = make_grad_b(plan, owner_g[0], own_a, back_a)
    back_0 = [plan.exchange(piece) for piece in grad_b0]
    waits = (owner_g[0], grad_b0[0], *got_b[1:2])
    owner_g.append(owned(plan.swap(after(grad, *waits))))
    grad_b_own = make_grad_b(plan, owner_g[1], own_a, [plan.half] * plan.subs)
    if two:
        b_second = [(piece, 0) for piece in got_b]
        b_first = b_first + b_second
        product = joined(make_product(plan, own_a, b_second))
        product = plan.swap(after(product, owner_g[1], back_0[0]))
        grad, kept, local = middle([(1 - side, 1)], 0, (kept,), grad_b_own[:1], product)
        local_mid += local
        owner_g.append(owned(plan.swap(after(grad, back_0[1]))))
        (grad_b1,) = make_grad_b(plan, owner_g[2], own_a, [plan.half])
        back_1 = plan.exchange(grad_b1)
        back_0[2] = after(back_0[2], grad_b1)
    grads = plan.swap(joined(make_grad_a(plan, owner_g, b_first, grad_b_own[0], back_0)))
    first, second = w_ab[:, : 2 * hidden], w_ab[:, 2 * hidden :]
    pair_grad, local_ab = make_last(
        plan, "both", 0, None, x, mask, [(grads, 0), (grads, plan.subs)], [kept], small
    )
    if two:
        grad_b = plan.swap(
            joined((grad_b_own[1].astype(F32) + back_1.astype(F32)).astype(BF16))
        )
        side_a = [gain, bias, w_t[: 2 * hidden], jnp.concatenate([first, w_gate], axis=1)]
        side_b = [gain, bias, w_t[2 * hidden :], second]
        base, local_a = make_last(plan, "a", 1, None, x, mask, [(grads, 1)], [kept], side_a)
        (local_b,) = make_last(plan, "b_sum", 1, None, x, mask, [(grad_b, 0)], [], side_b)
        (pair_grad,) = make_last(
            plan, "b", 1, pair_grad, x, mask, [(grad_b, 0)], [base], side_b
        )
        local_ab += jnp.concatenate([local_a, local_b], axis=1)
    total = tile_sum(jnp.concatenate([local_ab, local_mid], axis=1), tiles) / crop
    wide = 4 * hidden
    return (
        pair_grad.reshape(count, crop, chans),
        total[:, :wide],
        total[:, wide : wide + chans],
        total[:, wide + chans :],
    )


def solution(mesh):
    pairs = P(("crops", "tile"), None, None)
    return jax.shard_map(
        functools.partial(body, mesh.shape["tile"]),
        mesh=mesh,
        in_specs=(pairs, pairs, P("crops")) + (P(),) * 7,
        out_specs=(pairs,) + (P("crops", None),) * 3,
        check_vma=False,
    )
```

```python
import functools

import jax
import jax.numpy as jnp
from jax import lax
from jax.experimental import pallas as pl
from jax.experimental.pallas import tpu as pltpu
from jax.sharding import PartitionSpec as P

HELD = pl.BlockSpec(memory_space=pl.ANY)
EPS = 1e-05
CHANS = 4
F32 = jnp.float32
BF16 = jnp.bfloat16
NN = (((1,), (0,)), ((), ()))
NT = (((1,), (1,)), ((), ()))
TN = (((0,), (0,)), ((), ()))


def params(steps):
    return pltpu.CompilerParams(
        dimension_semantics=("arbitrary",) * steps, vmem_limit_bytes=50 * 1024 * 1024
    )


def cost(micros):
    return pl.CostEstimate(
        flops=int(micros * 1.0e9), bytes_accessed=int(micros * 3.0e6), transcendentals=0
    )


def dot(left, right, form=NN):
    return lax.dot_general(left, right, form, preferred_element_type=F32)


def sigmoid(value):
    return 0.5 * jnp.tanh(0.5 * value) + 0.5


def col_mean(value):
    return jnp.mean(value, axis=0, keepdims=True)


def stats(value):
    centered = value - col_mean(value)
    inv_std = lax.rsqrt(col_mean(centered * centered) + EPS)
    return centered * inv_std, inv_std


def norm_back(upstream, scaled, inv_std):
    return inv_std * (upstream - col_mean(upstream) - scaled * col_mean(upstream * scaled))


def turned(ref, row, count):
    block = ref[pl.ds(row, count)]
    return block.reshape(-1, block.shape[-1]).astype(F32).T


def lane_parts(scratch, count):
    return [(at, lane) for at in range(count) for lane in range(scratch.shape[0])]


def store_rows(scratch, row, count, rows, value):
    hidden = value.shape[0]
    for part, (at, lane) in enumerate(lane_parts(scratch, count)):
        scratch[lane, pl.ds(row + at, hidden, stride=rows), :] = value[:, part * 128 : (part + 1) * 128]


def load_rows(scratch, row, count, rows):
    hidden = scratch.shape[1] // rows
    return jnp.concatenate(
        [
            scratch[lane, pl.ds(row + at, hidden, stride=rows), :]
            for at, lane in lane_parts(scratch, count)
        ],
        axis=1,
    )


def gather_out(scratch, out_ref, rows, at=0):
    hidden = out_ref.shape[0]
    for lane in range(scratch.shape[0]):
        out_ref[:, at : at + rows, lane * 128 : (lane + 1) * 128] = (
            scratch[lane].reshape(hidden, rows, 128).astype(BF16)
        )


def spread_in(in_ref, scratch):
    hidden, rows, cols = in_ref.shape
    for lane in range(scratch.shape[0]):
        scratch[lane] = (
            in_ref[:, :, lane * 128 : (lane + 1) * 128].astype(F32).reshape(hidden * rows, 128)
        )


def flat_rows(ref, row, count):
    return jnp.concatenate([ref[pl.ds(row + at, 1), :] for at in range(count)], axis=1)


def whole(array):
    return pl.BlockSpec(array.shape, lambda *_: (0,) * array.ndim)


class Plan:
    def __init__(self, tiles, count, crop):
        self.tiles, self.count, self.crop = tiles, count, crop
        self.half = tiles // 2
        self.subs = 2 if count % 32 == 0 else 1
        self.rows = count // self.subs
        self.width = self.half * self.rows
        self.blocks = crop // self.width
        self.step = max(1, 512 // self.width)
        self.groups = [
            [side * self.half + at for at in range(self.half)] for side in range(2)
        ]
        self.partner = [(at, (at + self.half) % tiles) for at in range(tiles)]

    def view(self, array):
        return array.reshape(self.count, self.tiles, self.subs, self.rows, array.shape[-1])

    def pair_spec(self, chans, index):
        return pl.BlockSpec((self.rows, self.half, 1, self.rows, chans), index)

    def scratch(self, hidden):
        return pltpu.VMEM((self.width // 128, self.rows * hidden, 128), F32)

    def swap(self, array):
        return lax.all_to_all(
            array, "tile", split_axis=0, concat_axis=0, axis_index_groups=self.groups, tiled=True
        )

    def cut(self, *eighths):
        return [max(1, self.half * share // 8) for share in eighths]

    def pieces(self, array, counts):
        ends = [sum(counts[: at + 1]) for at in range(len(counts))]
        return [array[end - size : end] for size, end in zip(counts, ends)]

    def exchange(self, array):
        return lax.ppermute(array, "tile", self.partner)


def after_kernel(*refs):
    del refs


def after(value, *others):
    return pl.pallas_call(
        after_kernel,
        in_specs=[HELD] * (1 + len(others)),
        out_specs=HELD,
        out_shape=jax.ShapeDtypeStruct(value.shape, value.dtype),
        input_output_aliases={0: 0},
        compiler_params=params(0),
        cost_estimate=cost(0.1),
        name="after",
    )(value, *others)


def factors_kernel(step, joint, x_ref, mask_ref, gain_ref, bias_ref, w_ref, *refs):
    sa_ref, sb_ref = refs[-2:]
    rows = x_ref.shape[0]
    hidden = w_ref.shape[0] // 4

    @pl.loop(0, rows // step, unroll=min(4, rows // step))
    def _(turn):
        row = pl.multiple_of(turn * step, step)
        z_hat, _ = stats(turned(x_ref, row, step))
        normed = (z_hat * gain_ref[...] + bias_ref[...]).astype(BF16)
        mask = flat_rows(mask_ref, row, step)
        proj = dot(w_ref[...], normed)
        value_a, gate_a = proj[:hidden], proj[hidden : 2 * hidden]
        value_b, gate_b = proj[2 * hidden : 3 * hidden], proj[3 * hidden :]
        store_rows(sb_ref, row, step, rows, mask * sigmoid(gate_b) * value_b)
        store_rows(sa_ref, row, step, rows, mask * sigmoid(gate_a) * value_a)

    if joint:
        gather_out(sa_ref, refs[-3], rows)
        gather_out(sb_ref, refs[-3], rows, rows)
    else:
        gather_out(sa_ref, refs[-4], rows)
        gather_out(sb_ref, refs[-3], rows)


def make_factors(plan, sub, before, x, mask, gain, bias, w_t):
    chans = x.shape[-1]
    hidden = w_t.shape[0] // 4
    block = (hidden, plan.rows, plan.width)
    held = plan.rows * (3 if plan.subs == 2 else 1)
    out_specs = [
        pl.BlockSpec(block, lambda j: (0, 2 * (plan.subs - 1), j)),
        pl.BlockSpec(block, lambda j: (0, 0, j)),
    ]
    out_shape = [
        jax.ShapeDtypeStruct((hidden, held, plan.crop), BF16),
        jax.ShapeDtypeStruct((hidden, plan.rows, plan.crop), BF16),
    ]
    if before:
        out_specs = [pl.BlockSpec((hidden, 2 * plan.rows, plan.width), lambda j: (0, 0, j))]
        out_shape = out_shape[:1]
    return pl.pallas_call(
        functools.partial(factors_kernel, plan.step, bool(before)),
        grid=(plan.blocks,),
        in_specs=[
            plan.pair_spec(chans, lambda j: (sub, j % 2, j // 2, 0, 0)),
            pl.BlockSpec((plan.rows, plan.width), lambda j: (sub, j)),
            whole(gain),
            whole(bias),
            whole(w_t),
        ]
        + [HELD for _ in before],
        out_specs=out_specs,
        out_shape=out_shape,
        input_output_aliases={5: 0} if before else {},
        scratch_shapes=[plan.scratch(hidden)] * 2,
        compiler_params=params(1),
        cost_estimate=cost(0.2),
        name="factors",
    )(x, mask, gain, bias, w_t, *before)


def matrix(refs, chan):
    parts = [ref[:, chan].reshape(-1, ref.shape[-1]) for ref in refs]
    return jnp.concatenate(parts, axis=0) if len(parts) > 1 else parts[0]


def by_sub(ref, chan, subs):
    rows = ref.shape[2] // subs
    parts = [
        ref[:, chan, sub * rows : (sub + 1) * rows, :].reshape(-1, ref.shape[3])
        for sub in range(subs)
    ]
    return jnp.concatenate(parts, axis=0) if subs > 1 else parts[0]


def to_subs(ref, chan, value, subs, rows):
    part = value.shape[0] // subs
    for sub in range(subs):
        ref[:, chan, sub * rows : (sub + 1) * rows, :] = value[
            sub * part : (sub + 1) * part
        ].astype(BF16).reshape(ref.shape[0], rows, ref.shape[3])


def own_spec(array):
    src, _, rows, cols = array.shape
    return pl.BlockSpec((src, CHANS, rows, cols), lambda h: (0, h, 0, 0))


def view_spec(plan, view):
    array, at = view
    return pl.BlockSpec((array.shape[0], CHANS, plan.rows, array.shape[3]), lambda h: (0, h, at, 0))


def arrays(views):
    return [array for array, _ in views]


def product_kernel(subs, rows, *refs):
    a, b, p_ref = refs[:subs], refs[subs:-1], refs[-1]
    for chan in range(CHANS):
        to_subs(p_ref, chan, dot(matrix(a, chan), matrix(b, chan), NT), subs, rows)


def make_product(plan, a, b):
    tiles, chans = a[0][0].shape[:2]
    cols = sum(array.shape[0] for array in arrays(b)) * plan.rows
    out = jax.ShapeDtypeStruct((tiles, chans, plan.count, cols), BF16)
    return pl.pallas_call(
        functools.partial(product_kernel, plan.subs, plan.rows),
        grid=(chans // CHANS,),
        in_specs=[view_spec(plan, view) for view in (*a, *b)],
        out_specs=own_spec(out),
        out_shape=out,
        compiler_params=params(1),
        cost_estimate=cost(0.2),
        name="product",
    )(*arrays(a), *arrays(b))


def grad_b_kernel(subs, g_ref, *refs):
    a, outs = refs[:subs], refs[subs:]
    for chan in range(CHANS):
        grad = dot(by_sub(g_ref, chan, subs), matrix(a, chan), TN).astype(BF16)
        at = 0
        for out in outs:
            size = out.shape[0] * out.shape[2]
            out[:, chan] = grad[at : at + size].reshape(out.shape[0], *out.shape[2:])
            at += size


def make_grad_b(plan, g, a, tiles):
    outs = [
        jax.ShapeDtypeStruct((count, g.shape[1], plan.rows, plan.crop), BF16) for count in tiles
    ]
    return pl.pallas_call(
        functools.partial(grad_b_kernel, plan.subs),
        grid=(g.shape[1] // CHANS,),
        in_specs=[own_spec(g)] + [view_spec(plan, view) for view in a],
        out_specs=[own_spec(value) for value in outs],
        out_shape=outs,
        compiler_params=params(1),
        cost_estimate=cost(0.2),
        name="grad_b",
    )(g, *arrays(a))


def grad_a_kernel(subs, rows, counts, *refs):
    g, b = refs[: counts[0]], refs[counts[0] : counts[0] + counts[1]]
    own, back, out = refs[counts[0] + counts[1]], refs[counts[0] + counts[1] + 1 : -1], refs[-1]
    for chan in range(CHANS):
        left = jnp.concatenate([by_sub(ref, chan, subs) for ref in g], axis=1)
        to_subs(out, chan, dot(left, matrix(b, chan)), subs, rows)
        at = 0
        for piece in back:
            end = at + piece.shape[0]
            added = own[at:end, chan].astype(F32) + piece[:, chan].astype(F32)
            out[at:end, chan, subs * rows :, :] = added.astype(BF16)
            at = end


def make_grad_a(plan, g, b, own, back):
    chans = own.shape[1]
    out = jax.ShapeDtypeStruct((plan.half, chans, plan.count + plan.rows, plan.crop), BF16)
    return pl.pallas_call(
        functools.partial(grad_a_kernel, plan.subs, plan.rows, (len(g), len(b))),
        grid=(chans // CHANS,),
        in_specs=[own_spec(value) for value in g]
        + [view_spec(plan, view) for view in b]
        + [own_spec(value) for value in (own, *back)],
        out_specs=own_spec(out),
        out_shape=out,
        compiler_params=params(1),
        cost_estimate=cost(0.2),
        name="grad_a",
    )(*g, *arrays(b), own, *back)


def middle_kernel(
    step, _, x_ref, d_ref, p_ref, gain_ref, bias_ref, wg_ref, og_ref, ob_ref, wo_ref, wot_ref, *refs
):
    g_ref, gb_ref, gwo_ref, gwg_ref, s_ref = refs[-5:]
    rows = x_ref.shape[0]
    width = gb_ref.shape[-1]

    @pl.when((pl.program_id(0) == 0) & (pl.program_id(1) == 0))
    def _():
        gwo_ref[...] = jnp.zeros_like(gwo_ref)
        gwg_ref[...] = jnp.zeros_like(gwg_ref)

    spread_in(p_ref, s_ref)

    @pl.loop(0, rows // step, unroll=min(4, rows // step))
    def _(turn):
        row = pl.multiple_of(turn * step, step)
        z_hat, _ = stats(turned(x_ref, row, step))
        normed = (z_hat * gain_ref[...] + bias_ref[...]).astype(BF16)
        gate = sigmoid(dot(wg_ref[...], normed))
        x_hat, inv_std = stats(load_rows(s_ref, row, step, rows))
        x_norm = (x_hat * og_ref[...] + ob_ref[...]).astype(BF16)
        out_lin = dot(wot_ref[...], x_norm)
        lin = turned(d_ref, row, step) * gate
        grad_lin = lin.astype(BF16)
        gate_back = (lin * out_lin * (1.0 - gate)).astype(BF16)
        upstream = dot(wo_ref[...], grad_lin) * og_ref[...]
        store_rows(s_ref, row, step, rows, norm_back(upstream, x_hat, inv_std))
        for at in range(step):
            gb_ref[row + at] = gate_back[:, at * width : (at + 1) * width]
        gwo_ref[...] += dot(x_norm, grad_lin, NT)
        gwg_ref[...] += dot(normed, gate_back, NT)

    gather_out(s_ref, g_ref, rows)


def make_middle(plan, table, first, before, ready, x, d, p, small):
    chans = x.shape[-1]
    hidden = p.shape[0]
    cut = table.shape[0]
    grads = [jax.ShapeDtypeStruct((hidden, chans), F32), jax.ShapeDtypeStruct((chans, chans), F32)]
    pairs = plan.pair_spec(chans, lambda i, j, at: (i, at[j, 0], at[j, 1], 0, 0))
    channel = (hidden, plan.rows, plan.width)
    kept = [*before, *ready]
    return pl.pallas_call(
        functools.partial(middle_kernel, plan.step),
        grid_spec=pltpu.PrefetchScalarGridSpec(
            num_scalar_prefetch=1,
            grid=(plan.subs, cut),
            in_specs=[pairs, pairs, pl.BlockSpec(channel, lambda i, j, at: (0, i, first + j))]
            + [whole(value) for value in small]
            + [HELD for _ in kept],
            out_specs=[
                pl.BlockSpec(channel, lambda i, j, at: (0, i, j)),
                pl.BlockSpec(
                    (plan.rows, chans, plan.width),
                    lambda i, j, at: (i, 0, at[j, 1] * 2 + at[j, 0]),
                ),
            ]
            + [whole(value) for value in grads],
            scratch_shapes=[plan.scratch(hidden)],
        ),
        out_shape=[
            jax.ShapeDtypeStruct((hidden, plan.count, cut * plan.width), BF16),
            jax.ShapeDtypeStruct((plan.count, chans, plan.crop), BF16),
        ]
        + grads,
        input_output_aliases={4 + len(small): 1} if before else {},
        compiler_params=params(2),
        cost_estimate=cost(0.2),
        name="middle",
    )(table, x, d, p, *small, *kept)


def last_kernel(step, mode, *refs):
    sides, gated, based, out_kind, summed = MODES[mode]
    scratches, rest = refs[-len(sides) :], iter(refs[: -len(sides)])
    x_ref, mask_ref = next(rest), next(rest)
    grads = [next(rest) for _ in sides]
    gate_ref = next(rest) if gated else None
    base_ref = next(rest) if based else None
    gain_ref, bias_ref, wt_ref, wcat_ref, *outs = rest
    gw_ref = outs[-1]
    out_ref = outs[-1 - summed] if out_kind else None
    rows, _, _, _, _ = x_ref.shape
    hidden = grads[0].shape[0]
    width = mask_ref.shape[1]

    if summed:

        @pl.when(pl.program_id(0) == 0)
        def _():
            gw_ref[...] = jnp.zeros_like(gw_ref)

    for ref, scratch in zip(grads, scratches):
        spread_in(ref, scratch)

    @pl.loop(0, rows // step, unroll=min(4, rows // step))
    def _(turn):
        row = pl.multiple_of(turn * step, step)
        z_hat, inv_in = stats(turned(x_ref, row, step))
        normed = (z_hat * gain_ref[...] + bias_ref[...]).astype(BF16)
        mask = flat_rows(mask_ref, row, step)
        proj = dot(wt_ref[...], normed)
        parts = []
        for side, scratch in enumerate(scratches):
            value = proj[2 * side * hidden : (2 * side + 1) * hidden]
            sig = sigmoid(proj[(2 * side + 1) * hidden : (2 * side + 2) * hidden])
            to_value = load_rows(scratch, row, step, rows) * mask * sig
            parts += [to_value.astype(BF16), (to_value * value * (1.0 - sig)).astype(BF16)]
        grad_proj = jnp.concatenate(parts, axis=0)
        if summed:
            gw_ref[...] += dot(normed, grad_proj, NT)
        if out_kind:
            every = grad_proj
            if gated:
                gate_back = jnp.concatenate([gate_ref[row + at] for at in range(step)], axis=1)
                every = jnp.concatenate([grad_proj, gate_back], axis=0)
            upstream = dot(wcat_ref[...], every)
            if based:
                upstream += jnp.concatenate(
                    [base_ref[row + at].astype(F32) for at in range(step)], axis=1
                )
            if out_kind == "pair":
                grad = norm_back(upstream * gain_ref[...], z_hat, inv_in).T.astype(BF16)
                out_ref[pl.ds(row, step)] = grad.reshape((step,) + out_ref.shape[1:])
            else:
                for at in range(step):
                    out_ref[row + at] = upstream[:, at * width : (at + 1) * width].astype(BF16)


MODES = {
    "both": ((0, 1), True, False, "pair", True),
    "a": ((0,), True, False, "base", True),
    "b_sum": ((1,), False, False, "", True),
    "b": ((1,), False, True, "pair", False),
}


def make_last(plan, mode, sub, before, x, mask, grads, extra, small):
    sides, gated, based, out_kind, summed = MODES[mode]
    chans = x.shape[-1]
    hidden = grads[0][0].shape[0]
    grad = jax.ShapeDtypeStruct((chans, 2 * len(sides) * hidden), F32)
    pairs = plan.pair_spec(chans, lambda j: (sub, j % 2, j // 2, 0, 0))
    channel = (hidden, plan.rows, plan.width)
    lines = (plan.rows, chans, plan.width)
    kept = [] if before is None else [before]
    in_specs = [pairs, pl.BlockSpec((plan.rows, plan.width), lambda j: (sub, j))]
    for _, at in grads:
        in_specs.append(pl.BlockSpec(channel, lambda j, at=at: (0, at, j)))
    if gated:
        in_specs.append(pl.BlockSpec(lines, lambda j: (sub, 0, j)))
    if based:
        in_specs.append(pl.BlockSpec(lines, lambda j: (0, 0, j)))
    out_specs, out_shape = [], []
    if out_kind == "pair":
        out_specs.append(pairs)
        out_shape.append(jax.ShapeDtypeStruct(x.shape, BF16))
    if out_kind == "base":
        out_specs.append(pl.BlockSpec(lines, lambda j: (0, 0, j)))
        out_shape.append(jax.ShapeDtypeStruct((plan.rows, chans, plan.crop), BF16))
    if summed:
        out_specs.append(whole(grad))
        out_shape.append(grad)
    operands = [x, mask, *arrays(grads), *extra, *small]
    in_specs += [whole(value) for value in small]
    return pl.pallas_call(
        functools.partial(last_kernel, plan.step, mode),
        grid=(plan.blocks,),
        in_specs=in_specs + [HELD for _ in kept],
        out_specs=out_specs,
        out_shape=out_shape,
        scratch_shapes=[plan.scratch(hidden)] * len(sides),
        input_output_aliases={len(operands): 0} if kept else {},
        compiler_params=params(1),
        cost_estimate=cost(0.2),
        name="last_" + mode,
    )(*operands, *kept)


def swap_all(array):
    return lax.all_to_all(array, "tile", split_axis=0, concat_axis=0, tiled=True)


def tile_sum(array, tiles):
    chans, width = array.shape
    parts = swap_all(array.astype(BF16)).reshape(tiles, chans // tiles, width)
    part = jnp.sum(parts.astype(F32), axis=0).astype(BF16)
    spread = jnp.broadcast_to(part[None], (tiles,) + part.shape).reshape(chans, width)
    return swap_all(spread).astype(F32)


def body(
    tiles, x, d, token_mask, ln_in_gain, ln_in_bias, w_ab, w_gate, ln_out_gain, ln_out_bias, w_out
):
    count, crop, chans = x.shape
    hidden = w_out.shape[0]
    plan = Plan(tiles, count, crop)
    me = lax.axis_index("tile")
    side = (me // plan.half).astype(jnp.int32)
    valid = token_mask.astype(F32)
    own_valid = lax.dynamic_slice_in_dim(valid, me * count, count)
    turned_valid = valid.reshape(tiles, plan.subs, plan.rows).transpose(1, 0, 2).reshape(crop)
    mask = own_valid[:, None] * turned_valid[None, :]
    gain, bias = ln_in_gain[:, None], ln_in_bias[:, None]
    w_t = w_ab.T
    w_cat = jnp.concatenate([w_ab, w_gate], axis=1)
    mid = [gain, bias, w_gate.T, ln_out_gain[:, None], ln_out_bias[:, None], w_out, w_out.T]
    x, d = plan.view(x), plan.view(d)
    owned = lambda array: array.reshape(plan.half, hidden // plan.half, *array.shape[1:])
    joined = lambda array: array.reshape(hidden, *array.shape[2:])
    every = range(plan.subs)

    plan_cut = plan.cut
    two = plan.subs == 2
    cut_b, back_a = plan_cut(6, 2), plan_cut(3, 3, 2)
    small = [gain, bias, w_t, w_cat]

    def middle(at, first, before, ready, product):
        table = jnp.stack([jnp.stack([half, jnp.int32(sub)]) for half, sub in at])
        g, kept, *local = make_middle(plan, table, first, before, ready, x, d, product, mid)
        return g, kept, jnp.concatenate(local[::-1], axis=1)

    def product_of(b):
        return plan.swap(joined(make_product(plan, own_a, b)))

    held, factor_b0 = make_factors(plan, 0, (), x, mask, gain, bias, w_t)
    own_b0 = owned(plan.swap(factor_b0))
    if two:
        (held,) = make_factors(plan, 1, (held,), x, mask, gain, bias, w_t)
    other_0 = plan.exchange(own_b0)
    own_ab = owned(plan.swap(after(held, own_b0)))
    own_a, own_b, got_b = [(own_ab, 0)], [(own_b0, 0)], []
    if two:
        own_a, own_b = [(own_ab, 2), (own_ab, 0)], [(own_b0, 0), (own_ab, 1)]
        sent = plan.pieces(own_ab[:, :, plan.rows : 2 * plan.rows], cut_b)
        got_b = [plan.exchange(sent[0])]
    b_first = [(other_0, 0)] + own_b
    product = product_of(b_first)
    if two:
        got_b.append(plan.exchange(after(sent[1], product)))
    grad, kept, local_mid = middle([(1 - side, 0)], 0, (), (), product)
    owner_g = [owned(plan.swap(after(grad, *got_b[:1])))]
    grad, kept, local = middle([(side, sub) for sub in every], 1, (kept,), (), product)
    local_mid += local
    grad_b0 = make_grad_b(plan, owner_g[0], own_a, back_a)
    back_0 = [plan.exchange(piece) for piece in grad_b0]
    waits = (owner_g[0], grad_b0[0], *got_b[1:2])
    owner_g.append(owned(plan.swap(after(grad, *waits))))
    grad_b_own = make_grad_b(plan, owner_g[1], own_a, [plan.half] * plan.subs)
    if two:
        b_second = [(piece, 0) for piece in got_b]
        b_first = b_first + b_second
        product = joined(make_product(plan, own_a, b_second))
        product = plan.swap(after(product, owner_g[1], back_0[0]))
        grad, kept, local = middle([(1 - side, 1)], 0, (kept,), grad_b_own[:1], product)
        local_mid += local
        owner_g.append(owned(plan.swap(after(grad, back_0[1]))))
        (grad_b1,) = make_grad_b(plan, owner_g[2], own_a, [plan.half])
        back_1 = plan.exchange(grad_b1)
        back_0[2] = after(back_0[2], grad_b1)
    grads = plan.swap(joined(make_grad_a(plan, owner_g, b_first, grad_b_own[0], back_0)))
    first, second = w_ab[:, : 2 * hidden], w_ab[:, 2 * hidden :]
    pair_grad, local_ab = make_last(
        plan, "both", 0, None, x, mask, [(grads, 0), (grads, plan.subs)], [kept], small
    )
    if two:
        back_1 = after(back_1, grads)
        grad_b = plan.swap(
            joined((grad_b_own[1].astype(F32) + back_1.astype(F32)).astype(BF16))
        )
        side_a = [gain, bias, w_t[: 2 * hidden], jnp.concatenate([first, w_gate], axis=1)]
        side_b = [gain, bias, w_t[2 * hidden :], second]
        base, local_a = make_last(plan, "a", 1, None, x, mask, [(grads, 1)], [kept], side_a)
        grad_b = after(grad_b, local_ab, local_a)
        (local_b,) = make_last(plan, "b_sum", 1, None, x, mask, [(grad_b, 0)], [], side_b)
        (pair_grad,) = make_last(
            plan, "b", 1, pair_grad, x, mask, [(grad_b, 0)], [base], side_b
        )
        local_ab += jnp.concatenate([local_a, local_b], axis=1)
    total = tile_sum(jnp.concatenate([local_ab, local_mid], axis=1), tiles) / crop
    wide = 4 * hidden
    return (
        pair_grad.reshape(count, crop, chans),
        total[:, :wide],
        total[:, wide : wide + chans],
        total[:, wide + chans :],
    )


def solution(mesh):
    pairs = P(("crops", "tile"), None, None)
    return jax.shard_map(
        functools.partial(body, mesh.shape["tile"]),
        mesh=mesh,
        in_specs=(pairs, pairs, P("crops")) + (P(),) * 7,
        out_specs=(pairs,) + (P("crops", None),) * 3,
        check_vma=False,
    )
```

```python
import functools

import jax
import jax.numpy as jnp
from jax import lax
from jax.experimental import pallas as pl
from jax.experimental.pallas import tpu as pltpu
from jax.sharding import PartitionSpec as P

HELD = pl.BlockSpec(memory_space=pl.ANY)
EPS = 1e-05
CHANS = 4
F32 = jnp.float32
BF16 = jnp.bfloat16
NN = (((1,), (0,)), ((), ()))
NT = (((1,), (1,)), ((), ()))
TN = (((0,), (0,)), ((), ()))


def params(steps):
    return pltpu.CompilerParams(
        dimension_semantics=("arbitrary",) * steps, vmem_limit_bytes=50 * 1024 * 1024
    )


def cost(micros):
    return pl.CostEstimate(
        flops=int(micros * 1.0e9), bytes_accessed=int(micros * 3.0e6), transcendentals=0
    )


def dot(left, right, form=NN):
    return lax.dot_general(left, right, form, preferred_element_type=F32)


def sigmoid(value):
    return 0.5 * jnp.tanh(0.5 * value) + 0.5


def col_mean(value):
    return jnp.mean(value, axis=0, keepdims=True)


def stats(value):
    centered = value - col_mean(value)
    inv_std = lax.rsqrt(col_mean(centered * centered) + EPS)
    return centered * inv_std, inv_std


def norm_back(upstream, scaled, inv_std):
    return inv_std * (upstream - col_mean(upstream) - scaled * col_mean(upstream * scaled))


def turned(ref, row, count):
    block = ref[pl.ds(row, count)]
    return block.reshape(-1, block.shape[-1]).astype(F32).T


def lane_parts(scratch, count):
    return [(at, lane) for at in range(count) for lane in range(scratch.shape[0])]


def store_rows(scratch, row, count, rows, value):
    hidden = value.shape[0]
    for part, (at, lane) in enumerate(lane_parts(scratch, count)):
        scratch[lane, pl.ds(row + at, hidden, stride=rows), :] = value[:, part * 128 : (part + 1) * 128]


def load_rows(scratch, row, count, rows):
    hidden = scratch.shape[1] // rows
    return jnp.concatenate(
        [
            scratch[lane, pl.ds(row + at, hidden, stride=rows), :]
            for at, lane in lane_parts(scratch, count)
        ],
        axis=1,
    )


def gather_out(scratch, out_ref, rows, at=0):
    hidden = out_ref.shape[0]
    for lane in range(scratch.shape[0]):
        out_ref[:, at : at + rows, lane * 128 : (lane + 1) * 128] = (
            scratch[lane].reshape(hidden, rows, 128).astype(BF16)
        )


def spread_in(in_ref, scratch):
    hidden, rows, cols = in_ref.shape
    for lane in range(scratch.shape[0]):
        scratch[lane] = (
            in_ref[:, :, lane * 128 : (lane + 1) * 128].astype(F32).reshape(hidden * rows, 128)
        )


def flat_rows(ref, row, count):
    return jnp.concatenate([ref[pl.ds(row + at, 1), :] for at in range(count)], axis=1)


def whole(array):
    return pl.BlockSpec(array.shape, lambda *_: (0,) * array.ndim)


class Plan:
    def __init__(self, tiles, count, crop):
        self.tiles, self.count, self.crop = tiles, count, crop
        self.half = tiles // 2
        self.subs = 2 if count % 32 == 0 else 1
        self.rows = count // self.subs
        self.width = self.half * self.rows
        self.blocks = crop // self.width
        self.step = max(1, 512 // self.width)
        self.groups = [
            [side * self.half + at for at in range(self.half)] for side in range(2)
        ]
        self.partner = [(at, (at + self.half) % tiles) for at in range(tiles)]

    def view(self, array):
        return array.reshape(self.count, self.tiles, self.subs, self.rows, array.shape[-1])

    def pair_spec(self, chans, index):
        return pl.BlockSpec((self.rows, self.half, 1, self.rows, chans), index)

    def scratch(self, hidden):
        return pltpu.VMEM((self.width // 128, self.rows * hidden, 128), F32)

    def swap(self, array):
        return lax.all_to_all(
            array, "tile", split_axis=0, concat_axis=0, axis_index_groups=self.groups, tiled=True
        )

    def cut(self, *eighths):
        return [max(1, self.half * share // 8) for share in eighths]

    def pieces(self, array, counts):
        ends = [sum(counts[: at + 1]) for at in range(len(counts))]
        return [array[end - size : end] for size, end in zip(counts, ends)]

    def exchange(self, array):
        return lax.ppermute(array, "tile", self.partner)


def after_kernel(*refs):
    del refs


def after(value, *others):
    return pl.pallas_call(
        after_kernel,
        in_specs=[HELD] * (1 + len(others)),
        out_specs=HELD,
        out_shape=jax.ShapeDtypeStruct(value.shape, value.dtype),
        input_output_aliases={0: 0},
        compiler_params=params(0),
        cost_estimate=cost(0.1),
        name="after",
    )(value, *others)


def factors_kernel(step, joint, x_ref, mask_ref, norm_ref, w_ref, *refs):
    sa_ref, sb_ref = refs[-2:]
    rows = x_ref.shape[0]
    hidden = w_ref.shape[0] // 4

    @pl.loop(0, rows // step, unroll=min(4, rows // step))
    def _(turn):
        row = pl.multiple_of(turn * step, step)
        z_hat, _ = stats(turned(x_ref, row, step))
        normed = (z_hat * norm_ref[:, 0:1] + norm_ref[:, 1:2]).astype(BF16)
        mask = flat_rows(mask_ref, row, step)
        proj = dot(w_ref[...], normed)
        value_a, gate_a = proj[:hidden], proj[hidden : 2 * hidden]
        value_b, gate_b = proj[2 * hidden : 3 * hidden], proj[3 * hidden :]
        store_rows(sb_ref, row, step, rows, mask * sigmoid(gate_b) * value_b)
        store_rows(sa_ref, row, step, rows, mask * sigmoid(gate_a) * value_a)

    if joint:
        gather_out(sa_ref, refs[-3], rows)
        gather_out(sb_ref, refs[-3], rows, rows)
    else:
        gather_out(sa_ref, refs[-4], rows)
        gather_out(sb_ref, refs[-3], rows)


def make_factors(plan, sub, before, x, mask, norms, w_t):
    chans = x.shape[-1]
    hidden = w_t.shape[0] // 4
    block = (hidden, plan.rows, plan.width)
    held = plan.rows * (3 if plan.subs == 2 else 1)
    out_specs = [
        pl.BlockSpec(block, lambda j: (0, 2 * (plan.subs - 1), j)),
        pl.BlockSpec(block, lambda j: (0, 0, j)),
    ]
    out_shape = [
        jax.ShapeDtypeStruct((hidden, held, plan.crop), BF16),
        jax.ShapeDtypeStruct((hidden, plan.rows, plan.crop), BF16),
    ]
    if before:
        out_specs = [pl.BlockSpec((hidden, 2 * plan.rows, plan.width), lambda j: (0, 0, j))]
        out_shape = out_shape[:1]
    return pl.pallas_call(
        functools.partial(factors_kernel, plan.step, bool(before)),
        grid=(plan.blocks,),
        in_specs=[
            plan.pair_spec(chans, lambda j: (sub, j % 2, j // 2, 0, 0)),
            pl.BlockSpec((plan.rows, plan.width), lambda j: (sub, j)),
            whole(norms),
            whole(w_t),
        ]
        + [HELD for _ in before],
        out_specs=out_specs,
        out_shape=out_shape,
        input_output_aliases={4: 0} if before else {},
        scratch_shapes=[plan.scratch(hidden)] * 2,
        compiler_params=params(1),
        cost_estimate=cost(0.2),
        name="factors",
    )(x, mask, norms, w_t, *before)


def matrix(refs, chan):
    parts = [ref[:, chan].reshape(-1, ref.shape[-1]) for ref in refs]
    return jnp.concatenate(parts, axis=0) if len(parts) > 1 else parts[0]


def by_sub(ref, chan, subs):
    rows = ref.shape[2] // subs
    parts = [
        ref[:, chan, sub * rows : (sub + 1) * rows, :].reshape(-1, ref.shape[3])
        for sub in range(subs)
    ]
    return jnp.concatenate(parts, axis=0) if subs > 1 else parts[0]


def to_subs(ref, chan, value, subs, rows):
    part = value.shape[0] // subs
    for sub in range(subs):
        ref[:, chan, sub * rows : (sub + 1) * rows, :] = value[
            sub * part : (sub + 1) * part
        ].astype(BF16).reshape(ref.shape[0], rows, ref.shape[3])


def own_spec(array):
    src, _, rows, cols = array.shape
    return pl.BlockSpec((src, CHANS, rows, cols), lambda h: (0, h, 0, 0))


def view_spec(plan, view):
    array, at = view
    return pl.BlockSpec((array.shape[0], CHANS, plan.rows, array.shape[3]), lambda h: (0, h, at, 0))


def arrays(views):
    return [array for array, _ in views]


def product_kernel(subs, rows, *refs):
    a, b, p_ref = refs[:subs], refs[subs:-1], refs[-1]
    for chan in range(CHANS):
        to_subs(p_ref, chan, dot(matrix(a, chan), matrix(b, chan), NT), subs, rows)


def make_product(plan, a, b):
    tiles, chans = a[0][0].shape[:2]
    cols = sum(array.shape[0] for array in arrays(b)) * plan.rows
    out = jax.ShapeDtypeStruct((tiles, chans, plan.count, cols), BF16)
    return pl.pallas_call(
        functools.partial(product_kernel, plan.subs, plan.rows),
        grid=(chans // CHANS,),
        in_specs=[view_spec(plan, view) for view in (*a, *b)],
        out_specs=own_spec(out),
        out_shape=out,
        compiler_params=params(1),
        cost_estimate=cost(0.2),
        name="product",
    )(*arrays(a), *arrays(b))


def grad_b_kernel(subs, g_ref, *refs):
    a, outs = refs[:subs], refs[subs:]
    for chan in range(CHANS):
        grad = dot(by_sub(g_ref, chan, subs), matrix(a, chan), TN).astype(BF16)
        at = 0
        for out in outs:
            size = out.shape[0] * out.shape[2]
            out[:, chan] = grad[at : at + size].reshape(out.shape[0], *out.shape[2:])
            at += size


def make_grad_b(plan, g, a, tiles):
    outs = [
        jax.ShapeDtypeStruct((count, g.shape[1], plan.rows, plan.crop), BF16) for count in tiles
    ]
    return pl.pallas_call(
        functools.partial(grad_b_kernel, plan.subs),
        grid=(g.shape[1] // CHANS,),
        in_specs=[own_spec(g)] + [view_spec(plan, view) for view in a],
        out_specs=[own_spec(value) for value in outs],
        out_shape=outs,
        compiler_params=params(1),
        cost_estimate=cost(0.2),
        name="grad_b",
    )(g, *arrays(a))


def grad_a_kernel(subs, rows, counts, *refs):
    g, b = refs[: counts[0]], refs[counts[0] : counts[0] + counts[1]]
    own, back, out = refs[counts[0] + counts[1]], refs[counts[0] + counts[1] + 1 : -1], refs[-1]
    for chan in range(CHANS):
        left = jnp.concatenate([by_sub(ref, chan, subs) for ref in g], axis=1)
        to_subs(out, chan, dot(left, matrix(b, chan)), subs, rows)
        at = 0
        for piece in back:
            end = at + piece.shape[0]
            added = own[at:end, chan].astype(F32) + piece[:, chan].astype(F32)
            out[at:end, chan, subs * rows :, :] = added.astype(BF16)
            at = end


def make_grad_a(plan, g, b, own, back):
    chans = own.shape[1]
    out = jax.ShapeDtypeStruct((plan.half, chans, plan.count + plan.rows, plan.crop), BF16)
    return pl.pallas_call(
        functools.partial(grad_a_kernel, plan.subs, plan.rows, (len(g), len(b))),
        grid=(chans // CHANS,),
        in_specs=[own_spec(value) for value in g]
        + [view_spec(plan, view) for view in b]
        + [own_spec(value) for value in (own, *back)],
        out_specs=own_spec(out),
        out_shape=out,
        compiler_params=params(1),
        cost_estimate=cost(0.2),
        name="grad_a",
    )(*g, *arrays(b), own, *back)


def middle_kernel(
    step, _, x_ref, d_ref, p_ref, norm_ref, wg_ref, wo_ref, wot_ref, *refs
):
    g_ref, gb_ref, gwo_ref, gwg_ref, s_ref = refs[-5:]
    rows = x_ref.shape[0]
    width = gb_ref.shape[-1]

    @pl.when((pl.program_id(0) == 0) & (pl.program_id(1) == 0))
    def _():
        gwo_ref[...] = jnp.zeros_like(gwo_ref)
        gwg_ref[...] = jnp.zeros_like(gwg_ref)

    spread_in(p_ref, s_ref)

    @pl.loop(0, rows // step, unroll=min(4, rows // step))
    def _(turn):
        row = pl.multiple_of(turn * step, step)
        z_hat, _ = stats(turned(x_ref, row, step))
        normed = (z_hat * norm_ref[:, 0:1] + norm_ref[:, 1:2]).astype(BF16)
        gate = sigmoid(dot(wg_ref[...], normed))
        x_hat, inv_std = stats(load_rows(s_ref, row, step, rows))
        x_norm = (x_hat * norm_ref[:, 2:3] + norm_ref[:, 3:4]).astype(BF16)
        out_lin = dot(wot_ref[...], x_norm)
        lin = turned(d_ref, row, step) * gate
        grad_lin = lin.astype(BF16)
        gate_back = (lin * out_lin * (1.0 - gate)).astype(BF16)
        upstream = dot(wo_ref[...], grad_lin) * norm_ref[:, 2:3]
        store_rows(s_ref, row, step, rows, norm_back(upstream, x_hat, inv_std))
        for at in range(step):
            gb_ref[row + at] = gate_back[:, at * width : (at + 1) * width]
        gwo_ref[...] += dot(x_norm, grad_lin, NT)
        gwg_ref[...] += dot(normed, gate_back, NT)

    gather_out(s_ref, g_ref, rows)


def make_middle(plan, table, first, before, ready, x, d, p, small):
    chans = x.shape[-1]
    hidden = p.shape[0]
    cut = table.shape[0]
    grads = [jax.ShapeDtypeStruct((hidden, chans), F32), jax.ShapeDtypeStruct((chans, chans), F32)]
    pairs = plan.pair_spec(chans, lambda i, j, at: (i, at[j, 0], at[j, 1], 0, 0))
    channel = (hidden, plan.rows, plan.width)
    kept = [*before, *ready]
    return pl.pallas_call(
        functools.partial(middle_kernel, plan.step),
        grid_spec=pltpu.PrefetchScalarGridSpec(
            num_scalar_prefetch=1,
            grid=(plan.subs, cut),
            in_specs=[pairs, pairs, pl.BlockSpec(channel, lambda i, j, at: (0, i, first + j))]
            + [whole(value) for value in small]
            + [HELD for _ in kept],
            out_specs=[
                pl.BlockSpec(channel, lambda i, j, at: (0, i, j)),
                pl.BlockSpec(
                    (plan.rows, chans, plan.width),
                    lambda i, j, at: (i, 0, at[j, 1] * 2 + at[j, 0]),
                ),
            ]
            + [whole(value) for value in grads],
            scratch_shapes=[plan.scratch(hidden)],
        ),
        out_shape=[
            jax.ShapeDtypeStruct((hidden, plan.count, cut * plan.width), BF16),
            jax.ShapeDtypeStruct((plan.count, chans, plan.crop), BF16),
        ]
        + grads,
        input_output_aliases={4 + len(small): 1} if before else {},
        compiler_params=params(2),
        cost_estimate=cost(0.2),
        name="middle",
    )(table, x, d, p, *small, *kept)


def last_kernel(step, mode, *refs):
    sides, gated, based, out_kind, summed = MODES[mode]
    scratches, rest = refs[-len(sides) :], iter(refs[: -len(sides)])
    x_ref, mask_ref = next(rest), next(rest)
    grads = [next(rest) for _ in sides]
    gate_ref = next(rest) if gated else None
    base_ref = next(rest) if based else None
    norm_ref, wt_ref, wcat_ref, *outs = rest
    gw_ref = outs[-1]
    out_ref = outs[-1 - summed] if out_kind else None
    rows, _, _, _, _ = x_ref.shape
    hidden = grads[0].shape[0]
    width = mask_ref.shape[1]

    if summed:

        @pl.when(pl.program_id(0) == 0)
        def _():
            gw_ref[...] = jnp.zeros_like(gw_ref)

    for ref, scratch in zip(grads, scratches):
        spread_in(ref, scratch)

    @pl.loop(0, rows // step, unroll=min(4, rows // step))
    def _(turn):
        row = pl.multiple_of(turn * step, step)
        z_hat, inv_in = stats(turned(x_ref, row, step))
        normed = (z_hat * norm_ref[:, 0:1] + norm_ref[:, 1:2]).astype(BF16)
        mask = flat_rows(mask_ref, row, step)
        proj = dot(wt_ref[...], normed)
        parts = []
        for side, scratch in enumerate(scratches):
            value = proj[2 * side * hidden : (2 * side + 1) * hidden]
            sig = sigmoid(proj[(2 * side + 1) * hidden : (2 * side + 2) * hidden])
            to_value = load_rows(scratch, row, step, rows) * mask * sig
            parts += [to_value.astype(BF16), (to_value * value * (1.0 - sig)).astype(BF16)]
        grad_proj = jnp.concatenate(parts, axis=0)
        if summed:
            gw_ref[...] += dot(normed, grad_proj, NT)
        if out_kind:
            every = grad_proj
            if gated:
                gate_back = jnp.concatenate([gate_ref[row + at] for at in range(step)], axis=1)
                every = jnp.concatenate([grad_proj, gate_back], axis=0)
            upstream = dot(wcat_ref[...], every)
            if based:
                upstream += jnp.concatenate(
                    [base_ref[row + at].astype(F32) for at in range(step)], axis=1
                )
            if out_kind == "pair":
                grad = norm_back(upstream * norm_ref[:, 0:1], z_hat, inv_in).T.astype(BF16)
                out_ref[pl.ds(row, step)] = grad.reshape((step,) + out_ref.shape[1:])
            else:
                for at in range(step):
                    out_ref[row + at] = upstream[:, at * width : (at + 1) * width].astype(BF16)


MODES = {
    "both": ((0, 1), True, False, "pair", True),
    "a": ((0,), True, False, "base", True),
    "b_sum": ((1,), False, False, "", True),
    "b": ((1,), False, True, "pair", False),
}


def make_last(plan, mode, sub, before, x, mask, grads, extra, small):
    sides, gated, based, out_kind, summed = MODES[mode]
    chans = x.shape[-1]
    hidden = grads[0][0].shape[0]
    grad = jax.ShapeDtypeStruct((chans, 2 * len(sides) * hidden), F32)
    pairs = plan.pair_spec(chans, lambda j: (sub, j % 2, j // 2, 0, 0))
    channel = (hidden, plan.rows, plan.width)
    lines = (plan.rows, chans, plan.width)
    kept = [] if before is None else [before]
    in_specs = [pairs, pl.BlockSpec((plan.rows, plan.width), lambda j: (sub, j))]
    for _, at in grads:
        in_specs.append(pl.BlockSpec(channel, lambda j, at=at: (0, at, j)))
    if gated:
        in_specs.append(pl.BlockSpec(lines, lambda j: (sub, 0, j)))
    if based:
        in_specs.append(pl.BlockSpec(lines, lambda j: (0, 0, j)))
    out_specs, out_shape = [], []
    if out_kind == "pair":
        out_specs.append(pairs)
        out_shape.append(jax.ShapeDtypeStruct(x.shape, BF16))
    if out_kind == "base":
        out_specs.append(pl.BlockSpec(lines, lambda j: (0, 0, j)))
        out_shape.append(jax.ShapeDtypeStruct((plan.rows, chans, plan.crop), BF16))
    if summed:
        out_specs.append(whole(grad))
        out_shape.append(grad)
    operands = [x, mask, *arrays(grads), *extra, *small]
    in_specs += [whole(value) for value in small]
    return pl.pallas_call(
        functools.partial(last_kernel, plan.step, mode),
        grid=(plan.blocks,),
        in_specs=in_specs + [HELD for _ in kept],
        out_specs=out_specs,
        out_shape=out_shape,
        scratch_shapes=[plan.scratch(hidden)] * len(sides),
        input_output_aliases={len(operands): 0} if kept else {},
        compiler_params=params(1),
        cost_estimate=cost(0.2),
        name="last_" + mode,
    )(*operands, *kept)


def swap_all(array):
    return lax.all_to_all(array, "tile", split_axis=0, concat_axis=0, tiled=True)


def tile_sum(array, tiles):
    chans, width = array.shape
    parts = swap_all(array.astype(BF16)).reshape(tiles, chans // tiles, width)
    part = jnp.sum(parts.astype(F32), axis=0).astype(BF16)
    spread = jnp.broadcast_to(part[None], (tiles,) + part.shape).reshape(chans, width)
    return swap_all(spread).astype(F32)


def body(
    tiles, x, d, token_mask, ln_in_gain, ln_in_bias, w_ab, w_gate, ln_out_gain, ln_out_bias, w_out
):
    count, crop, chans = x.shape
    hidden = w_out.shape[0]
    plan = Plan(tiles, count, crop)
    me = lax.axis_index("tile")
    side = (me // plan.half).astype(jnp.int32)
    valid = token_mask.astype(F32)
    own_valid = lax.dynamic_slice_in_dim(valid, me * count, count)
    turned_valid = valid.reshape(tiles, plan.subs, plan.rows).transpose(1, 0, 2).reshape(crop)
    mask = own_valid[:, None] * turned_valid[None, :]
    norms = jnp.stack([ln_in_gain, ln_in_bias, ln_out_gain, ln_out_bias], axis=1)
    w_t = w_ab.T
    w_cat = jnp.concatenate([w_ab, w_gate], axis=1)
    mid = [norms, w_gate.T, w_out, w_out.T]
    x, d = plan.view(x), plan.view(d)
    owned = lambda array: array.reshape(plan.half, hidden // plan.half, *array.shape[1:])
    joined = lambda array: array.reshape(hidden, *array.shape[2:])
    every = range(plan.subs)

    plan_cut = plan.cut
    two = plan.subs == 2
    cut_b, back_a = plan_cut(6, 2), plan_cut(3, 3, 2)
    small = [norms, w_t, w_cat]

    def middle(at, first, before, ready, product):
        table = jnp.stack([jnp.stack([half, jnp.int32(sub)]) for half, sub in at])
        g, kept, *local = make_middle(plan, table, first, before, ready, x, d, product, mid)
        return g, kept, jnp.concatenate(local[::-1], axis=1)

    def product_of(b):
        return plan.swap(joined(make_product(plan, own_a, b)))

    held, factor_b0 = make_factors(plan, 0, (), x, mask, norms, w_t)
    own_b0 = owned(plan.swap(factor_b0))
    if two:
        (held,) = make_factors(plan, 1, (held,), x, mask, norms, w_t)
    other_0 = plan.exchange(own_b0)
    own_ab = owned(plan.swap(after(held, own_b0)))
    own_a, own_b, got_b = [(own_ab, 0)], [(own_b0, 0)], []
    if two:
        own_a, own_b = [(own_ab, 2), (own_ab, 0)], [(own_b0, 0), (own_ab, 1)]
        sent = plan.pieces(own_ab[:, :, plan.rows : 2 * plan.rows], cut_b)
        got_b = [plan.exchange(sent[0])]
    b_first = [(other_0, 0)] + own_b
    product = product_of(b_first)
    if two:
        got_b.append(plan.exchange(after(sent[1], product)))
    grad, kept, local_mid = middle([(1 - side, 0)], 0, (), (), product)
    owner_g = [owned(plan.swap(after(grad, *got_b[:1])))]
    grad, kept, local = middle([(side, sub) for sub in every], 1, (kept,), (), product)
    local_mid += local
    grad_b0 = make_grad_b(plan, owner_g[0], own_a, back_a)
    back_0 = [plan.exchange(piece) for piece in grad_b0]
    waits = (owner_g[0], grad_b0[0], *got_b[1:2])
    owner_g.append(owned(plan.swap(after(grad, *waits))))
    grad_b_own = make_grad_b(plan, owner_g[1], own_a, [plan.half] * plan.subs)
    if two:
        b_second = [(piece, 0) for piece in got_b]
        b_first = b_first + b_second
        product = joined(make_product(plan, own_a, b_second))
        product = plan.swap(after(product, owner_g[1], back_0[0]))
        grad, kept, local = middle([(1 - side, 1)], 0, (kept,), grad_b_own[:1], product)
        local_mid += local
        owner_g.append(owned(plan.swap(after(grad, back_0[1]))))
        (grad_b1,) = make_grad_b(plan, owner_g[2], own_a, [plan.half])
        back_1 = plan.exchange(grad_b1)
        back_0[2] = after(back_0[2], grad_b1)
    grads = plan.swap(joined(make_grad_a(plan, owner_g, b_first, grad_b_own[0], back_0)))
    first, second = w_ab[:, : 2 * hidden], w_ab[:, 2 * hidden :]
    pair_grad, local_ab = make_last(
        plan, "both", 0, None, x, mask, [(grads, 0), (grads, plan.subs)], [kept], small
    )
    if two:
        back_1 = after(back_1, grads)
        grad_b = plan.swap(
            joined((grad_b_own[1].astype(F32) + back_1.astype(F32)).astype(BF16))
        )
        side_a = [norms, w_t[: 2 * hidden], jnp.concatenate([first, w_gate], axis=1)]
        side_b = [norms, w_t[2 * hidden :], second]
        base, local_a = make_last(plan, "a", 1, None, x, mask, [(grads, 1)], [kept], side_a)
        grad_b = after(grad_b, local_ab, local_a)
        (local_b,) = make_last(plan, "b_sum", 1, None, x, mask, [(grad_b, 0)], [], side_b)
        (pair_grad,) = make_last(
            plan, "b", 1, pair_grad, x, mask, [(grad_b, 0)], [base], side_b
        )
        local_ab += jnp.concatenate([local_a, local_b], axis=1)
    total = tile_sum(jnp.concatenate([local_ab, local_mid], axis=1), tiles) / crop
    wide = 4 * hidden
    return (
        pair_grad.reshape(count, crop, chans),
        total[:, :wide],
        total[:, wide : wide + chans],
        total[:, wide + chans :],
    )


def solution(mesh):
    pairs = P(("crops", "tile"), None, None)
    return jax.shard_map(
        functools.partial(body, mesh.shape["tile"]),
        mesh=mesh,
        in_specs=(pairs, pairs, P("crops")) + (P(),) * 7,
        out_specs=(pairs,) + (P("crops", None),) * 3,
        check_vma=False,
    )
```

```python
import functools

import jax
import jax.numpy as jnp
from jax import lax
from jax.experimental import pallas as pl
from jax.experimental.pallas import tpu as pltpu
from jax.sharding import PartitionSpec as P

HELD = pl.BlockSpec(memory_space=pl.ANY)
EPS = 1e-05
CHANS = 4
F32 = jnp.float32
BF16 = jnp.bfloat16
NN = (((1,), (0,)), ((), ()))
NT = (((1,), (1,)), ((), ()))
TN = (((0,), (0,)), ((), ()))


def params(steps):
    return pltpu.CompilerParams(
        dimension_semantics=("arbitrary",) * steps, vmem_limit_bytes=50 * 1024 * 1024
    )


def cost(micros):
    return pl.CostEstimate(
        flops=int(micros * 1.0e9), bytes_accessed=int(micros * 3.0e6), transcendentals=0
    )


def dot(left, right, form=NN):
    return lax.dot_general(left, right, form, preferred_element_type=F32)


def sigmoid(value):
    return 0.5 * jnp.tanh(0.5 * value) + 0.5


def col_mean(value):
    return jnp.mean(value, axis=0, keepdims=True)


def stats(value):
    centered = value - col_mean(value)
    inv_std = lax.rsqrt(col_mean(centered * centered) + EPS)
    return centered * inv_std, inv_std


def norm_back(upstream, scaled, inv_std):
    return inv_std * (upstream - col_mean(upstream) - scaled * col_mean(upstream * scaled))


def turned(ref, row, count):
    block = ref[pl.ds(row, count)]
    return block.reshape(-1, block.shape[-1]).astype(F32).T


def lane_parts(scratch, count):
    return [(at, lane) for at in range(count) for lane in range(scratch.shape[0])]


def store_rows(scratch, row, count, rows, value):
    hidden = value.shape[0]
    for part, (at, lane) in enumerate(lane_parts(scratch, count)):
        scratch[lane, pl.ds(row + at, hidden, stride=rows), :] = value[:, part * 128 : (part + 1) * 128]


def load_rows(scratch, row, count, rows):
    hidden = scratch.shape[1] // rows
    return jnp.concatenate(
        [
            scratch[lane, pl.ds(row + at, hidden, stride=rows), :]
            for at, lane in lane_parts(scratch, count)
        ],
        axis=1,
    )


def gather_out(scratch, out_ref, rows, at=0):
    hidden = out_ref.shape[0]
    for lane in range(scratch.shape[0]):
        out_ref[:, at : at + rows, lane * 128 : (lane + 1) * 128] = (
            scratch[lane].reshape(hidden, rows, 128).astype(BF16)
        )


def spread_in(in_ref, scratch):
    hidden, rows, cols = in_ref.shape
    for lane in range(scratch.shape[0]):
        scratch[lane] = (
            in_ref[:, :, lane * 128 : (lane + 1) * 128].astype(F32).reshape(hidden * rows, 128)
        )


def flat_rows(ref, row, count):
    return jnp.concatenate([ref[pl.ds(row + at, 1), :] for at in range(count)], axis=1)


def whole(array):
    return pl.BlockSpec(array.shape, lambda *_: (0,) * array.ndim)


class Plan:
    def __init__(self, tiles, count, crop):
        self.tiles, self.count, self.crop = tiles, count, crop
        self.half = tiles // 2
        self.subs = 2 if count % 32 == 0 else 1
        self.rows = count // self.subs
        self.width = self.half * self.rows
        self.blocks = crop // self.width
        self.step = max(1, 512 // self.width)
        self.groups = [
            [side * self.half + at for at in range(self.half)] for side in range(2)
        ]
        self.partner = [(at, (at + self.half) % tiles) for at in range(tiles)]

    def view(self, array):
        return array.reshape(self.count, self.tiles, self.subs, self.rows, array.shape[-1])

    def pair_spec(self, chans, index):
        return pl.BlockSpec((self.rows, self.half, 1, self.rows, chans), index)

    def scratch(self, hidden):
        return pltpu.VMEM((self.width // 128, self.rows * hidden, 128), F32)

    def swap(self, array):
        return lax.all_to_all(
            array, "tile", split_axis=0, concat_axis=0, axis_index_groups=self.groups, tiled=True
        )

    def cut(self, *eighths):
        return [max(1, self.half * share // 8) for share in eighths]

    def pieces(self, array, counts):
        ends = [sum(counts[: at + 1]) for at in range(len(counts))]
        return [array[end - size : end] for size, end in zip(counts, ends)]

    def exchange(self, array):
        return lax.ppermute(array, "tile", self.partner)


def after_kernel(*refs):
    del refs


def after(value, *others):
    return pl.pallas_call(
        after_kernel,
        in_specs=[HELD] * (1 + len(others)),
        out_specs=HELD,
        out_shape=jax.ShapeDtypeStruct(value.shape, value.dtype),
        input_output_aliases={0: 0},
        compiler_params=params(0),
        cost_estimate=cost(0.1),
        name="after",
    )(value, *others)


def factors_kernel(step, joint, x_ref, mask_ref, norm_ref, w_ref, *refs):
    sa_ref, sb_ref = refs[-2:]
    rows = x_ref.shape[0]
    hidden = w_ref.shape[0] // 4

    @pl.loop(0, rows // step, unroll=min(4, rows // step))
    def _(turn):
        row = pl.multiple_of(turn * step, step)
        z_hat, _ = stats(turned(x_ref, row, step))
        normed = (z_hat * norm_ref[:, 0:1] + norm_ref[:, 1:2]).astype(BF16)
        mask = flat_rows(mask_ref, row, step)
        proj = dot(w_ref[...], normed)
        value_a, gate_a = proj[:hidden], proj[hidden : 2 * hidden]
        value_b, gate_b = proj[2 * hidden : 3 * hidden], proj[3 * hidden :]
        store_rows(sb_ref, row, step, rows, mask * sigmoid(gate_b) * value_b)
        store_rows(sa_ref, row, step, rows, mask * sigmoid(gate_a) * value_a)

    if joint:
        gather_out(sa_ref, refs[-3], rows)
        gather_out(sb_ref, refs[-3], rows, rows)
    else:
        gather_out(sa_ref, refs[-4], rows)
        gather_out(sb_ref, refs[-3], rows)


def make_factors(plan, sub, before, x, mask, norms, w_t):
    chans = x.shape[-1]
    hidden = w_t.shape[0] // 4
    block = (hidden, plan.rows, plan.width)
    held = plan.rows * (3 if plan.subs == 2 else 1)
    out_specs = [
        pl.BlockSpec(block, lambda j: (0, 2 * (plan.subs - 1), j)),
        pl.BlockSpec(block, lambda j: (0, 0, j)),
    ]
    out_shape = [
        jax.ShapeDtypeStruct((hidden, held, plan.crop), BF16),
        jax.ShapeDtypeStruct((hidden, plan.rows, plan.crop), BF16),
    ]
    if before:
        out_specs = [pl.BlockSpec((hidden, 2 * plan.rows, plan.width), lambda j: (0, 0, j))]
        out_shape = out_shape[:1]
    return pl.pallas_call(
        functools.partial(factors_kernel, plan.step, bool(before)),
        grid=(plan.blocks,),
        in_specs=[
            plan.pair_spec(chans, lambda j: (sub, j % 2, j // 2, 0, 0)),
            pl.BlockSpec((plan.rows, plan.width), lambda j: (sub, j)),
            whole(norms),
            whole(w_t),
        ]
        + [HELD for _ in before],
        out_specs=out_specs,
        out_shape=out_shape,
        input_output_aliases={4: 0} if before else {},
        scratch_shapes=[plan.scratch(hidden)] * 2,
        compiler_params=params(1),
        cost_estimate=cost(0.2),
        name="factors",
    )(x, mask, norms, w_t, *before)


def matrix(refs, chan):
    parts = [ref[:, chan].reshape(-1, ref.shape[-1]) for ref in refs]
    return jnp.concatenate(parts, axis=0) if len(parts) > 1 else parts[0]


def by_sub(ref, chan, subs):
    rows = ref.shape[2] // subs
    parts = [
        ref[:, chan, sub * rows : (sub + 1) * rows, :].reshape(-1, ref.shape[3])
        for sub in range(subs)
    ]
    return jnp.concatenate(parts, axis=0) if subs > 1 else parts[0]


def to_subs(ref, chan, value, subs, rows):
    part = value.shape[0] // subs
    for sub in range(subs):
        ref[:, chan, sub * rows : (sub + 1) * rows, :] = value[
            sub * part : (sub + 1) * part
        ].astype(BF16).reshape(ref.shape[0], rows, ref.shape[3])


def own_spec(array):
    src, _, rows, cols = array.shape
    return pl.BlockSpec((src, CHANS, rows, cols), lambda h: (0, h, 0, 0))


def view_spec(plan, view):
    array, at = view
    return pl.BlockSpec((array.shape[0], CHANS, plan.rows, array.shape[3]), lambda h: (0, h, at, 0))


def arrays(views):
    return [array for array, _ in views]


def product_kernel(subs, rows, *refs):
    a, b, p_ref = refs[:subs], refs[subs:-1], refs[-1]
    for chan in range(CHANS):
        to_subs(p_ref, chan, dot(matrix(a, chan), matrix(b, chan), NT), subs, rows)


def make_product(plan, a, b):
    tiles, chans = a[0][0].shape[:2]
    cols = sum(array.shape[0] for array in arrays(b)) * plan.rows
    out = jax.ShapeDtypeStruct((tiles, chans, plan.count, cols), BF16)
    return pl.pallas_call(
        functools.partial(product_kernel, plan.subs, plan.rows),
        grid=(chans // CHANS,),
        in_specs=[view_spec(plan, view) for view in (*a, *b)],
        out_specs=own_spec(out),
        out_shape=out,
        compiler_params=params(1),
        cost_estimate=cost(0.2),
        name="product",
    )(*arrays(a), *arrays(b))


def grad_b_kernel(subs, g_ref, *refs):
    a, outs = refs[:subs], refs[subs:]
    for chan in range(CHANS):
        grad = dot(by_sub(g_ref, chan, subs), matrix(a, chan), TN).astype(BF16)
        at = 0
        for out in outs:
            size = out.shape[0] * out.shape[2]
            out[:, chan] = grad[at : at + size].reshape(out.shape[0], *out.shape[2:])
            at += size


def make_grad_b(plan, g, a, tiles):
    outs = [
        jax.ShapeDtypeStruct((count, g.shape[1], plan.rows, plan.crop), BF16) for count in tiles
    ]
    return pl.pallas_call(
        functools.partial(grad_b_kernel, plan.subs),
        grid=(g.shape[1] // CHANS,),
        in_specs=[own_spec(g)] + [view_spec(plan, view) for view in a],
        out_specs=[own_spec(value) for value in outs],
        out_shape=outs,
        compiler_params=params(1),
        cost_estimate=cost(0.2),
        name="grad_b",
    )(g, *arrays(a))


def grad_a_kernel(subs, rows, counts, *refs):
    g, b = refs[: counts[0]], refs[counts[0] : counts[0] + counts[1]]
    own, back, out = refs[counts[0] + counts[1]], refs[counts[0] + counts[1] + 1 : -1], refs[-1]
    for chan in range(CHANS):
        left = jnp.concatenate([by_sub(ref, chan, subs) for ref in g], axis=1)
        to_subs(out, chan, dot(left, matrix(b, chan)), subs, rows)
        at = 0
        for piece in back:
            end = at + piece.shape[0]
            added = own[at:end, chan].astype(F32) + piece[:, chan].astype(F32)
            out[at:end, chan, subs * rows :, :] = added.astype(BF16)
            at = end


def make_grad_a(plan, g, b, own, back):
    chans = own.shape[1]
    out = jax.ShapeDtypeStruct((plan.half, chans, plan.count + plan.rows, plan.crop), BF16)
    return pl.pallas_call(
        functools.partial(grad_a_kernel, plan.subs, plan.rows, (len(g), len(b))),
        grid=(chans // CHANS,),
        in_specs=[own_spec(value) for value in g]
        + [view_spec(plan, view) for view in b]
        + [own_spec(value) for value in (own, *back)],
        out_specs=own_spec(out),
        out_shape=out,
        compiler_params=params(1),
        cost_estimate=cost(0.2),
        name="grad_a",
    )(*g, *arrays(b), own, *back)


def middle_kernel(
    step, _, x_ref, d_ref, p_ref, norm_ref, wg_ref, wo_ref, wot_ref, *refs
):
    g_ref, gb_ref, gwo_ref, gwg_ref, s_ref = refs[-5:]
    rows = x_ref.shape[0]
    width = gb_ref.shape[-1]

    @pl.when((pl.program_id(0) == 0) & (pl.program_id(1) == 0))
    def _():
        gwo_ref[...] = jnp.zeros_like(gwo_ref)
        gwg_ref[...] = jnp.zeros_like(gwg_ref)

    spread_in(p_ref, s_ref)

    @pl.loop(0, rows // step, unroll=min(4, rows // step))
    def _(turn):
        row = pl.multiple_of(turn * step, step)
        z_hat, _ = stats(turned(x_ref, row, step))
        normed = (z_hat * norm_ref[:, 0:1] + norm_ref[:, 1:2]).astype(BF16)
        gate = sigmoid(dot(wg_ref[...], normed))
        x_hat, inv_std = stats(load_rows(s_ref, row, step, rows))
        x_norm = (x_hat * norm_ref[:, 2:3] + norm_ref[:, 3:4]).astype(BF16)
        out_lin = dot(wot_ref[...], x_norm)
        lin = turned(d_ref, row, step) * gate
        grad_lin = lin.astype(BF16)
        gate_back = (lin * out_lin * (1.0 - gate)).astype(BF16)
        upstream = dot(wo_ref[...], grad_lin) * norm_ref[:, 2:3]
        store_rows(s_ref, row, step, rows, norm_back(upstream, x_hat, inv_std))
        for at in range(step):
            gb_ref[row + at] = gate_back[:, at * width : (at + 1) * width]
        gwo_ref[...] += dot(x_norm, grad_lin, NT)
        gwg_ref[...] += dot(normed, gate_back, NT)

    gather_out(s_ref, g_ref, rows)


def make_middle(plan, table, first, before, ready, x, d, p, small):
    chans = x.shape[-1]
    hidden = p.shape[0]
    cut = table.shape[0]
    grads = [jax.ShapeDtypeStruct((hidden, chans), F32), jax.ShapeDtypeStruct((chans, chans), F32)]
    pairs = plan.pair_spec(chans, lambda i, j, at: (i, at[j, 0], at[j, 1], 0, 0))
    channel = (hidden, plan.rows, plan.width)
    kept = [*before, *ready]
    return pl.pallas_call(
        functools.partial(middle_kernel, plan.step),
        grid_spec=pltpu.PrefetchScalarGridSpec(
            num_scalar_prefetch=1,
            grid=(plan.subs, cut),
            in_specs=[pairs, pairs, pl.BlockSpec(channel, lambda i, j, at: (0, i, first + j))]
            + [whole(value) for value in small]
            + [HELD for _ in kept],
            out_specs=[
                pl.BlockSpec(channel, lambda i, j, at: (0, i, j)),
                pl.BlockSpec(
                    (plan.rows, chans, plan.width),
                    lambda i, j, at: (i, 0, at[j, 1] * 2 + at[j, 0]),
                ),
            ]
            + [whole(value) for value in grads],
            scratch_shapes=[plan.scratch(hidden)],
        ),
        out_shape=[
            jax.ShapeDtypeStruct((hidden, plan.count, cut * plan.width), BF16),
            jax.ShapeDtypeStruct((plan.count, chans, plan.crop), BF16),
        ]
        + grads,
        input_output_aliases={4 + len(small): 1} if before else {},
        compiler_params=params(2),
        cost_estimate=cost(0.2),
        name="middle",
    )(table, x, d, p, *small, *kept)


def last_kernel(step, mode, *refs):
    sides, gated, based, out_kind, summed = MODES[mode]
    scratches, rest = refs[-len(sides) :], iter(refs[: -len(sides)])
    x_ref, mask_ref = next(rest), next(rest)
    grads = [next(rest) for _ in sides]
    gate_ref = next(rest) if gated else None
    base_ref = next(rest) if based else None
    norm_ref, wt_ref, wcat_ref, *outs = rest
    gw_ref = outs[-1]
    out_ref = outs[-1 - summed] if out_kind else None
    rows, _, _, _, _ = x_ref.shape
    hidden = grads[0].shape[0]
    width = mask_ref.shape[1]

    if summed:

        @pl.when(pl.program_id(0) == 0)
        def _():
            gw_ref[...] = jnp.zeros_like(gw_ref)

    for ref, scratch in zip(grads, scratches):
        spread_in(ref, scratch)

    @pl.loop(0, rows // step, unroll=min(4, rows // step))
    def _(turn):
        row = pl.multiple_of(turn * step, step)
        z_hat, inv_in = stats(turned(x_ref, row, step))
        normed = (z_hat * norm_ref[:, 0:1] + norm_ref[:, 1:2]).astype(BF16)
        mask = flat_rows(mask_ref, row, step)
        proj = dot(wt_ref[...], normed)
        parts = []
        for side, scratch in enumerate(scratches):
            value = proj[2 * side * hidden : (2 * side + 1) * hidden]
            sig = sigmoid(proj[(2 * side + 1) * hidden : (2 * side + 2) * hidden])
            to_value = load_rows(scratch, row, step, rows) * mask * sig
            parts += [to_value.astype(BF16), (to_value * value * (1.0 - sig)).astype(BF16)]
        grad_proj = jnp.concatenate(parts, axis=0)
        if summed:
            gw_ref[...] += dot(normed, grad_proj, NT)
        if out_kind:
            every = grad_proj
            if gated:
                gate_back = jnp.concatenate([gate_ref[row + at] for at in range(step)], axis=1)
                every = jnp.concatenate([grad_proj, gate_back], axis=0)
            upstream = dot(wcat_ref[...], every)
            if based:
                upstream += jnp.concatenate(
                    [base_ref[row + at].astype(F32) for at in range(step)], axis=1
                )
            if out_kind == "pair":
                grad = norm_back(upstream * norm_ref[:, 0:1], z_hat, inv_in).T.astype(BF16)
                out_ref[pl.ds(row, step)] = grad.reshape((step,) + out_ref.shape[1:])
            else:
                for at in range(step):
                    out_ref[row + at] = upstream[:, at * width : (at + 1) * width].astype(BF16)


MODES = {
    "both": ((0, 1), True, False, "pair", True),
    "a": ((0,), True, False, "base", True),
    "b_sum": ((1,), False, False, "", True),
    "b": ((1,), False, True, "pair", False),
}


def make_last(plan, mode, sub, before, x, mask, grads, extra, small):
    sides, gated, based, out_kind, summed = MODES[mode]
    chans = x.shape[-1]
    hidden = grads[0][0].shape[0]
    grad = jax.ShapeDtypeStruct((chans, 2 * len(sides) * hidden), F32)
    pairs = plan.pair_spec(chans, lambda j: (sub, j % 2, j // 2, 0, 0))
    channel = (hidden, plan.rows, plan.width)
    lines = (plan.rows, chans, plan.width)
    kept = [] if before is None else [before]
    in_specs = [pairs, pl.BlockSpec((plan.rows, plan.width), lambda j: (sub, j))]
    for _, at in grads:
        in_specs.append(pl.BlockSpec(channel, lambda j, at=at: (0, at, j)))
    if gated:
        in_specs.append(pl.BlockSpec(lines, lambda j: (sub, 0, j)))
    if based:
        in_specs.append(pl.BlockSpec(lines, lambda j: (0, 0, j)))
    out_specs, out_shape = [], []
    if out_kind == "pair":
        out_specs.append(pairs)
        out_shape.append(jax.ShapeDtypeStruct(x.shape, BF16))
    if out_kind == "base":
        out_specs.append(pl.BlockSpec(lines, lambda j: (0, 0, j)))
        out_shape.append(jax.ShapeDtypeStruct((plan.rows, chans, plan.crop), BF16))
    if summed:
        out_specs.append(whole(grad))
        out_shape.append(grad)
    operands = [x, mask, *arrays(grads), *extra, *small]
    in_specs += [whole(value) for value in small]
    return pl.pallas_call(
        functools.partial(last_kernel, plan.step, mode),
        grid=(plan.blocks,),
        in_specs=in_specs + [HELD for _ in kept],
        out_specs=out_specs,
        out_shape=out_shape,
        scratch_shapes=[plan.scratch(hidden)] * len(sides),
        input_output_aliases={len(operands): 0} if kept else {},
        compiler_params=params(1),
        cost_estimate=cost(0.2),
        name="last_" + mode,
    )(*operands, *kept)


def swap_all(array):
    return lax.all_to_all(array, "tile", split_axis=0, concat_axis=0, tiled=True)


def tile_sum(array, tiles, ready):
    chans, width = array.shape
    parts = swap_all(array.astype(BF16)).reshape(tiles, chans // tiles, width)
    part = jnp.sum(parts.astype(F32), axis=0).astype(BF16)
    spread = jnp.broadcast_to(part[None], (tiles,) + part.shape).reshape(chans, width)
    return swap_all(after(spread, ready)).astype(F32)


def body(
    tiles, x, d, token_mask, ln_in_gain, ln_in_bias, w_ab, w_gate, ln_out_gain, ln_out_bias, w_out
):
    count, crop, chans = x.shape
    hidden = w_out.shape[0]
    plan = Plan(tiles, count, crop)
    me = lax.axis_index("tile")
    side = (me // plan.half).astype(jnp.int32)
    valid = token_mask.astype(F32)
    own_valid = lax.dynamic_slice_in_dim(valid, me * count, count)
    turned_valid = valid.reshape(tiles, plan.subs, plan.rows).transpose(1, 0, 2).reshape(crop)
    mask = own_valid[:, None] * turned_valid[None, :]
    norms = jnp.stack([ln_in_gain, ln_in_bias, ln_out_gain, ln_out_bias], axis=1)
    w_t = w_ab.T
    w_cat = jnp.concatenate([w_ab, w_gate], axis=1)
    mid = [norms, w_gate.T, w_out, w_out.T]
    x, d = plan.view(x), plan.view(d)
    owned = lambda array: array.reshape(plan.half, hidden // plan.half, *array.shape[1:])
    joined = lambda array: array.reshape(hidden, *array.shape[2:])
    every = range(plan.subs)

    plan_cut = plan.cut
    two = plan.subs == 2
    cut_b, back_a = plan_cut(6, 2), plan_cut(3, 3, 2)
    small = [norms, w_t, w_cat]

    def middle(at, first, before, ready, product):
        table = jnp.stack([jnp.stack([half, jnp.int32(sub)]) for half, sub in at])
        g, kept, *local = make_middle(plan, table, first, before, ready, x, d, product, mid)
        return g, kept, jnp.concatenate(local[::-1], axis=1)

    def product_of(b):
        return plan.swap(joined(make_product(plan, own_a, b)))

    held, factor_b0 = make_factors(plan, 0, (), x, mask, norms, w_t)
    own_b0 = owned(plan.swap(factor_b0))
    if two:
        (held,) = make_factors(plan, 1, (held,), x, mask, norms, w_t)
    other_0 = plan.exchange(own_b0)
    own_ab = owned(plan.swap(after(held, own_b0)))
    own_a, own_b, got_b = [(own_ab, 0)], [(own_b0, 0)], []
    if two:
        own_a, own_b = [(own_ab, 2), (own_ab, 0)], [(own_b0, 0), (own_ab, 1)]
        sent = plan.pieces(own_ab[:, :, plan.rows : 2 * plan.rows], cut_b)
        got_b = [plan.exchange(sent[0])]
    b_first = [(other_0, 0)] + own_b
    product = product_of(b_first)
    if two:
        got_b.append(plan.exchange(after(sent[1], product)))
    grad, kept, local_mid = middle([(1 - side, 0)], 0, (), (), product)
    owner_g = [owned(plan.swap(after(grad, *got_b[:1])))]
    grad, kept, local = middle([(side, sub) for sub in every], 1, (kept,), (), product)
    local_mid += local
    grad_b0 = make_grad_b(plan, owner_g[0], own_a, back_a)
    back_0 = [plan.exchange(piece) for piece in grad_b0]
    waits = (owner_g[0], grad_b0[0])
    if two:
        b_second = [(piece, 0) for piece in got_b]
        b_first = b_first + b_second
        product = plan.swap(after(joined(make_product(plan, own_a, b_second)), *waits))
        waits = (product, back_0[0])
    owner_g.append(owned(plan.swap(after(grad, *waits))))
    grad_b_own = make_grad_b(plan, owner_g[1], own_a, [plan.half] * plan.subs)
    if two:
        grad, kept, local = middle([(1 - side, 1)], 0, (kept,), (), product)
        local_mid += local
        grad = plan.swap(after(grad, owner_g[1], back_0[1]))
        owner_g.append(after(owned(grad), grad_b_own[0]))
        (grad_b1,) = make_grad_b(plan, owner_g[2], own_a, [plan.half])
        back_1 = plan.exchange(grad_b1)
        back_0[2] = after(back_0[2], grad_b1)
    grads = plan.swap(joined(make_grad_a(plan, owner_g, b_first, grad_b_own[0], back_0)))
    first, second = w_ab[:, : 2 * hidden], w_ab[:, 2 * hidden :]
    pair_grad, local_ab = make_last(
        plan, "both", 0, None, x, mask, [(grads, 0), (grads, plan.subs)], [kept], small
    )
    if two:
        back_1 = after(back_1, grads)
        grad_b = plan.swap(
            joined((grad_b_own[1].astype(F32) + back_1.astype(F32)).astype(BF16))
        )
        side_a = [norms, w_t[: 2 * hidden], jnp.concatenate([first, w_gate], axis=1)]
        side_b = [norms, w_t[2 * hidden :], second]
        base, local_a = make_last(plan, "a", 1, None, x, mask, [(grads, 1)], [kept], side_a)
        grad_b = after(grad_b, local_ab, local_a)
        (local_b,) = make_last(plan, "b_sum", 1, None, x, mask, [(grad_b, 0)], [], side_b)
        (pair_grad,) = make_last(
            plan, "b", 1, pair_grad, x, mask, [(grad_b, 0)], [base], side_b
        )
        local_ab += jnp.concatenate([local_a, local_b], axis=1)
    total = tile_sum(jnp.concatenate([local_ab, local_mid], axis=1), tiles, pair_grad) / crop
    wide = 4 * hidden
    return (
        pair_grad.reshape(count, crop, chans),
        total[:, :wide],
        total[:, wide : wide + chans],
        total[:, wide + chans :],
    )


def solution(mesh):
    pairs = P(("crops", "tile"), None, None)
    return jax.shard_map(
        functools.partial(body, mesh.shape["tile"]),
        mesh=mesh,
        in_specs=(pairs, pairs, P("crops")) + (P(),) * 7,
        out_specs=(pairs,) + (P("crops", None),) * 3,
        check_vma=False,
    )
```

```python
import functools

import jax
import jax.numpy as jnp
from jax import lax
from jax.experimental import pallas as pl
from jax.experimental.pallas import tpu as pltpu
from jax.sharding import PartitionSpec as P

HELD = pl.BlockSpec(memory_space=pl.ANY)
EPS = 1e-05
CHANS = 8
F32 = jnp.float32
BF16 = jnp.bfloat16
NN = (((1,), (0,)), ((), ()))
NT = (((1,), (1,)), ((), ()))
TN = (((0,), (0,)), ((), ()))


def params(steps):
    return pltpu.CompilerParams(
        dimension_semantics=("arbitrary",) * steps, vmem_limit_bytes=50 * 1024 * 1024
    )


def cost(micros):
    return pl.CostEstimate(
        flops=int(micros * 1.0e9), bytes_accessed=int(micros * 3.0e6), transcendentals=0
    )


def dot(left, right, form=NN):
    return lax.dot_general(left, right, form, preferred_element_type=F32)


def sigmoid(value):
    return 0.5 * jnp.tanh(0.5 * value) + 0.5


def col_mean(value):
    return jnp.mean(value, axis=0, keepdims=True)


def stats(value):
    centered = value - col_mean(value)
    inv_std = lax.rsqrt(col_mean(centered * centered) + EPS)
    return centered * inv_std, inv_std


def norm_back(upstream, scaled, inv_std):
    return inv_std * (upstream - col_mean(upstream) - scaled * col_mean(upstream * scaled))


def turned(ref, row, count):
    block = ref[pl.ds(row, count)]
    return block.reshape(-1, block.shape[-1]).astype(F32).T


def lane_parts(scratch, count):
    return [(at, lane) for at in range(count) for lane in range(scratch.shape[0])]


def store_rows(scratch, row, count, rows, value):
    hidden = value.shape[0]
    for part, (at, lane) in enumerate(lane_parts(scratch, count)):
        scratch[lane, pl.ds(row + at, hidden, stride=rows), :] = value[:, part * 128 : (part + 1) * 128]


def load_rows(scratch, row, count, rows):
    hidden = scratch.shape[1] // rows
    return jnp.concatenate(
        [
            scratch[lane, pl.ds(row + at, hidden, stride=rows), :]
            for at, lane in lane_parts(scratch, count)
        ],
        axis=1,
    )


def gather_out(scratch, out_ref, rows, at=0):
    hidden = out_ref.shape[0]
    for lane in range(scratch.shape[0]):
        out_ref[:, at : at + rows, lane * 128 : (lane + 1) * 128] = (
            scratch[lane].reshape(hidden, rows, 128).astype(BF16)
        )


def spread_in(in_ref, scratch):
    hidden, rows, cols = in_ref.shape
    for lane in range(scratch.shape[0]):
        scratch[lane] = (
            in_ref[:, :, lane * 128 : (lane + 1) * 128].astype(F32).reshape(hidden * rows, 128)
        )


def flat_rows(ref, row, count):
    return jnp.concatenate([ref[pl.ds(row + at, 1), :] for at in range(count)], axis=1)


def whole(array):
    return pl.BlockSpec(array.shape, lambda *_: (0,) * array.ndim)


class Plan:
    def __init__(self, tiles, count, crop):
        self.tiles, self.count, self.crop = tiles, count, crop
        self.half = tiles // 2
        self.subs = 2 if count % 32 == 0 else 1
        self.rows = count // self.subs
        self.width = self.half * self.rows
        self.blocks = crop // self.width
        self.step = max(1, 512 // self.width)
        self.groups = [
            [side * self.half + at for at in range(self.half)] for side in range(2)
        ]
        self.partner = [(at, (at + self.half) % tiles) for at in range(tiles)]

    def view(self, array):
        return array.reshape(self.count, self.tiles, self.subs, self.rows, array.shape[-1])

    def pair_spec(self, chans, index):
        return pl.BlockSpec((self.rows, self.half, 1, self.rows, chans), index)

    def scratch(self, hidden):
        return pltpu.VMEM((self.width // 128, self.rows * hidden, 128), F32)

    def swap(self, array):
        return lax.all_to_all(
            array, "tile", split_axis=0, concat_axis=0, axis_index_groups=self.groups, tiled=True
        )

    def cut(self, *eighths):
        return [max(1, self.half * share // 8) for share in eighths]

    def pieces(self, array, counts):
        ends = [sum(counts[: at + 1]) for at in range(len(counts))]
        return [array[end - size : end] for size, end in zip(counts, ends)]

    def exchange(self, array):
        return lax.ppermute(array, "tile", self.partner)


def after_kernel(*refs):
    del refs


def after(value, *others):
    return pl.pallas_call(
        after_kernel,
        in_specs=[HELD] * (1 + len(others)),
        out_specs=HELD,
        out_shape=jax.ShapeDtypeStruct(value.shape, value.dtype),
        input_output_aliases={0: 0},
        compiler_params=params(0),
        cost_estimate=cost(0.1),
        name="after",
    )(value, *others)


def factors_kernel(step, joint, x_ref, mask_ref, norm_ref, w_ref, *refs):
    sa_ref, sb_ref = refs[-2:]
    rows = x_ref.shape[0]
    hidden = w_ref.shape[0] // 4

    @pl.loop(0, rows // step, unroll=min(4, rows // step))
    def _(turn):
        row = pl.multiple_of(turn * step, step)
        z_hat, _ = stats(turned(x_ref, row, step))
        normed = (z_hat * norm_ref[:, 0:1] + norm_ref[:, 1:2]).astype(BF16)
        mask = flat_rows(mask_ref, row, step)
        proj = dot(w_ref[...], normed)
        value_a, gate_a = proj[:hidden], proj[hidden : 2 * hidden]
        value_b, gate_b = proj[2 * hidden : 3 * hidden], proj[3 * hidden :]
        store_rows(sb_ref, row, step, rows, mask * sigmoid(gate_b) * value_b)
        store_rows(sa_ref, row, step, rows, mask * sigmoid(gate_a) * value_a)

    if joint:
        gather_out(sa_ref, refs[-3], rows)
        gather_out(sb_ref, refs[-3], rows, rows)
    else:
        gather_out(sa_ref, refs[-4], rows)
        gather_out(sb_ref, refs[-3], rows)


def make_factors(plan, sub, before, x, mask, norms, w_t):
    chans = x.shape[-1]
    hidden = w_t.shape[0] // 4
    block = (hidden, plan.rows, plan.width)
    held = plan.rows * (3 if plan.subs == 2 else 1)
    out_specs = [
        pl.BlockSpec(block, lambda j: (0, 2 * (plan.subs - 1), j)),
        pl.BlockSpec(block, lambda j: (0, 0, j)),
    ]
    out_shape = [
        jax.ShapeDtypeStruct((hidden, held, plan.crop), BF16),
        jax.ShapeDtypeStruct((hidden, plan.rows, plan.crop), BF16),
    ]
    if before:
        out_specs = [pl.BlockSpec((hidden, 2 * plan.rows, plan.width), lambda j: (0, 0, j))]
        out_shape = out_shape[:1]
    return pl.pallas_call(
        functools.partial(factors_kernel, plan.step, bool(before)),
        grid=(plan.blocks,),
        in_specs=[
            plan.pair_spec(chans, lambda j: (sub, j % 2, j // 2, 0, 0)),
            pl.BlockSpec((plan.rows, plan.width), lambda j: (sub, j)),
            whole(norms),
            whole(w_t),
        ]
        + [HELD for _ in before],
        out_specs=out_specs,
        out_shape=out_shape,
        input_output_aliases={4: 0} if before else {},
        scratch_shapes=[plan.scratch(hidden)] * 2,
        compiler_params=params(1),
        cost_estimate=cost(0.2),
        name="factors",
    )(x, mask, norms, w_t, *before)


def matrix(refs, chan):
    parts = [ref[:, chan].reshape(-1, ref.shape[-1]) for ref in refs]
    return jnp.concatenate(parts, axis=0) if len(parts) > 1 else parts[0]


def by_sub(ref, chan, subs):
    rows = ref.shape[2] // subs
    parts = [
        ref[:, chan, sub * rows : (sub + 1) * rows, :].reshape(-1, ref.shape[3])
        for sub in range(subs)
    ]
    return jnp.concatenate(parts, axis=0) if subs > 1 else parts[0]


def to_subs(ref, chan, value, subs, rows):
    part = value.shape[0] // subs
    for sub in range(subs):
        ref[:, chan, sub * rows : (sub + 1) * rows, :] = value[
            sub * part : (sub + 1) * part
        ].astype(BF16).reshape(ref.shape[0], rows, ref.shape[3])


def own_spec(array):
    src, _, rows, cols = array.shape
    return pl.BlockSpec((src, CHANS, rows, cols), lambda h: (0, h, 0, 0))


def view_spec(plan, view):
    array, at = view
    return pl.BlockSpec((array.shape[0], CHANS, plan.rows, array.shape[3]), lambda h: (0, h, at, 0))


def arrays(views):
    return [array for array, _ in views]


def product_kernel(subs, rows, *refs):
    a, b, p_ref = refs[:subs], refs[subs:-1], refs[-1]
    for chan in range(CHANS):
        to_subs(p_ref, chan, dot(matrix(a, chan), matrix(b, chan), NT), subs, rows)


def make_product(plan, a, b):
    tiles, chans = a[0][0].shape[:2]
    cols = sum(array.shape[0] for array in arrays(b)) * plan.rows
    out = jax.ShapeDtypeStruct((tiles, chans, plan.count, cols), BF16)
    return pl.pallas_call(
        functools.partial(product_kernel, plan.subs, plan.rows),
        grid=(chans // CHANS,),
        in_specs=[view_spec(plan, view) for view in (*a, *b)],
        out_specs=own_spec(out),
        out_shape=out,
        compiler_params=params(1),
        cost_estimate=cost(0.2),
        name="product",
    )(*arrays(a), *arrays(b))


def grad_b_kernel(subs, g_ref, *refs):
    a, outs = refs[:subs], refs[subs:]
    for chan in range(CHANS):
        grad = dot(by_sub(g_ref, chan, subs), matrix(a, chan), TN).astype(BF16)
        at = 0
        for out in outs:
            size = out.shape[0] * out.shape[2]
            out[:, chan] = grad[at : at + size].reshape(out.shape[0], *out.shape[2:])
            at += size


def make_grad_b(plan, g, a, tiles):
    outs = [
        jax.ShapeDtypeStruct((count, g.shape[1], plan.rows, plan.crop), BF16) for count in tiles
    ]
    return pl.pallas_call(
        functools.partial(grad_b_kernel, plan.subs),
        grid=(g.shape[1] // CHANS,),
        in_specs=[own_spec(g)] + [view_spec(plan, view) for view in a],
        out_specs=[own_spec(value) for value in outs],
        out_shape=outs,
        compiler_params=params(1),
        cost_estimate=cost(0.2),
        name="grad_b",
    )(g, *arrays(a))


def grad_a_kernel(subs, rows, counts, *refs):
    g, b = refs[: counts[0]], refs[counts[0] : counts[0] + counts[1]]
    own, back, out = refs[counts[0] + counts[1]], refs[counts[0] + counts[1] + 1 : -1], refs[-1]
    for chan in range(CHANS):
        left = jnp.concatenate([by_sub(ref, chan, subs) for ref in g], axis=1)
        to_subs(out, chan, dot(left, matrix(b, chan)), subs, rows)
        at = 0
        for piece in back:
            end = at + piece.shape[0]
            added = own[at:end, chan].astype(F32) + piece[:, chan].astype(F32)
            out[at:end, chan, subs * rows :, :] = added.astype(BF16)
            at = end


def make_grad_a(plan, g, b, own, back):
    chans = own.shape[1]
    out = jax.ShapeDtypeStruct((plan.half, chans, plan.count + plan.rows, plan.crop), BF16)
    return pl.pallas_call(
        functools.partial(grad_a_kernel, plan.subs, plan.rows, (len(g), len(b))),
        grid=(chans // CHANS,),
        in_specs=[own_spec(value) for value in g]
        + [view_spec(plan, view) for view in b]
        + [own_spec(value) for value in (own, *back)],
        out_specs=own_spec(out),
        out_shape=out,
        compiler_params=params(1),
        cost_estimate=cost(0.2),
        name="grad_a",
    )(*g, *arrays(b), own, *back)


def middle_kernel(
    step, _, x_ref, d_ref, p_ref, norm_ref, wg_ref, wo_ref, wot_ref, *refs
):
    g_ref, gb_ref, gwo_ref, gwg_ref, s_ref = refs[-5:]
    rows = x_ref.shape[0]
    width = gb_ref.shape[-1]

    @pl.when((pl.program_id(0) == 0) & (pl.program_id(1) == 0))
    def _():
        gwo_ref[...] = jnp.zeros_like(gwo_ref)
        gwg_ref[...] = jnp.zeros_like(gwg_ref)

    spread_in(p_ref, s_ref)

    @pl.loop(0, rows // step, unroll=min(4, rows // step))
    def _(turn):
        row = pl.multiple_of(turn * step, step)
        z_hat, _ = stats(turned(x_ref, row, step))
        normed = (z_hat * norm_ref[:, 0:1] + norm_ref[:, 1:2]).astype(BF16)
        gate = sigmoid(dot(wg_ref[...], normed))
        x_hat, inv_std = stats(load_rows(s_ref, row, step, rows))
        x_norm = (x_hat * norm_ref[:, 2:3] + norm_ref[:, 3:4]).astype(BF16)
        out_lin = dot(wot_ref[...], x_norm)
        lin = turned(d_ref, row, step) * gate
        grad_lin = lin.astype(BF16)
        gate_back = (lin * out_lin * (1.0 - gate)).astype(BF16)
        upstream = dot(wo_ref[...], grad_lin) * norm_ref[:, 2:3]
        store_rows(s_ref, row, step, rows, norm_back(upstream, x_hat, inv_std))
        for at in range(step):
            gb_ref[row + at] = gate_back[:, at * width : (at + 1) * width]
        gwo_ref[...] += dot(x_norm, grad_lin, NT)
        gwg_ref[...] += dot(normed, gate_back, NT)

    gather_out(s_ref, g_ref, rows)


def make_middle(plan, table, first, before, ready, x, d, p, small):
    chans = x.shape[-1]
    hidden = p.shape[0]
    cut = table.shape[0]
    grads = [jax.ShapeDtypeStruct((hidden, chans), F32), jax.ShapeDtypeStruct((chans, chans), F32)]
    pairs = plan.pair_spec(chans, lambda i, j, at: (i, at[j, 0], at[j, 1], 0, 0))
    channel = (hidden, plan.rows, plan.width)
    kept = [*before, *ready]
    return pl.pallas_call(
        functools.partial(middle_kernel, plan.step),
        grid_spec=pltpu.PrefetchScalarGridSpec(
            num_scalar_prefetch=1,
            grid=(plan.subs, cut),
            in_specs=[pairs, pairs, pl.BlockSpec(channel, lambda i, j, at: (0, i, first + j))]
            + [whole(value) for value in small]
            + [HELD for _ in kept],
            out_specs=[
                pl.BlockSpec(channel, lambda i, j, at: (0, i, j)),
                pl.BlockSpec(
                    (plan.rows, chans, plan.width),
                    lambda i, j, at: (i, 0, at[j, 1] * 2 + at[j, 0]),
                ),
            ]
            + [whole(value) for value in grads],
            scratch_shapes=[plan.scratch(hidden)],
        ),
        out_shape=[
            jax.ShapeDtypeStruct((hidden, plan.count, cut * plan.width), BF16),
            jax.ShapeDtypeStruct((plan.count, chans, plan.crop), BF16),
        ]
        + grads,
        input_output_aliases={4 + len(small): 1} if before else {},
        compiler_params=params(2),
        cost_estimate=cost(0.2),
        name="middle",
    )(table, x, d, p, *small, *kept)


def last_kernel(step, mode, *refs):
    sides, gated, based, out_kind, summed = MODES[mode]
    scratches, rest = refs[-len(sides) :], iter(refs[: -len(sides)])
    x_ref, mask_ref = next(rest), next(rest)
    grads = [next(rest) for _ in sides]
    gate_ref = next(rest) if gated else None
    base_ref = next(rest) if based else None
    norm_ref, wt_ref, wcat_ref, *outs = rest
    gw_ref = outs[-1]
    out_ref = outs[-1 - summed] if out_kind else None
    rows, _, _, _, _ = x_ref.shape
    hidden = grads[0].shape[0]
    width = mask_ref.shape[1]

    if summed:

        @pl.when(pl.program_id(0) == 0)
        def _():
            gw_ref[...] = jnp.zeros_like(gw_ref)

    for ref, scratch in zip(grads, scratches):
        spread_in(ref, scratch)

    @pl.loop(0, rows // step, unroll=min(4, rows // step))
    def _(turn):
        row = pl.multiple_of(turn * step, step)
        z_hat, inv_in = stats(turned(x_ref, row, step))
        normed = (z_hat * norm_ref[:, 0:1] + norm_ref[:, 1:2]).astype(BF16)
        mask = flat_rows(mask_ref, row, step)
        proj = dot(wt_ref[...], normed)
        parts = []
        for side, scratch in enumerate(scratches):
            value = proj[2 * side * hidden : (2 * side + 1) * hidden]
            sig = sigmoid(proj[(2 * side + 1) * hidden : (2 * side + 2) * hidden])
            to_value = load_rows(scratch, row, step, rows) * mask * sig
            parts += [to_value.astype(BF16), (to_value * value * (1.0 - sig)).astype(BF16)]
        grad_proj = jnp.concatenate(parts, axis=0)
        if summed:
            gw_ref[...] += dot(normed, grad_proj, NT)
        if out_kind:
            every = grad_proj
            if gated:
                gate_back = jnp.concatenate([gate_ref[row + at] for at in range(step)], axis=1)
                every = jnp.concatenate([grad_proj, gate_back], axis=0)
            upstream = dot(wcat_ref[...], every)
            if based:
                upstream += jnp.concatenate(
                    [base_ref[row + at].astype(F32) for at in range(step)], axis=1
                )
            if out_kind == "pair":
                grad = norm_back(upstream * norm_ref[:, 0:1], z_hat, inv_in).T.astype(BF16)
                out_ref[pl.ds(row, step)] = grad.reshape((step,) + out_ref.shape[1:])
            else:
                for at in range(step):
                    out_ref[row + at] = upstream[:, at * width : (at + 1) * width].astype(BF16)


MODES = {
    "both": ((0, 1), True, False, "pair", True),
    "a": ((0,), True, False, "base", True),
    "b_sum": ((1,), False, False, "", True),
    "b": ((1,), False, True, "pair", False),
}


def make_last(plan, mode, sub, before, x, mask, grads, extra, small):
    sides, gated, based, out_kind, summed = MODES[mode]
    chans = x.shape[-1]
    hidden = grads[0][0].shape[0]
    grad = jax.ShapeDtypeStruct((chans, 2 * len(sides) * hidden), F32)
    pairs = plan.pair_spec(chans, lambda j: (sub, j % 2, j // 2, 0, 0))
    channel = (hidden, plan.rows, plan.width)
    lines = (plan.rows, chans, plan.width)
    kept = [] if before is None else [before]
    in_specs = [pairs, pl.BlockSpec((plan.rows, plan.width), lambda j: (sub, j))]
    for _, at in grads:
        in_specs.append(pl.BlockSpec(channel, lambda j, at=at: (0, at, j)))
    if gated:
        in_specs.append(pl.BlockSpec(lines, lambda j: (sub, 0, j)))
    if based:
        in_specs.append(pl.BlockSpec(lines, lambda j: (0, 0, j)))
    out_specs, out_shape = [], []
    if out_kind == "pair":
        out_specs.append(pairs)
        out_shape.append(jax.ShapeDtypeStruct(x.shape, BF16))
    if out_kind == "base":
        out_specs.append(pl.BlockSpec(lines, lambda j: (0, 0, j)))
        out_shape.append(jax.ShapeDtypeStruct((plan.rows, chans, plan.crop), BF16))
    if summed:
        out_specs.append(whole(grad))
        out_shape.append(grad)
    operands = [x, mask, *arrays(grads), *extra, *small]
    in_specs += [whole(value) for value in small]
    return pl.pallas_call(
        functools.partial(last_kernel, plan.step, mode),
        grid=(plan.blocks,),
        in_specs=in_specs + [HELD for _ in kept],
        out_specs=out_specs,
        out_shape=out_shape,
        scratch_shapes=[plan.scratch(hidden)] * len(sides),
        input_output_aliases={len(operands): 0} if kept else {},
        compiler_params=params(1),
        cost_estimate=cost(0.2),
        name="last_" + mode,
    )(*operands, *kept)


def swap_all(array):
    return lax.all_to_all(array, "tile", split_axis=0, concat_axis=0, tiled=True)


def tile_sum(array, tiles):
    chans, width = array.shape
    parts = swap_all(array.astype(BF16)).reshape(tiles, chans // tiles, width)
    part = jnp.sum(parts.astype(F32), axis=0).astype(BF16)
    spread = jnp.broadcast_to(part[None], (tiles,) + part.shape).reshape(chans, width)
    return swap_all(spread).astype(F32)


def body(
    tiles, x, d, token_mask, ln_in_gain, ln_in_bias, w_ab, w_gate, ln_out_gain, ln_out_bias, w_out
):
    count, crop, chans = x.shape
    hidden = w_out.shape[0]
    plan = Plan(tiles, count, crop)
    me = lax.axis_index("tile")
    side = (me // plan.half).astype(jnp.int32)
    valid = token_mask.astype(F32)
    own_valid = lax.dynamic_slice_in_dim(valid, me * count, count)
    turned_valid = valid.reshape(tiles, plan.subs, plan.rows).transpose(1, 0, 2).reshape(crop)
    mask = own_valid[:, None] * turned_valid[None, :]
    norms = jnp.stack([ln_in_gain, ln_in_bias, ln_out_gain, ln_out_bias], axis=1)
    w_t = w_ab.T
    w_cat = jnp.concatenate([w_ab, w_gate], axis=1)
    mid = [norms, w_gate.T, w_out, w_out.T]
    x, d = plan.view(x), plan.view(d)
    owned = lambda array: array.reshape(plan.half, hidden // plan.half, *array.shape[1:])
    joined = lambda array: array.reshape(hidden, *array.shape[2:])
    every = range(plan.subs)

    plan_cut = plan.cut
    two = plan.subs == 2
    cut_b, back_a = plan_cut(6, 2), plan_cut(3, 3, 2)
    small = [norms, w_t, w_cat]

    def middle(at, first, before, ready, product):
        table = jnp.stack([jnp.stack([half, jnp.int32(sub)]) for half, sub in at])
        g, kept, *local = make_middle(plan, table, first, before, ready, x, d, product, mid)
        return g, kept, jnp.concatenate(local[::-1], axis=1)

    def product_of(b):
        return plan.swap(joined(make_product(plan, own_a, b)))

    held, factor_b0 = make_factors(plan, 0, (), x, mask, norms, w_t)
    own_b0 = owned(plan.swap(factor_b0))
    if two:
        (held,) = make_factors(plan, 1, (held,), x, mask, norms, w_t)
    other_0 = plan.exchange(own_b0)
    own_ab = owned(plan.swap(after(held, own_b0)))
    own_a, own_b, got_b = [(own_ab, 0)], [(own_b0, 0)], []
    if two:
        own_a, own_b = [(own_ab, 2), (own_ab, 0)], [(own_b0, 0), (own_ab, 1)]
        sent = plan.pieces(own_ab[:, :, plan.rows : 2 * plan.rows], cut_b)
        got_b = [plan.exchange(sent[0])]
    b_first = [(other_0, 0)] + own_b
    product = product_of(b_first)
    if two:
        got_b.append(plan.exchange(after(sent[1], product)))
    grad, kept, local_mid = middle([(1 - side, 0)], 0, (), (), product)
    owner_g = [owned(plan.swap(after(grad, *got_b[:1])))]
    grad, kept, local = middle([(side, sub) for sub in every], 1, (kept,), (), product)
    local_mid += local
    grad_b0 = make_grad_b(plan, owner_g[0], own_a, back_a)
    back_0 = [plan.exchange(piece) for piece in grad_b0]
    waits = (owner_g[0], grad_b0[0], *got_b[1:2])
    owner_g.append(owned(plan.swap(after(grad, *waits))))
    grad_b_own = make_grad_b(plan, owner_g[1], own_a, [plan.half] * plan.subs)
    if two:
        b_second = [(piece, 0) for piece in got_b]
        b_first = b_first + b_second
        product = joined(make_product(plan, own_a, b_second))
        product = plan.swap(after(product, owner_g[1], back_0[0]))
        grad, kept, local = middle([(1 - side, 1)], 0, (kept,), grad_b_own[:1], product)
        local_mid += local
        owner_g.append(owned(plan.swap(after(grad, back_0[1]))))
        (grad_b1,) = make_grad_b(plan, owner_g[2], own_a, [plan.half])
        back_1 = plan.exchange(grad_b1)
        back_0[2] = after(back_0[2], grad_b1)
    grads = plan.swap(joined(make_grad_a(plan, owner_g, b_first, grad_b_own[0], back_0)))
    first, second = w_ab[:, : 2 * hidden], w_ab[:, 2 * hidden :]
    pair_grad, local_ab = make_last(
        plan, "both", 0, None, x, mask, [(grads, 0), (grads, plan.subs)], [kept], small
    )
    if two:
        back_1 = after(back_1, grads)
        grad_b = plan.swap(
            joined((grad_b_own[1].astype(F32) + back_1.astype(F32)).astype(BF16))
        )
        side_a = [norms, w_t[: 2 * hidden], jnp.concatenate([first, w_gate], axis=1)]
        side_b = [norms, w_t[2 * hidden :], second]
        base, local_a = make_last(plan, "a", 1, None, x, mask, [(grads, 1)], [kept], side_a)
        grad_b = after(grad_b, local_ab, local_a)
        (local_b,) = make_last(plan, "b_sum", 1, None, x, mask, [(grad_b, 0)], [], side_b)
        (pair_grad,) = make_last(
            plan, "b", 1, pair_grad, x, mask, [(grad_b, 0)], [base], side_b
        )
        local_ab += jnp.concatenate([local_a, local_b], axis=1)
    total = tile_sum(jnp.concatenate([local_ab, local_mid], axis=1), tiles) / crop
    wide = 4 * hidden
    return (
        pair_grad.reshape(count, crop, chans),
        total[:, :wide],
        total[:, wide : wide + chans],
        total[:, wide + chans :],
    )


def solution(mesh):
    pairs = P(("crops", "tile"), None, None)
    return jax.shard_map(
        functools.partial(body, mesh.shape["tile"]),
        mesh=mesh,
        in_specs=(pairs, pairs, P("crops")) + (P(),) * 7,
        out_specs=(pairs,) + (P("crops", None),) * 3,
        check_vma=False,
    )
```

```python
import functools

import jax
import jax.numpy as jnp
from jax import lax
from jax.experimental import pallas as pl
from jax.experimental.pallas import tpu as pltpu
from jax.sharding import PartitionSpec as P

HELD = pl.BlockSpec(memory_space=pl.ANY)
EPS = 1e-05
CHANS = 8
F32 = jnp.float32
BF16 = jnp.bfloat16
NN = (((1,), (0,)), ((), ()))
NT = (((1,), (1,)), ((), ()))
TN = (((0,), (0,)), ((), ()))


def params(steps):
    return pltpu.CompilerParams(
        dimension_semantics=("arbitrary",) * steps, vmem_limit_bytes=50 * 1024 * 1024
    )


def cost(micros):
    return pl.CostEstimate(
        flops=int(micros * 1.0e9), bytes_accessed=int(micros * 3.0e6), transcendentals=0
    )


def dot(left, right, form=NN):
    return lax.dot_general(left, right, form, preferred_element_type=F32)


def sigmoid(value):
    return 0.5 * jnp.tanh(0.5 * value) + 0.5


def col_mean(value):
    return jnp.mean(value, axis=0, keepdims=True)


def stats(value):
    centered = value - col_mean(value)
    inv_std = lax.rsqrt(col_mean(centered * centered) + EPS)
    return centered * inv_std, inv_std


def norm_back(upstream, scaled, inv_std):
    return inv_std * (upstream - col_mean(upstream) - scaled * col_mean(upstream * scaled))


def turned(ref, row, count):
    block = ref[pl.ds(row, count)]
    return block.reshape(-1, block.shape[-1]).astype(F32).T


def lane_parts(scratch, count):
    return [(at, lane) for at in range(count) for lane in range(scratch.shape[0])]


def store_rows(scratch, row, count, rows, value):
    hidden = value.shape[0]
    for part, (at, lane) in enumerate(lane_parts(scratch, count)):
        scratch[lane, pl.ds(row + at, hidden, stride=rows), :] = value[:, part * 128 : (part + 1) * 128]


def load_rows(scratch, row, count, rows):
    hidden = scratch.shape[1] // rows
    return jnp.concatenate(
        [
            scratch[lane, pl.ds(row + at, hidden, stride=rows), :]
            for at, lane in lane_parts(scratch, count)
        ],
        axis=1,
    )


def gather_out(scratch, out_ref, rows, at=0):
    hidden = out_ref.shape[0]
    for lane in range(scratch.shape[0]):
        out_ref[:, at : at + rows, lane * 128 : (lane + 1) * 128] = (
            scratch[lane].reshape(hidden, rows, 128).astype(BF16)
        )


def spread_in(in_ref, scratch):
    hidden, rows, cols = in_ref.shape
    for lane in range(scratch.shape[0]):
        scratch[lane] = (
            in_ref[:, :, lane * 128 : (lane + 1) * 128].astype(F32).reshape(hidden * rows, 128)
        )


def flat_rows(ref, row, count):
    return jnp.concatenate([ref[pl.ds(row + at, 1), :] for at in range(count)], axis=1)


def whole(array):
    return pl.BlockSpec(array.shape, lambda *_: (0,) * array.ndim)


class Plan:
    def __init__(self, tiles, count, crop):
        self.tiles, self.count, self.crop = tiles, count, crop
        self.half = tiles // 2
        self.subs = 2 if count % 32 == 0 else 1
        self.rows = count // self.subs
        self.width = self.half * self.rows
        self.blocks = crop // self.width
        self.step = max(1, 512 // self.width)
        self.groups = [
            [side * self.half + at for at in range(self.half)] for side in range(2)
        ]
        self.partner = [(at, (at + self.half) % tiles) for at in range(tiles)]

    def view(self, array):
        return array.reshape(self.count, self.tiles, self.subs, self.rows, array.shape[-1])

    def pair_spec(self, chans, index):
        return pl.BlockSpec((self.rows, self.half, 1, self.rows, chans), index)

    def scratch(self, hidden):
        return pltpu.VMEM((self.width // 128, self.rows * hidden, 128), F32)

    def swap(self, array):
        return lax.all_to_all(
            array, "tile", split_axis=0, concat_axis=0, axis_index_groups=self.groups, tiled=True
        )

    def cut(self, *eighths):
        return [max(1, self.half * share // 8) for share in eighths]

    def pieces(self, array, counts):
        ends = [sum(counts[: at + 1]) for at in range(len(counts))]
        return [array[end - size : end] for size, end in zip(counts, ends)]

    def exchange(self, array):
        return lax.ppermute(array, "tile", self.partner)


def after_kernel(*refs):
    del refs


def after(value, *others):
    return pl.pallas_call(
        after_kernel,
        in_specs=[HELD] * (1 + len(others)),
        out_specs=HELD,
        out_shape=jax.ShapeDtypeStruct(value.shape, value.dtype),
        input_output_aliases={0: 0},
        compiler_params=params(0),
        cost_estimate=cost(0.1),
        name="after",
    )(value, *others)


def factors_kernel(step, joint, x_ref, mask_ref, norm_ref, w_ref, *refs):
    sa_ref, sb_ref = refs[-2:]
    rows = x_ref.shape[0]
    hidden = w_ref.shape[0] // 4

    @pl.loop(0, rows // step, unroll=min(4, rows // step))
    def _(turn):
        row = pl.multiple_of(turn * step, step)
        z_hat, _ = stats(turned(x_ref, row, step))
        normed = (z_hat * norm_ref[:, 0:1] + norm_ref[:, 1:2]).astype(BF16)
        mask = flat_rows(mask_ref, row, step)
        proj = dot(w_ref[...], normed)
        value_a, gate_a = proj[:hidden], proj[hidden : 2 * hidden]
        value_b, gate_b = proj[2 * hidden : 3 * hidden], proj[3 * hidden :]
        store_rows(sb_ref, row, step, rows, mask * sigmoid(gate_b) * value_b)
        store_rows(sa_ref, row, step, rows, mask * sigmoid(gate_a) * value_a)

    if joint:
        gather_out(sa_ref, refs[-3], rows)
        gather_out(sb_ref, refs[-3], rows, rows)
    else:
        gather_out(sa_ref, refs[-4], rows)
        gather_out(sb_ref, refs[-3], rows)


def make_factors(plan, sub, before, x, mask, norms, w_t):
    chans = x.shape[-1]
    hidden = w_t.shape[0] // 4
    block = (hidden, plan.rows, plan.width)
    held = plan.rows * (3 if plan.subs == 2 else 1)
    out_specs = [
        pl.BlockSpec(block, lambda j: (0, 2 * (plan.subs - 1), j)),
        pl.BlockSpec(block, lambda j: (0, 0, j)),
    ]
    out_shape = [
        jax.ShapeDtypeStruct((hidden, held, plan.crop), BF16),
        jax.ShapeDtypeStruct((hidden, plan.rows, plan.crop), BF16),
    ]
    if before:
        out_specs = [pl.BlockSpec((hidden, 2 * plan.rows, plan.width), lambda j: (0, 0, j))]
        out_shape = out_shape[:1]
    return pl.pallas_call(
        functools.partial(factors_kernel, plan.step, bool(before)),
        grid=(plan.blocks,),
        in_specs=[
            plan.pair_spec(chans, lambda j: (sub, j % 2, j // 2, 0, 0)),
            pl.BlockSpec((plan.rows, plan.width), lambda j: (sub, j)),
            whole(norms),
            whole(w_t),
        ]
        + [HELD for _ in before],
        out_specs=out_specs,
        out_shape=out_shape,
        input_output_aliases={4: 0} if before else {},
        scratch_shapes=[plan.scratch(hidden)] * 2,
        compiler_params=params(1),
        cost_estimate=cost(0.2),
        name="factors",
    )(x, mask, norms, w_t, *before)


def matrix(refs, chan):
    parts = [ref[:, chan].reshape(-1, ref.shape[-1]) for ref in refs]
    return jnp.concatenate(parts, axis=0) if len(parts) > 1 else parts[0]


def by_sub(ref, chan, subs):
    rows = ref.shape[2] // subs
    parts = [
        ref[:, chan, sub * rows : (sub + 1) * rows, :].reshape(-1, ref.shape[3])
        for sub in range(subs)
    ]
    return jnp.concatenate(parts, axis=0) if subs > 1 else parts[0]


def to_subs(ref, chan, value, subs, rows):
    part = value.shape[0] // subs
    for sub in range(subs):
        ref[:, chan, sub * rows : (sub + 1) * rows, :] = value[
            sub * part : (sub + 1) * part
        ].astype(BF16).reshape(ref.shape[0], rows, ref.shape[3])


def own_spec(array):
    src, _, rows, cols = array.shape
    return pl.BlockSpec((src, CHANS, rows, cols), lambda h: (0, h, 0, 0))


def view_spec(plan, view):
    array, at = view
    return pl.BlockSpec((array.shape[0], CHANS, plan.rows, array.shape[3]), lambda h: (0, h, at, 0))


def arrays(views):
    return [array for array, _ in views]


def product_kernel(subs, rows, *refs):
    a, b, p_ref = refs[:subs], refs[subs:-1], refs[-1]
    for chan in range(CHANS):
        to_subs(p_ref, chan, dot(matrix(a, chan), matrix(b, chan), NT), subs, rows)


def make_product(plan, a, b):
    tiles, chans = a[0][0].shape[:2]
    cols = sum(array.shape[0] for array in arrays(b)) * plan.rows
    out = jax.ShapeDtypeStruct((tiles, chans, plan.count, cols), BF16)
    return pl.pallas_call(
        functools.partial(product_kernel, plan.subs, plan.rows),
        grid=(chans // CHANS,),
        in_specs=[view_spec(plan, view) for view in (*a, *b)],
        out_specs=own_spec(out),
        out_shape=out,
        compiler_params=params(1),
        cost_estimate=cost(0.2),
        name="product",
    )(*arrays(a), *arrays(b))


def grad_b_kernel(subs, g_ref, *refs):
    a, outs = refs[:subs], refs[subs:]
    for chan in range(CHANS):
        grad = dot(by_sub(g_ref, chan, subs), matrix(a, chan), TN).astype(BF16)
        at = 0
        for out in outs:
            size = out.shape[0] * out.shape[2]
            out[:, chan] = grad[at : at + size].reshape(out.shape[0], *out.shape[2:])
            at += size


def make_grad_b(plan, g, a, tiles):
    outs = [
        jax.ShapeDtypeStruct((count, g.shape[1], plan.rows, plan.crop), BF16) for count in tiles
    ]
    return pl.pallas_call(
        functools.partial(grad_b_kernel, plan.subs),
        grid=(g.shape[1] // CHANS,),
        in_specs=[own_spec(g)] + [view_spec(plan, view) for view in a],
        out_specs=[own_spec(value) for value in outs],
        out_shape=outs,
        compiler_params=params(1),
        cost_estimate=cost(0.2),
        name="grad_b",
    )(g, *arrays(a))


def grad_a_kernel(subs, rows, counts, *refs):
    g, b = refs[: counts[0]], refs[counts[0] : counts[0] + counts[1]]
    own, back, out = refs[counts[0] + counts[1]], refs[counts[0] + counts[1] + 1 : -1], refs[-1]
    for chan in range(CHANS):
        left = jnp.concatenate([by_sub(ref, chan, subs) for ref in g], axis=1)
        to_subs(out, chan, dot(left, matrix(b, chan)), subs, rows)
        at = 0
        for piece in back:
            end = at + piece.shape[0]
            added = own[at:end, chan].astype(F32) + piece[:, chan].astype(F32)
            out[at:end, chan, subs * rows :, :] = added.astype(BF16)
            at = end


def make_grad_a(plan, g, b, own, back):
    chans = own.shape[1]
    out = jax.ShapeDtypeStruct((plan.half, chans, plan.count + plan.rows, plan.crop), BF16)
    return pl.pallas_call(
        functools.partial(grad_a_kernel, plan.subs, plan.rows, (len(g), len(b))),
        grid=(chans // CHANS,),
        in_specs=[own_spec(value) for value in g]
        + [view_spec(plan, view) for view in b]
        + [own_spec(value) for value in (own, *back)],
        out_specs=own_spec(out),
        out_shape=out,
        compiler_params=params(1),
        cost_estimate=cost(0.2),
        name="grad_a",
    )(*g, *arrays(b), own, *back)


def middle_kernel(
    step, _, x_ref, d_ref, p_ref, norm_ref, wg_ref, wo_ref, wot_ref, *refs
):
    g_ref, gb_ref, gwo_ref, gwg_ref, s_ref = refs[-5:]
    rows = x_ref.shape[0]
    width = gb_ref.shape[-1]

    @pl.when((pl.program_id(0) == 0) & (pl.program_id(1) == 0))
    def _():
        gwo_ref[...] = jnp.zeros_like(gwo_ref)
        gwg_ref[...] = jnp.zeros_like(gwg_ref)

    spread_in(p_ref, s_ref)

    @pl.loop(0, rows // step, unroll=min(4, rows // step))
    def _(turn):
        row = pl.multiple_of(turn * step, step)
        z_hat, _ = stats(turned(x_ref, row, step))
        normed = (z_hat * norm_ref[:, 0:1] + norm_ref[:, 1:2]).astype(BF16)
        gate = sigmoid(dot(wg_ref[...], normed))
        x_hat, inv_std = stats(load_rows(s_ref, row, step, rows))
        x_norm = (x_hat * norm_ref[:, 2:3] + norm_ref[:, 3:4]).astype(BF16)
        out_lin = dot(wot_ref[...], x_norm)
        lin = turned(d_ref, row, step) * gate
        grad_lin = lin.astype(BF16)
        gate_back = (lin * out_lin * (1.0 - gate)).astype(BF16)
        upstream = dot(wo_ref[...], grad_lin) * norm_ref[:, 2:3]
        store_rows(s_ref, row, step, rows, norm_back(upstream, x_hat, inv_std))
        for at in range(step):
            gb_ref[row + at] = gate_back[:, at * width : (at + 1) * width]
        gwo_ref[...] += dot(x_norm, grad_lin, NT)
        gwg_ref[...] += dot(normed, gate_back, NT)

    gather_out(s_ref, g_ref, rows)


def make_middle(plan, table, first, before, ready, x, d, p, small):
    chans = x.shape[-1]
    hidden = p.shape[0]
    cut = table.shape[0]
    grads = [jax.ShapeDtypeStruct((hidden, chans), F32), jax.ShapeDtypeStruct((chans, chans), F32)]
    pairs = plan.pair_spec(chans, lambda i, j, at: (i, at[j, 0], at[j, 1], 0, 0))
    channel = (hidden, plan.rows, plan.width)
    kept = [*before, *ready]
    return pl.pallas_call(
        functools.partial(middle_kernel, plan.step),
        grid_spec=pltpu.PrefetchScalarGridSpec(
            num_scalar_prefetch=1,
            grid=(plan.subs, cut),
            in_specs=[pairs, pairs, pl.BlockSpec(channel, lambda i, j, at: (0, i, first + j))]
            + [whole(value) for value in small]
            + [HELD for _ in kept],
            out_specs=[
                pl.BlockSpec(channel, lambda i, j, at: (0, i, j)),
                pl.BlockSpec(
                    (plan.rows, chans, plan.width),
                    lambda i, j, at: (i, 0, at[j, 1] * 2 + at[j, 0]),
                ),
            ]
            + [whole(value) for value in grads],
            scratch_shapes=[plan.scratch(hidden)],
        ),
        out_shape=[
            jax.ShapeDtypeStruct((hidden, plan.count, cut * plan.width), BF16),
            jax.ShapeDtypeStruct((plan.count, chans, plan.crop), BF16),
        ]
        + grads,
        input_output_aliases={4 + len(small): 1} if before else {},
        compiler_params=params(2),
        cost_estimate=cost(0.2),
        name="middle",
    )(table, x, d, p, *small, *kept)


def last_kernel(step, mode, *refs):
    sides, gated, based, out_kind, summed = MODES[mode]
    scratches, rest = refs[-len(sides) :], iter(refs[: -len(sides)])
    x_ref, mask_ref = next(rest), next(rest)
    grads = [next(rest) for _ in sides]
    gate_ref = next(rest) if gated else None
    base_ref = next(rest) if based else None
    norm_ref, wt_ref, wcat_ref, *outs = rest
    gw_ref = outs[-1]
    out_ref = outs[-1 - summed] if out_kind else None
    rows, _, _, _, _ = x_ref.shape
    hidden = grads[0].shape[0]
    width = mask_ref.shape[1]

    if summed:

        @pl.when(pl.program_id(0) == 0)
        def _():
            gw_ref[...] = jnp.zeros_like(gw_ref)

    for ref, scratch in zip(grads, scratches):
        spread_in(ref, scratch)

    @pl.loop(0, rows // step, unroll=min(4, rows // step))
    def _(turn):
        row = pl.multiple_of(turn * step, step)
        z_hat, inv_in = stats(turned(x_ref, row, step))
        normed = (z_hat * norm_ref[:, 0:1] + norm_ref[:, 1:2]).astype(BF16)
        mask = flat_rows(mask_ref, row, step)
        proj = dot(wt_ref[...], normed)
        parts = []
        for side, scratch in enumerate(scratches):
            value = proj[2 * side * hidden : (2 * side + 1) * hidden]
            sig = sigmoid(proj[(2 * side + 1) * hidden : (2 * side + 2) * hidden])
            to_value = load_rows(scratch, row, step, rows) * mask * sig
            parts += [to_value.astype(BF16), (to_value * value * (1.0 - sig)).astype(BF16)]
        grad_proj = jnp.concatenate(parts, axis=0)
        if summed:
            gw_ref[...] += dot(normed, grad_proj, NT)
        if out_kind:
            every = grad_proj
            if gated:
                gate_back = jnp.concatenate([gate_ref[row + at] for at in range(step)], axis=1)
                every = jnp.concatenate([grad_proj, gate_back], axis=0)
            upstream = dot(wcat_ref[...], every)
            if based:
                upstream += jnp.concatenate(
                    [base_ref[row + at].astype(F32) for at in range(step)], axis=1
                )
            if out_kind == "pair":
                grad = norm_back(upstream * norm_ref[:, 0:1], z_hat, inv_in).T.astype(BF16)
                out_ref[pl.ds(row, step)] = grad.reshape((step,) + out_ref.shape[1:])
            else:
                for at in range(step):
                    out_ref[row + at] = upstream[:, at * width : (at + 1) * width].astype(BF16)


MODES = {
    "both": ((0, 1), True, False, "pair", True),
    "a": ((0,), True, False, "base", True),
    "b_sum": ((1,), False, False, "", True),
    "b": ((1,), False, True, "pair", False),
}


def make_last(plan, mode, sub, before, x, mask, grads, extra, small):
    sides, gated, based, out_kind, summed = MODES[mode]
    chans = x.shape[-1]
    hidden = grads[0][0].shape[0]
    grad = jax.ShapeDtypeStruct((chans, 2 * len(sides) * hidden), F32)
    pairs = plan.pair_spec(chans, lambda j: (sub, j % 2, j // 2, 0, 0))
    channel = (hidden, plan.rows, plan.width)
    lines = (plan.rows, chans, plan.width)
    kept = [] if before is None else [before]
    in_specs = [pairs, pl.BlockSpec((plan.rows, plan.width), lambda j: (sub, j))]
    for _, at in grads:
        in_specs.append(pl.BlockSpec(channel, lambda j, at=at: (0, at, j)))
    if gated:
        in_specs.append(pl.BlockSpec(lines, lambda j: (sub, 0, j)))
    if based:
        in_specs.append(pl.BlockSpec(lines, lambda j: (0, 0, j)))
    out_specs, out_shape = [], []
    if out_kind == "pair":
        out_specs.append(pairs)
        out_shape.append(jax.ShapeDtypeStruct(x.shape, BF16))
    if out_kind == "base":
        out_specs.append(pl.BlockSpec(lines, lambda j: (0, 0, j)))
        out_shape.append(jax.ShapeDtypeStruct((plan.rows, chans, plan.crop), BF16))
    if summed:
        out_specs.append(whole(grad))
        out_shape.append(grad)
    operands = [x, mask, *arrays(grads), *extra, *small]
    in_specs += [whole(value) for value in small]
    return pl.pallas_call(
        functools.partial(last_kernel, plan.step, mode),
        grid=(plan.blocks,),
        in_specs=in_specs + [HELD for _ in kept],
        out_specs=out_specs,
        out_shape=out_shape,
        scratch_shapes=[plan.scratch(hidden)] * len(sides),
        input_output_aliases={len(operands): 0} if kept else {},
        compiler_params=params(1),
        cost_estimate=cost(0.2),
        name="last_" + mode,
    )(*operands, *kept)


def swap_all(array):
    return lax.all_to_all(array, "tile", split_axis=0, concat_axis=0, tiled=True)


def tile_sum(array, tiles):
    chans, width = array.shape
    parts = swap_all(array.astype(BF16)).reshape(tiles, chans // tiles, width)
    part = jnp.sum(parts.astype(F32), axis=0).astype(BF16)
    spread = jnp.broadcast_to(part[None], (tiles,) + part.shape).reshape(chans, width)
    return swap_all(spread).astype(F32)


def body(
    tiles, x, d, token_mask, ln_in_gain, ln_in_bias, w_ab, w_gate, ln_out_gain, ln_out_bias, w_out
):
    count, crop, chans = x.shape
    hidden = w_out.shape[0]
    plan = Plan(tiles, count, crop)
    me = lax.axis_index("tile")
    side = (me // plan.half).astype(jnp.int32)
    valid = token_mask.astype(F32)
    own_valid = lax.dynamic_slice_in_dim(valid, me * count, count)
    turned_valid = valid.reshape(tiles, plan.subs, plan.rows).transpose(1, 0, 2).reshape(crop)
    mask = own_valid[:, None] * turned_valid[None, :]
    norms = jnp.stack([ln_in_gain, ln_in_bias, ln_out_gain, ln_out_bias], axis=1)
    w_t = w_ab.T
    w_cat = jnp.concatenate([w_ab, w_gate], axis=1)
    mid = [norms, w_gate.T, w_out, w_out.T]
    x, d = plan.view(x), plan.view(d)
    owned = lambda array: array.reshape(plan.half, hidden // plan.half, *array.shape[1:])
    joined = lambda array: array.reshape(hidden, *array.shape[2:])
    every = range(plan.subs)

    plan_cut = plan.cut
    two = plan.subs == 2
    cut_b, back_a = plan_cut(6, 2), plan_cut(2, 3, 3)
    small = [norms, w_t, w_cat]

    def middle(at, first, before, ready, product):
        table = jnp.stack([jnp.stack([half, jnp.int32(sub)]) for half, sub in at])
        g, kept, *local = make_middle(plan, table, first, before, ready, x, d, product, mid)
        return g, kept, jnp.concatenate(local[::-1], axis=1)

    def product_of(b):
        return plan.swap(joined(make_product(plan, own_a, b)))

    held, factor_b0 = make_factors(plan, 0, (), x, mask, norms, w_t)
    own_b0 = owned(plan.swap(factor_b0))
    if two:
        (held,) = make_factors(plan, 1, (held,), x, mask, norms, w_t)
    other_0 = plan.exchange(own_b0)
    own_ab = owned(plan.swap(after(held, own_b0)))
    own_a, own_b, got_b = [(own_ab, 0)], [(own_b0, 0)], []
    if two:
        own_a, own_b = [(own_ab, 2), (own_ab, 0)], [(own_b0, 0), (own_ab, 1)]
        sent = plan.pieces(own_ab[:, :, plan.rows : 2 * plan.rows], cut_b)
        got_b = [plan.exchange(sent[0])]
    b_first = [(other_0, 0)] + own_b
    product = product_of(b_first)
    if two:
        got_b.append(plan.exchange(after(sent[1], product)))
    grad, kept, local_mid = middle([(1 - side, 0)], 0, (), (), product)
    owner_g = [owned(plan.swap(after(grad, *got_b[:1])))]
    grad, kept, local = middle([(side, sub) for sub in every], 1, (kept,), (), product)
    local_mid += local
    grad_b0 = make_grad_b(plan, owner_g[0], own_a, back_a)
    back_0 = [plan.exchange(piece) for piece in grad_b0]
    waits = (owner_g[0], grad_b0[0], *got_b[1:2])
    owner_g.append(owned(plan.swap(after(grad, *waits))))
    grad_b_own = make_grad_b(plan, owner_g[1], own_a, [plan.half] * plan.subs)
    if two:
        b_second = [(piece, 0) for piece in got_b]
        b_first = b_first + b_second
        product = joined(make_product(plan, own_a, b_second))
        product = plan.swap(after(product, owner_g[1], back_0[0]))
        grad, kept, local = middle([(1 - side, 1)], 0, (kept,), grad_b_own[:1], product)
        local_mid += local
        owner_g.append(owned(plan.swap(after(grad, back_0[1]))))
        (grad_b1,) = make_grad_b(plan, owner_g[2], own_a, [plan.half])
        back_1 = plan.exchange(grad_b1)
        back_0[2] = after(back_0[2], grad_b1)
    grads = plan.swap(joined(make_grad_a(plan, owner_g, b_first, grad_b_own[0], back_0)))
    first, second = w_ab[:, : 2 * hidden], w_ab[:, 2 * hidden :]
    pair_grad, local_ab = make_last(
        plan, "both", 0, None, x, mask, [(grads, 0), (grads, plan.subs)], [kept], small
    )
    if two:
        back_1 = after(back_1, grads)
        grad_b = plan.swap(
            joined((grad_b_own[1].astype(F32) + back_1.astype(F32)).astype(BF16))
        )
        side_a = [norms, w_t[: 2 * hidden], jnp.concatenate([first, w_gate], axis=1)]
        side_b = [norms, w_t[2 * hidden :], second]
        base, local_a = make_last(plan, "a", 1, None, x, mask, [(grads, 1)], [kept], side_a)
        grad_b = after(grad_b, local_ab, local_a)
        (local_b,) = make_last(plan, "b_sum", 1, None, x, mask, [(grad_b, 0)], [], side_b)
        (pair_grad,) = make_last(
            plan, "b", 1, pair_grad, x, mask, [(grad_b, 0)], [base], side_b
        )
        local_ab += jnp.concatenate([local_a, local_b], axis=1)
    total = tile_sum(jnp.concatenate([local_ab, local_mid], axis=1), tiles) / crop
    wide = 4 * hidden
    return (
        pair_grad.reshape(count, crop, chans),
        total[:, :wide],
        total[:, wide : wide + chans],
        total[:, wide + chans :],
    )


def solution(mesh):
    pairs = P(("crops", "tile"), None, None)
    return jax.shard_map(
        functools.partial(body, mesh.shape["tile"]),
        mesh=mesh,
        in_specs=(pairs, pairs, P("crops")) + (P(),) * 7,
        out_specs=(pairs,) + (P("crops", None),) * 3,
        check_vma=False,
    )
```
